32 devices in a mesh: sample: 8 (over y, x, core), cls: 4 (over z).
Axes of the slice: x: 2, y: 2, z: 4, core: 2. Of those that a mesh axis runs over, the one named last changes fastest.
Arguments:
- features: bfloat16 [4096, 2048], P('sample', 'cls'), may hold values from -1.5 to 1.5
- head: bfloat16 [2048, 8192], P('sample', 'cls'), may hold values from -1.5859375 to 1.5859375
- class_cap: bfloat16 [8192], P('cls'), may hold values from 0.5 to 4
Outputs:
- targets: bfloat16 [4096, 8192], P('sample', 'cls')
- grad_features: bfloat16 [4096, 2048], P('sample', 'cls')
- grad_head: bfloat16 [2048, 8192], P('sample', 'cls')
The draws below stay inside these ranges and needn't reach their ends.
All inputs are finite; a program needn't handle non-finite values.
Results may differ from the reference program's by a relative error of at most 0.02.
Values may be sent and summed in bfloat16 or wider, within the bound.
No kernel may reach another device: no remote copies, remote signals or barrier semaphores. Data moves between devices by JAX's collectives and lax.ppermute only.
A program may use at most 64 MiB of HBM per device.

```python
import math
import jax
import jax.numpy as jnp
from jax import lax

D = 2048
K = 8192
ITERS = 3
N = 4096
N_SAMPLE = 8
N_CLS = 4


def shard_levels(stream_key, shape, cuts, least, largest):
    factor_of, own = 1.0, jax.random.fold_in(stream_key, 6)
    for position, shards_of in cuts:
        heights = jnp.exp(jax.random.uniform(jax.random.fold_in(own, position), (shards_of,), jnp.float32, least / len(cuts), largest / len(cuts)))
        factor_of = factor_of * jnp.repeat(heights, shape[position] // shards_of).reshape([-1 if axis == position else 1 for axis in range(len(shape))])
    return factor_of


def normal_values(rng, extent, scale, limit, shards=(), dtype=jnp.bfloat16):
    array = scale * jax.random.normal(rng, extent, jnp.float32)
    if shards:
        array = array * shard_levels(rng, extent, shards, -0.22, 0.18)
    return jnp.clip(array, -limit, limit).astype(dtype)


def setup_inputs(seed: int = 0) -> dict:
    key_of = jax.random.split(jax.random.key(seed), 4)
    features = normal_values(key_of[0], (N, D), 0.25, 1.5, ((0, 8), (1, 4)))
    head = normal_values(key_of[1], (D, K), (12.0 / D ** 0.5), 1.5859375, ((0, 8), (1, 4)))
    class_cap = jnp.clip(jnp.exp(math.log(4.0) - 2.0794415 * jax.random.uniform(key_of[2], (K,), jnp.float32) ** shard_levels(key_of[2], (K,), ((0, 4),), -0.2, 0.2)), 0.5, 4.0).astype(jnp.bfloat16)
    return dict(features=features, head=head, class_cap=class_cap)


softcap = 15.0
sharpen = 2.0


def reference(features, head, class_cap):
    row_count = features.shape[0]
    class_count = head.shape[1]
    width = features.shape[1]
    logits = jnp.dot(features, head, preferred_element_type=jnp.float32)
    capped = softcap * jnp.tanh(logits / softcap)
    student = jnp.exp(capped)
    student = student / jnp.sum(student, axis=1, keepdims=True)
    transport = jnp.exp(capped * sharpen)
    ceiling = class_cap.astype(jnp.float32) * (row_count / class_count)
    for iteration in range(ITERS):
        transport = transport / jnp.sum(transport, axis=1, keepdims=True)
        column_mass = jnp.sum(transport, axis=0)
        transport = transport * jnp.minimum(1.0, ceiling / column_mass)
    targets = (transport / jnp.sum(transport, axis=1, keepdims=True)).astype(jnp.bfloat16)
    tanh_slope = 1.0 - (capped / softcap) ** 2
    grad_logits = ((student - targets.astype(jnp.float32)) * tanh_slope).astype(jnp.bfloat16)

    feature_blocks = features.reshape(N_SAMPLE, row_count // N_SAMPLE, width)
    grad_blocks = grad_logits.reshape(N_SAMPLE, row_count // N_SAMPLE, class_count)

    def add_head(total, pair):
        partial_sum = lax.dot_general(pair[0], pair[1], (((0,), (0,)), ((), ())), preferred_element_type=jnp.float32)
        rounded = lax.optimization_barrier(partial_sum.astype(jnp.bfloat16))
        return total + rounded.astype(jnp.float32), None

    head_total, _ = lax.scan(add_head, jnp.zeros((width, class_count), jnp.float32), (feature_blocks, grad_blocks))

    class_local = class_count // N_CLS
    head_blocks = jnp.transpose(head.reshape(width, N_CLS, class_local), (1, 0, 2))
    logit_blocks = jnp.transpose(grad_logits.reshape(row_count, N_CLS, class_local), (1, 0, 2))

    def add_feature(total, pair):
        partial_sum = lax.dot_general(pair[1], pair[0], (((1,), (1,)), ((), ())), preferred_element_type=jnp.float32)
        rounded = lax.optimization_barrier(partial_sum.astype(jnp.bfloat16))
        return total + rounded.astype(jnp.float32), None

    feature_total, _ = lax.scan(add_feature, jnp.zeros((row_count, width), jnp.float32), (head_blocks, logit_blocks))
    return targets, feature_total.astype(jnp.bfloat16), head_total.astype(jnp.bfloat16)
```

```python
import jax
import jax.numpy as jnp
from jax import lax
from jax.sharding import PartitionSpec as P

ITERS = 3


softcap = 15.0
sharpen = 2.0
f32 = jnp.float32
bf16 = jnp.bfloat16


def matmul(left, right, dims):
    return lax.dot_general(left, right, (dims, ((), ())), preferred_element_type=f32)


def flip(value, axis, mask):
    size = lax.axis_size(axis)
    return lax.ppermute(value, axis, [(i, i ^ mask) for i in range(size)])


def step(value, axis, hop):
    size = lax.axis_size(axis)
    pairs = [(i, i + hop) for i in range(size) if 0 <= i + hop < size]
    return lax.ppermute(value, axis, pairs)


def row_total(value):
    size = lax.axis_size("cls")
    shifted = [
        lax.ppermute(value, "cls", [(i, (i + hop) % size) for i in range(size)])
        for hop in range(1, size)
    ]
    return sum(shifted, value)


def column_total(value):
    size = lax.axis_size("sample")
    value = value + flip(value, "sample", 1)
    others = [flip(value, "sample", mask) for mask in range(2, size, 2)]
    return sum(others, value)


def chip_axes(size):
    chips = size // 2
    bits = chips.bit_length() - 1
    low = 1 << ((bits + 1) // 2)
    first = [2 * m for m in range(1, low)]
    second = [2 * low * m for m in range(1, chips // low)]
    return first, second


def gather_head(head):
    size = lax.axis_size("sample")
    first, second = chip_axes(size)
    held = {0: head}
    for mask in first + second:
        held[mask] = flip(head, "sample", mask)
    half = head.shape[0] // 2
    for a in first:
        for b in second:
            top = flip(held[a][:half], "sample", b)
            bottom = flip(held[b][half:], "sample", a)
            held[a | b] = jnp.concatenate([top, bottom], axis=0)
    return held


def gather_features(features):
    size = lax.axis_size("cls")
    me = lax.axis_index("cls")
    right, left = [], []
    up = down = features
    for _ in range(1, size):
        up = step(up, "cls", 1)
        down = step(down, "cls", -1)
        right.append(up)
        left.append(down)
    blocks = [features] + [
        jnp.where(me >= hop, right[hop - 1], left[size - hop - 1]) for hop in range(1, size)
    ]
    width = features.shape[1]
    whole = jnp.zeros((features.shape[0], width * size), features.dtype)
    for hop, block in enumerate(blocks):
        whole = lax.dynamic_update_slice(whole, block, (0, lax.rem(me - hop + size, size) * width))
    return whole


def scatter_features(block_of):
    size = lax.axis_size("cls")
    me = lax.axis_index("cls")
    clip = lambda index: jnp.clip(index, 0, size - 1)
    up = down = None
    for t in range(1, size):
        right = block_of(clip(size - t + me))
        leftward = block_of(clip(me - (size - t)))
        if up is not None:
            right = (right.astype(f32) + up.astype(f32)).astype(bf16)
            leftward = (leftward.astype(f32) + down.astype(f32)).astype(bf16)
        up = step(right, "cls", 1)
        down = step(leftward, "cls", -1)
    return (block_of(me).astype(f32) + up.astype(f32) + down.astype(f32)).astype(bf16)


def scatter_head(partial_of):
    size = lax.axis_size("sample")
    first, second = chip_axes(size)

    def both(mask):
        other = flip(partial_of(mask | 1), "sample", 1)
        return partial_of(mask).astype(f32) + other.astype(f32)

    half = partial_of(0).shape[0] // 2
    tops, bottoms = {}, {}
    for a in first:
        for b in second:
            block = both(a | b).astype(bf16)
            tops.setdefault(b, []).append(flip(block[:half], "sample", a))
            bottoms.setdefault(a, []).append(flip(block[half:], "sample", b))
    total = None
    for mask in first + second:
        block = both(mask)
        top, bottom = block[:half], block[half:]
        for part in tops.get(mask, []):
            top = top + part.astype(f32)
        for part in bottoms.get(mask, []):
            bottom = bottom + part.astype(f32)
        sent = flip(jnp.concatenate([top, bottom], axis=0).astype(bf16), "sample", mask).astype(f32)
        total = sent if total is None else total + sent
    return (both(0) + total).astype(bf16)


def per_device(features, head, class_cap):
    local_rows = features.shape[0]
    depth = head.shape[0]
    class_local = head.shape[1]
    sample_count = lax.axis_size("sample")
    class_groups = lax.axis_size("cls")
    ratio = local_rows * sample_count / (class_local * class_groups)
    me = lax.axis_index("sample")
    core = me & 1

    same = gather_head(head)
    whole = gather_features(features)
    masks = sorted(same)
    pieces = []
    for mask in masks:
        sibling = flip(same[mask], "sample", 1)
        pieces.append(jnp.where(core == 0, same[mask], sibling))
        pieces.append(jnp.where(core == 0, sibling, same[mask]))
    head_full = jnp.concatenate(pieces, axis=0)
    wide = jnp.concatenate(
        [
            lax.dynamic_slice(whole, (0, ((me >> 1) ^ (mask >> 1)) * 2 * depth), (local_rows, 2 * depth))
            for mask in masks
        ],
        axis=1,
    )
    logits = matmul(wide, head_full, ((1,), (0,)))
    tanh = jnp.tanh(logits / softcap)
    student = jnp.exp(softcap * tanh)
    plan = student * student
    masses = row_total(jnp.stack([jnp.sum(student, axis=1), jnp.sum(plan, axis=1)]))
    ceiling = class_cap.astype(f32) * ratio
    row_mass = masses[1]
    scale = jnp.ones((class_local,), f32)
    for iteration in range(ITERS):
        if iteration > 0:
            row_mass = row_total(jnp.sum(plan * scale[None, :], axis=1))
        mass = column_total(jnp.sum(plan * (1.0 / row_mass)[:, None], axis=0) * scale)
        scale = scale * jnp.minimum(1.0, ceiling / mass)
    row_mass = row_total(jnp.sum(plan * scale[None, :], axis=1))
    targets = (plan * scale[None, :] * (1.0 / row_mass)[:, None]).astype(bf16)
    slope = 1.0 - tanh * tanh
    grad_logits = ((student * (1.0 / masses[0])[:, None] - targets.astype(f32)) * slope).astype(bf16)

    def head_partial(mask):
        first = (me ^ mask) * depth
        columns = lax.dynamic_slice(whole, (0, first), (local_rows, depth))
        return matmul(columns, grad_logits, ((0,), (0,))).astype(bf16)

    partials = {mask: head_partial(mask) for mask in range(sample_count)}
    shares = matmul(grad_logits, head_full, ((1,), (1,))).astype(bf16)
    width = features.shape[1]

    def feature_block(index):
        return lax.dynamic_slice(shares, (0, (index ^ (me >> 1)) * width), (local_rows, width))

    grad_features = scatter_features(feature_block)
    grad_head = scatter_head(lambda mask: partials[mask])
    return (targets, grad_features, grad_head)


def solution(mesh):
    return jax.shard_map(
        per_device,
        mesh=mesh,
        in_specs=(P("sample", "cls"), P("sample", "cls"), P("cls")),
        out_specs=(P("sample", "cls"), P("sample", "cls"), P("sample", "cls")),
        check_vma=False,
    )
```

```python
import functools

import jax
import jax.numpy as jnp
from jax import lax
from jax.experimental import pallas as pl
from jax.experimental.pallas import tpu as pltpu
from jax.sharding import PartitionSpec as P

ITERS = 3


softcap = 15.0
sharpen = 2.0
f32 = jnp.float32
bf16 = jnp.bfloat16
VMEM = pltpu.VMEM
LANES = 128


def matmul(left, right, dims):
    return lax.dot_general(left, right, (dims, ((), ())), preferred_element_type=f32)


def flip(value, axis, mask):
    size = lax.axis_size(axis)
    return lax.ppermute(value, axis, [(i, i ^ mask) for i in range(size)])


def butterfly(value, axis):
    mask = 1
    while mask < lax.axis_size(axis):
        value = value + flip(value, axis, mask)
        mask *= 2
    return value


def row_total(value):
    return butterfly(value, "cls")


def column_total(value):
    return butterfly(value, "sample")


def link_pairs(parity, size):
    other = [((i + parity) ^ 1) - parity for i in range(size)]
    return [(i, j if 0 <= j < size else i) for i, j in enumerate(other)]


def swap(value, parity):
    return lax.ppermute(value, "cls", link_pairs(parity, lax.axis_size("cls")))


def line_source(parity, hop, me, size):
    rightward = (me & 1) == parity
    above, below = me + hop, me - hop
    above = jnp.where(above >= size, 2 * size - 1 - above, above)
    below = jnp.where(below < 0, -1 - below, below)
    return jnp.where(rightward, above, below)


def chip_axes(size):
    chips = size // 2
    bits = chips.bit_length() - 1
    low = 1 << ((bits + 1) // 2)
    first = [2 * m for m in range(1, low)]
    second = [2 * low * m for m in range(1, chips // low)]
    return first, second


def gather_head(head):
    size = lax.axis_size("sample")
    first, second = chip_axes(size)
    half = head.shape[0] // 2
    top, bottom = head[:half], head[half:]
    own = [(0, 0, head)]
    held = {}
    for mask in first:
        held[mask, 0] = flip(top, "sample", mask)
    for mask in second:
        held[mask, half] = flip(bottom, "sample", mask)
    for mask in first:
        held[mask, half] = flip(bottom, "sample", mask)
    for mask in second:
        held[mask, 0] = flip(top, "sample", mask)
    for a in first:
        for b in second:
            held[a | b, 0] = flip(held[a, 0], "sample", b)
            held[a | b, half] = flip(held[b, half], "sample", a)
    same = own + [(mask, offset, block) for (mask, offset), block in held.items()]
    return same + [(mask | 1, offset, flip(block, "sample", 1)) for mask, offset, block in same]


def gather_features(features):
    size = lax.axis_size("cls")
    pieces = [(0, 0, features)]
    even = odd = features
    for hop in range(1, size):
        even, odd = swap(odd, 0), swap(even, 1)
        pieces.append((0, hop, even))
        if hop < size - 1 or size % 2:
            pieces.append((1, hop, odd))
    return pieces


def scatter_features(block_of):
    size = lax.axis_size("cls")
    me = lax.axis_index("cls")
    has = {True: me > 0, False: me < size - 1}

    def joined(block, received, rightward):
        if received is None:
            return block
        keep = jnp.where(rightward, has[True], has[False])
        return (block.astype(f32) + jnp.where(keep, received.astype(f32), 0.0)).astype(bf16)

    received = {0: None, 1: None}
    for hop in range(1, size):
        sent = {}
        for parity in (0, 1):
            if parity == 1 and hop == 1 and size % 2 == 0:
                sent[1] = None
                continue
            rightward = (me & 1) == parity
            index = jnp.where(rightward, size - hop + me, me - (size - hop))
            block = block_of(jnp.clip(index, 0, size - 1))
            sent[parity] = swap(joined(block, received[1 - parity], rightward), parity)
        received = sent
    total = block_of(me).astype(f32)
    for parity in (0, 1):
        if received[parity] is None:
            continue
        from_right = (me & 1) == parity
        keep = jnp.where(from_right, has[False], has[True])
        total = total + jnp.where(keep, received[parity].astype(f32), 0.0)
    return total.astype(bf16)


def scatter_head(partial_of):
    size = lax.axis_size("sample")
    first, second = chip_axes(size)

    def both(mask):
        other = flip(partial_of(mask | 1), "sample", 1)
        return partial_of(mask).astype(f32) + other.astype(f32)

    half = partial_of(0).shape[0] // 2
    extra = {}
    for a in first:
        for b in second:
            block = both(a | b).astype(bf16)
            extra.setdefault((b, 0), []).append(flip(block[:half], "sample", a))
            extra.setdefault((a, 1), []).append(flip(block[half:], "sample", b))
    totals = {0: [], 1: []}
    for mask in first + second:
        block = both(mask)
        parts = {0: block[:half], 1: block[half:]}
        for part in sorted((0, 1), key=lambda part: (mask, part) in extra):
            value = parts[part]
            for more in extra.get((mask, part), []):
                value = value + more.astype(f32)
            totals[part].append(flip(value.astype(bf16), "sample", mask))
    own = both(0)
    halves = [sum((t.astype(f32) for t in totals[part]), own[part * half : (part + 1) * half]) for part in (0, 1)]
    return jnp.concatenate(halves, axis=0).astype(bf16)


def logits_kernel(features_at, head_at, depth, tile, *refs):
    count_f, count_h = len(features_at), len(head_at)
    feature_refs = refs[:count_f]
    head_refs = refs[count_f : count_f + count_h]
    student_ref, slope_ref, sums_ref, whole, acc, student_sum, plan_sum = refs[count_f + count_h :]
    me, place = lax.axis_index("sample"), lax.axis_index("cls")
    groups = lax.axis_size("cls")
    width = feature_refs[0].shape[1]
    for (parity, hop), ref in zip(features_at, feature_refs):
        source = line_source(parity, hop, place, groups) if hop else place
        whole[:, pl.ds(pl.multiple_of(source * width, LANES), width)] = ref[...]
    student_sum[...] = jnp.zeros_like(student_sum)
    plan_sum[...] = jnp.zeros_like(plan_sum)
    tiles = student_ref.shape[1] // tile

    def product(i, slot):
        columns = pl.ds(pl.multiple_of(i * tile, tile), tile)
        total = None
        for (mask, offset), ref in zip(head_at, head_refs):
            first = pl.multiple_of((me ^ mask) * depth + offset, LANES)
            part = jnp.dot(
                whole[:, pl.ds(first, ref.shape[0])], ref[:, columns], preferred_element_type=f32
            )
            total = part if total is None else total + part
        acc[slot] = total

    def finish(i, slot):
        columns = pl.ds(pl.multiple_of(i * tile, tile), tile)
        tanh = jnp.tanh(acc[slot] * (1.0 / softcap))
        student = jnp.exp(softcap * tanh)
        plan = student * student
        student_ref[:, columns] = student
        slope_ref[:, columns] = (1.0 - tanh * tanh).astype(bf16)
        for first in range(0, tile, LANES):
            student_sum[...] += student[:, first : first + LANES]
            plan_sum[...] += plan[:, first : first + LANES]

    product(0, 0)

    def body(i, carry):
        slot = lax.rem(i, 2)
        product(i, slot)
        finish(i - 1, 1 - slot)
        return carry

    lax.fori_loop(1, tiles, body, 0)
    finish(tiles - 1, (tiles - 1) % 2)
    sums_ref[0:1, :] = jnp.sum(jnp.transpose(student_sum[...]), axis=0, keepdims=True)
    sums_ref[1:2, :] = jnp.sum(jnp.transpose(plan_sum[...]), axis=0, keepdims=True)


def in_vmem(values):
    return [pltpu.with_memory_space_constraint(value, VMEM) for value in values]


def whole_spec():
    return pl.BlockSpec(memory_space=VMEM)


def logits_call(feature_pieces, head_pieces, depth):
    rows = feature_pieces[0][2].shape[0]
    classes = head_pieces[0][2].shape[1]
    width = feature_pieces[0][2].shape[1] * lax.axis_size("cls")
    tile = min(256, classes)
    kernel = functools.partial(
        logits_kernel,
        [(parity, hop) for parity, hop, _ in feature_pieces],
        [(mask, offset) for mask, offset, _ in head_pieces],
        depth,
        tile,
    )
    operands = [block for _, _, block in feature_pieces] + [block for _, _, block in head_pieces]
    return pl.pallas_call(
        kernel,
        out_shape=(
            jax.ShapeDtypeStruct((rows, classes), f32),
            jax.ShapeDtypeStruct((rows, classes), bf16),
            jax.ShapeDtypeStruct((2, rows), f32),
        ),
        in_specs=[whole_spec()] * len(operands),
        out_specs=(whole_spec(),) * 3,
        scratch_shapes=[
            pltpu.VMEM((rows, width), bf16),
            pltpu.VMEM((2, rows, tile), f32),
            pltpu.VMEM((rows, LANES), f32),
            pltpu.VMEM((rows, LANES), f32),
        ],
        compiler_params=pltpu.CompilerParams(vmem_limit_bytes=48 << 20),
        cost_estimate=pl.CostEstimate(
            flops=2 * rows * width * classes, bytes_accessed=2 * width * classes, transcendentals=2 * rows * classes
        ),
    )(*in_vmem(operands))


def shares_kernel(head_at, depth, grad_ref, *refs):
    head_refs, shares_ref = refs[:-1], refs[-1]
    me = lax.axis_index("sample")
    width = shares_ref.shape[2]
    for (mask, offset), ref in zip(head_at, head_refs):
        first = (me ^ mask) * depth + offset
        block = first // width
        column = pl.multiple_of(first - block * width, LANES)
        product = lax.dot_general(
            grad_ref[...], ref[...], (((1,), (1,)), ((), ())), preferred_element_type=f32
        )
        shares_ref[block, :, pl.ds(column, ref.shape[0])] = product.astype(bf16)


def shares_call(grad_logits, head_pieces, depth, width):
    rows = grad_logits.shape[0]
    groups = lax.axis_size("cls")
    kernel = functools.partial(shares_kernel, [(mask, offset) for mask, offset, _ in head_pieces], depth)
    operands = [grad_logits] + [block for _, _, block in head_pieces]
    return pl.pallas_call(
        kernel,
        out_shape=jax.ShapeDtypeStruct((groups, rows, width), bf16),
        in_specs=[whole_spec()] * len(operands),
        out_specs=whole_spec(),
        compiler_params=pltpu.CompilerParams(vmem_limit_bytes=48 << 20),
        cost_estimate=pl.CostEstimate(
            flops=2 * rows * grad_logits.shape[1] * width * groups,
            bytes_accessed=2 * width * groups * grad_logits.shape[1],
            transcendentals=0,
        ),
    )(*in_vmem(operands))


def per_device(features, head, class_cap):
    local_rows, width = features.shape
    depth, class_local = head.shape
    sample_count = lax.axis_size("sample")
    class_groups = lax.axis_size("cls")
    ratio = local_rows * sample_count / (class_local * class_groups)
    me = lax.axis_index("sample")
    place = lax.axis_index("cls")
    aligned = depth % (2 * LANES) == 0 and width % (2 * LANES) == 0 and local_rows % LANES == 0

    head_pieces = gather_head(head)
    feature_pieces = gather_features(features)
    whole = jnp.zeros((local_rows, width * class_groups), bf16)
    for parity, hop, block in feature_pieces:
        source = line_source(parity, hop, place, class_groups) if hop else place
        whole = lax.dynamic_update_slice(whole, block, (0, source * width))

    if aligned:
        student, slope, sums = logits_call(feature_pieces, head_pieces, depth)
    else:
        head_full = jnp.zeros((depth * sample_count, class_local), bf16)
        for mask, offset, block in head_pieces:
            head_full = lax.dynamic_update_slice(head_full, block, ((me ^ mask) * depth + offset, 0))
        tanh = jnp.tanh(matmul(whole, head_full, ((1,), (0,))) / softcap)
        student = jnp.exp(softcap * tanh)
        slope = 1.0 - tanh * tanh
        sums = jnp.stack([jnp.sum(student, axis=1), jnp.sum(student * student, axis=1)])

    masses = row_total(sums)
    ceiling = class_cap.astype(f32) * ratio
    row_mass = masses[1]
    scale = jnp.ones((class_local,), f32)
    for iteration in range(ITERS):
        if iteration > 0:
            row_mass = row_total(jnp.sum(student * student * scale[None, :], axis=1))
        mass = column_total(jnp.sum(student * student * (1.0 / row_mass)[:, None], axis=0) * scale)
        scale = scale * jnp.minimum(1.0, ceiling / mass)
    row_mass = row_total(jnp.sum(student * student * scale[None, :], axis=1))
    targets = (student * student * scale[None, :] * (1.0 / row_mass)[:, None]).astype(bf16)
    grad_logits = (
        (student * (1.0 / masses[0])[:, None] - targets.astype(f32)) * slope.astype(f32)
    ).astype(bf16)

    def head_partial(mask):
        first = (me ^ mask) * depth
        columns = lax.dynamic_slice(whole, (0, first), (local_rows, depth))
        return matmul(columns, grad_logits, ((0,), (0,))).astype(bf16)

    partials = {mask: head_partial(mask) for mask in range(sample_count)}
    if aligned:
        shares = shares_call(grad_logits, head_pieces, depth, width)
    else:
        product = matmul(grad_logits, head_full, ((1,), (1,))).astype(bf16)
        shares = jnp.transpose(product.reshape(local_rows, class_groups, width), (1, 0, 2))

    def feature_block(index):
        return lax.dynamic_index_in_dim(shares, index, 0, keepdims=False)

    grad_features = scatter_features(feature_block)
    grad_head = scatter_head(lambda mask: partials[mask])
    return (targets, grad_features, grad_head)


def solution(mesh):
    return jax.shard_map(
        per_device,
        mesh=mesh,
        in_specs=(P("sample", "cls"), P("sample", "cls"), P("cls")),
        out_specs=(P("sample", "cls"), P("sample", "cls"), P("sample", "cls")),
        check_vma=False,
    )
```

```python
import jax
import jax.numpy as jnp
from jax import lax
from jax.sharding import PartitionSpec as P

ITERS = 3


softcap = 15.0
sharpen = 2.0
f32 = jnp.float32
bf16 = jnp.bfloat16


def matmul(left, right, dims):
    return lax.dot_general(left, right, (dims, ((), ())), preferred_element_type=f32)


def flip(value, mask):
    size = lax.axis_size("sample")
    return lax.ppermute(value, "sample", [(i, i ^ mask) for i in range(size)])


def swap(value, parity):
    samples, size = lax.axis_size("sample"), lax.axis_size("cls")
    pairs = []
    for sample in range(samples):
        for i in range(size):
            j = ((i + parity) ^ 1) - parity
            there = sample * size + j if 0 <= j < size else (sample ^ 1) * size + i
            pairs.append((sample * size + i, there))
    return lax.ppermute(value, ("sample", "cls"), pairs)


def total_over(value, axis):
    copies = jnp.broadcast_to(value[None], (lax.axis_size(axis),) + value.shape)
    return jnp.sum(lax.all_to_all(copies, axis, 0, 0), axis=0)


def row_total(value):
    return total_over(value, "cls")


def column_total(value):
    return total_over(value, "sample")


def after(value, *others):
    return lax.optimization_barrier((value,) + others)[0]


def chip_axes(size):
    chips = size // 2
    bits = chips.bit_length() - 1
    low = 1 << ((bits + 1) // 2)
    first = [2 * m for m in range(1, low)]
    second = [2 * low * m for m in range(1, chips // low)]
    return first, second


def gather_head(head):
    size = lax.axis_size("sample")
    first, second = chip_axes(size)
    half = head.shape[0] // 2
    held = {mask: flip(head, mask) for mask in first + second}
    same = [(0, 0, head)] + [(mask, 0, block) for mask, block in held.items()]
    for a in first:
        for b in second:
            same.append((a | b, 0, flip(held[a][:half], b)))
            same.append((a | b, half, flip(held[b][half:], a)))
    return same + [(mask | 1, offset, flip(block, 1)) for mask, offset, block in same]


def gather_features(features):
    size = lax.axis_size("cls")
    me = lax.axis_index("cls")
    rows, width = features.shape
    pieces = []
    even = odd = features
    for hop in range(1, size):
        even, odd = swap(odd, 0), swap(even, 1)
        pieces.append((0, hop, even))
        if hop < size - 1 or size % 2:
            pieces.append((1, hop, odd))
    whole = jnp.zeros((rows, width * size), features.dtype)
    for parity, hop, block in reversed(pieces):
        above, below = me + hop, me - hop
        above = jnp.where(above >= size, 2 * size - 1 - above, above)
        below = jnp.where(below < 0, -1 - below, below)
        source = jnp.where((me & 1) == parity, above, below)
        whole = lax.dynamic_update_slice(whole, block, (0, source * width))
    return lax.dynamic_update_slice(whole, features, (0, me * width))


def per_device(features, head, class_cap):
    local_rows, width = features.shape
    depth, class_local = head.shape
    samples = lax.axis_size("sample")
    groups = lax.axis_size("cls")
    ratio = local_rows * samples / (class_local * groups)
    me = lax.axis_index("sample")
    place = lax.axis_index("cls")
    first, second = chip_axes(samples)
    half = depth // 2

    pieces = {(mask, offset): block for mask, offset, block in gather_head(head)}
    whole = gather_features(features)
    parts, columns = [], []
    for mask in range(0, samples, 2):
        offsets = [offset for m, offset in pieces if m == mask]
        same = [pieces[mask, offset] for offset in offsets]
        other = [pieces[mask | 1, offset] for offset in offsets]
        lead = (me & 1) == 0
        parts += [jnp.where(lead, s, o) for s, o in zip(same, other)]
        parts += [jnp.where(lead, o, s) for s, o in zip(same, other)]
        columns.append(lax.dynamic_slice(whole, (0, ((me ^ mask) // 2) * 2 * depth), (local_rows, 2 * depth)))
    head_full = jnp.concatenate(parts, axis=0)
    wide = jnp.concatenate(columns, axis=1)

    logits = matmul(wide, head_full, ((1,), (0,)))
    tanh = jnp.tanh(logits / softcap)
    student = jnp.exp(softcap * tanh)
    plan = student * student
    masses = row_total(jnp.stack([jnp.sum(student, axis=1), jnp.sum(plan, axis=1)]))
    ceiling = class_cap.astype(f32) * ratio
    row_mass = masses[1]
    scale = jnp.ones((class_local,), f32)
    for iteration in range(ITERS):
        if iteration > 0:
            row_mass = row_total(jnp.sum(plan * scale[None, :], axis=1))
        mass = column_total(jnp.sum(plan * (1.0 / row_mass)[:, None], axis=0) * scale)
        scale = scale * jnp.minimum(1.0, ceiling / mass)
    row_mass = row_total(jnp.sum(plan * scale[None, :], axis=1))
    targets = (plan * scale[None, :] * (1.0 / row_mass)[:, None]).astype(bf16)
    slope = 1.0 - tanh * tanh
    grad = ((student * (1.0 / masses[0])[:, None] - targets.astype(f32)) * slope).astype(bf16)

    def head_partial(mask, grad):
        blocks = lax.dynamic_slice(whole, (0, (me ^ mask) * depth), (local_rows, depth))
        return matmul(blocks, grad, ((0,), (0,))).astype(bf16)

    def both(mask, grad):
        theirs = head_partial(mask | 1, grad)
        mine = head_partial(mask, grad)
        return mine, flip(theirs, 1)

    def share(index, grad):
        rows = lax.dynamic_slice(
            head_full, (((jnp.clip(index, 0, groups - 1) * width // (2 * depth)) ^ (me // 2)) * 2 * depth, 0), (width, class_local)
        )
        return matmul(grad, rows, ((1,), (1,)))

    extra = {}
    for a in first:
        for b in second:
            mine, theirs = both(a | b, grad)
            grad = after(grad, mine)
            block = (mine.astype(f32) + theirs.astype(f32)).astype(bf16)
            extra.setdefault((b, 0), []).append(flip(block[:half], a))
            extra.setdefault((a, 1), []).append(flip(block[half:], b))

    def line_block(hop, parity, grad):
        rightward = (place & 1) == parity
        index = jnp.where(rightward, groups - hop + place, place - (groups - hop))
        return rightward, share(index, grad)

    has_left, has_right = place > 0, place < groups - 1
    received = {0: None, 1: None}
    mixed = {}
    for hop in range(1, groups):
        sent = {0: None, 1: None}
        for parity in (0, 1):
            if parity == 1 and hop == 1 and groups % 2 == 0:
                continue
            rightward, block = line_block(hop, parity, grad)
            if received[1 - parity] is not None:
                keep = jnp.where(rightward, has_left, has_right)
                block = block + jnp.where(keep, received[1 - parity].astype(f32), 0.0)
            block = block.astype(bf16)
            grad = after(grad, block) if hop == 1 else grad
            sent[parity] = swap(block, parity)
        received = sent
        if hop == 1:
            for mask in first + second:
                mixed[mask] = both(mask, grad)
            mixed[0] = both(0, grad)
    total = share(place, grad)
    for parity in (0, 1):
        if received[parity] is not None:
            keep = jnp.where((place & 1) == parity, has_right, has_left)
            total = total + jnp.where(keep, received[parity].astype(f32), 0.0)
    grad_features = total.astype(bf16)

    total = mixed[0][0].astype(f32) + mixed[0][1].astype(f32)
    for mask in first + second:
        block = mixed[mask][0].astype(f32) + mixed[mask][1].astype(f32)
        halves = [block[:half], block[half:]]
        for part in (0, 1):
            for more in extra.get((mask, part), []):
                halves[part] = halves[part] + more.astype(f32)
        total = total + flip(jnp.concatenate(halves, axis=0).astype(bf16), mask).astype(f32)
    return (targets, grad_features, total.astype(bf16))


def solution(mesh):
    return jax.shard_map(
        per_device,
        mesh=mesh,
        in_specs=(P("sample", "cls"), P("sample", "cls"), P("cls")),
        out_specs=(P("sample", "cls"), P("sample", "cls"), P("sample", "cls")),
        check_vma=False,
    )
```

```python
import jax
import jax.numpy as jnp
from jax import lax
from jax.sharding import PartitionSpec as P

ITERS = 3


softcap = 15.0
sharpen = 2.0
f32 = jnp.float32
bf16 = jnp.bfloat16


def matmul(left, right, dims):
    return lax.dot_general(left, right, (dims, ((), ())), preferred_element_type=f32)


def flip(value, mask):
    size = lax.axis_size("sample")
    return lax.ppermute(value, "sample", [(i, i ^ mask) for i in range(size)])


def swap(value, parity):
    samples, size = lax.axis_size("sample"), lax.axis_size("cls")
    pairs = []
    for sample in range(samples):
        for i in range(size):
            j = ((i + parity) ^ 1) - parity
            there = sample * size + j if 0 <= j < size else (sample ^ 1) * size + i
            pairs.append((sample * size + i, there))
    return lax.ppermute(value, ("sample", "cls"), pairs)


def row_total(value):
    return jnp.sum(lax.all_gather(value, "cls", axis=0), axis=0)


def column_total(value):
    value = value + flip(value, 1)
    return sum([flip(value, mask) for mask in range(2, lax.axis_size("sample"), 2)], value)


def after(value, *others):
    return lax.optimization_barrier((value,) + others)[0]


def wide(value):
    return value.astype(f32)


def chip_axes(size):
    chips = size // 2
    bits = chips.bit_length() - 1
    low = 1 << ((bits + 1) // 2)
    first = [2 * m for m in range(1, low)]
    second = [2 * low * m for m in range(1, chips // low)]
    return first, second


def gather_head(head):
    size = lax.axis_size("sample")
    first, second = chip_axes(size)
    half = head.shape[0] // 2
    held = {mask: flip(head, mask) for mask in first + second}
    same = [(0, 0, head)] + [(mask, 0, block) for mask, block in held.items()]
    for a in first:
        for b in second:
            same.append((a | b, 0, flip(held[a][:half], b)))
            same.append((a | b, half, flip(held[b][half:], a)))
    return same + [(mask | 1, offset, flip(block, 1)) for mask, offset, block in same]


def cut(value):
    half = value.shape[0] // 2
    return value[:half], value[half:]


def gather_features(features):
    size = lax.axis_size("cls")
    me = lax.axis_index("cls")
    rows, width = features.shape
    pieces = []
    even = odd = cut(features)
    for hop in range(1, size):
        even, odd = [swap(part, 0) for part in odd], [swap(part, 1) for part in even]
        pieces.append((0, hop, even))
        if hop < size - 1 or size % 2:
            pieces.append((1, hop, odd))
    whole = jnp.zeros((size, rows, width), features.dtype)
    for parity, hop, parts in reversed(pieces):
        above, below = me + hop, me - hop
        above = jnp.where(above >= size, 2 * size - 1 - above, above)
        below = jnp.where(below < 0, -1 - below, below)
        source = jnp.where((me & 1) == parity, above, below)
        for i, part in enumerate(parts):
            whole = lax.dynamic_update_slice(whole, part[None], (source, i * (rows // 2), 0))
    return lax.dynamic_update_slice(whole, features[None], (me, 0, 0))


def per_device(features, head, class_cap):
    local_rows, width = features.shape
    depth, class_local = head.shape
    samples = lax.axis_size("sample")
    groups = lax.axis_size("cls")
    ratio = local_rows * samples / (class_local * groups)
    me = lax.axis_index("sample")
    place = lax.axis_index("cls")
    chip, core = me // 2, me & 1
    first, second = chip_axes(samples)
    half = depth // 2

    pieces = {(mask, offset): block for mask, offset, block in gather_head(head)}
    blocks = gather_features(features)

    def feature_columns(start, count):
        group = start // width
        return lax.dynamic_slice(blocks, (group, 0, start - group * width), (1, local_rows, count))[0]

    heads, logits = {}, None
    for mask in sorted({m for m, _ in pieces if m % 2 == 0}, key=lambda m: (bin(m).count("1"), m)):
        offsets = [offset for m, offset in pieces if m == mask]
        same = [pieces[mask, offset] for offset in offsets]
        other = [pieces[mask | 1, offset] for offset in offsets]
        parts = [jnp.where(core == 0, s, o) for s, o in zip(same, other)]
        parts += [jnp.where(core == 0, o, s) for s, o in zip(same, other)]
        heads[mask] = lax.optimization_barrier(jnp.concatenate(parts, axis=0))
        product = matmul(feature_columns((chip ^ (mask // 2)) * 2 * depth, 2 * depth), heads[mask], ((1,), (0,)))
        logits = product if logits is None else logits + product

    tanh = jnp.tanh(logits / softcap)
    student = jnp.exp(softcap * tanh)
    slope = (1.0 - tanh * tanh).astype(bf16)
    sums = jnp.stack([jnp.sum(student, axis=1), jnp.sum(student * student, axis=1)])
    student, slope, sums = lax.optimization_barrier((student, slope, sums))
    masses = row_total(sums)
    ceiling = class_cap.astype(f32) * ratio
    row_mass = masses[1]
    scale = jnp.ones((class_local,), f32)
    for iteration in range(ITERS):
        if iteration > 0:
            row_mass = row_total(jnp.sum(student * student * scale[None, :], axis=1))
        mass = column_total(jnp.sum(student * student * (1.0 / row_mass)[:, None], axis=0) * scale)
        scale = scale * jnp.minimum(1.0, ceiling / mass)
    row_mass = row_total(jnp.sum(student * student * scale[None, :], axis=1))
    targets = (student * student * scale[None, :] * (1.0 / row_mass)[:, None]).astype(bf16)
    grad = ((student * (1.0 / masses[0])[:, None] - wide(targets)) * wide(slope)).astype(bf16)

    def head_partial(mask, grad):
        return matmul(feature_columns((me ^ mask) * depth, depth), grad, ((0,), (0,))).astype(bf16)

    def both(mask, grad):
        theirs = head_partial(mask | 1, grad)
        mine = head_partial(mask, grad)
        return mine, flip(theirs, 1), (mine, theirs)

    stacked = jnp.stack([heads[mask] for mask in range(0, samples, 2)])

    def share(index, grad):
        start = jnp.clip(index, 0, groups - 1) * width
        group = start // (2 * depth)
        rows = lax.dynamic_slice(stacked, (group ^ chip, start - group * 2 * depth, 0), (1, width, class_local))[0]
        return matmul(grad, rows, ((1,), (1,))).astype(bf16)

    def line_share(hop, parity, grad):
        index = jnp.where((place & 1) == parity, groups - hop + place, place - (groups - hop))
        return share(index, grad)

    diagonal = {}
    for a in first:
        for b in second:
            mine, theirs, made = both(a | b, grad)
            grad = after(grad, *made)
            diagonal[a, b] = mine, theirs
    hops = [(hop, parity) for hop in range(1, groups) for parity in (0, 1)]
    hops = [(hop, parity) for hop, parity in hops if not (parity and hop == 1 and groups % 2 == 0)]
    shares = {at: line_share(*at, grad) for at in hops if at[0] == 1}
    sums = {at: (wide(mine) + wide(theirs)).astype(bf16) for at, (mine, theirs) in diagonal.items()}
    ready = lax.optimization_barrier(tuple(sums.values()) + tuple(shares.values()) + (grad,))
    grad = ready[-1]
    sums, shares = dict(zip(list(sums), ready)), dict(zip(list(shares), ready[len(sums):]))
    extra = {}
    for (a, b), block in sums.items():
        top, bottom = cut(block)
        extra.setdefault((b, 0), []).append(flip(top, a))
        extra.setdefault((a, 1), []).append(flip(bottom, b))

    mixed = {}
    for mask in first + second + [0]:
        mine, theirs, made = both(mask, grad)
        grad = after(grad, *made)
        mixed[mask] = mine, theirs
    rest = [at for at in hops if at[0] > 1]
    late = lax.optimization_barrier(tuple(line_share(*at, grad) for at in rest) + (share(place, grad),))
    own_share = late[-1]

    totals = {0: [], 1: []}
    waiting = []
    for mask in first + second:
        parts = cut(wide(mixed[mask][0]) + wide(mixed[mask][1]))
        for part in (0, 1):
            if (mask, part) in extra:
                waiting.append((mask, part, parts[part]))
            else:
                totals[part].append(flip(parts[part].astype(bf16), mask))
    own = cut(lax.optimization_barrier(wide(mixed[0][0]) + wide(mixed[0][1])))

    has_left, has_right = place > 0, place < groups - 1
    received = {0: None, 1: None}
    late = dict(zip(rest, late))
    for hop in range(1, groups):
        sent = {0: None, 1: None}
        for parity in (0, 1):
            if (hop, parity) not in hops:
                continue
            parts = cut(shares[hop, parity] if hop == 1 else late[hop, parity])
            if received[1 - parity] is not None:
                keep = jnp.where((place & 1) == parity, has_left, has_right)
                parts = [
                    (wide(part) + jnp.where(keep, wide(more), 0.0)).astype(bf16)
                    for part, more in zip(parts, received[1 - parity])
                ]
            sent[parity] = [swap(part, parity) for part in parts]
        received = sent
    totals_f = [wide(part) for part in cut(own_share)]
    for parity in (0, 1):
        if received[parity] is not None:
            keep = jnp.where((place & 1) == parity, has_right, has_left)
            totals_f = [t + jnp.where(keep, wide(more), 0.0) for t, more in zip(totals_f, received[parity])]
    grad_features = jnp.concatenate(totals_f, axis=0).astype(bf16)

    for mask, part, value in waiting:
        for more in extra[mask, part]:
            value = value + wide(more)
        totals[part].append(flip(value.astype(bf16), mask))
    halves = [sum([wide(t) for t in totals[part]], own[part]) for part in (0, 1)]
    grad_head = jnp.concatenate(halves, axis=0).astype(bf16)
    return (targets, grad_features, grad_head)


def solution(mesh):
    return jax.shard_map(
        per_device,
        mesh=mesh,
        in_specs=(P("sample", "cls"), P("sample", "cls"), P("cls")),
        out_specs=(P("sample", "cls"), P("sample", "cls"), P("sample", "cls")),
        check_vma=False,
    )
```

```python
import functools

import jax
import jax.numpy as jnp
from jax import lax
from jax.experimental import pallas as pl
from jax.experimental.pallas import tpu as pltpu
from jax.sharding import PartitionSpec as P

ITERS = 3


softcap = 15.0
sharpen = 2.0
f32 = jnp.float32
bf16 = jnp.bfloat16
LANES = 128


def wide(value):
    return value.astype(f32)


def matmul(left, right, dims):
    return lax.dot_general(left, right, (dims, ((), ())), preferred_element_type=f32)


def flip(value, axis, mask):
    return lax.ppermute(value, axis, [(i, i ^ mask) for i in range(lax.axis_size(axis))])


def cut(value):
    half = value.shape[0] // 2
    return value[:half], value[half:]


def chip_axes(size):
    chips = size // 2
    bits = chips.bit_length() - 1
    low = 1 << ((bits + 1) // 2)
    first = [2 * m for m in range(1, low)]
    second = [2 * low * m for m in range(1, chips // low)]
    return first, second


def gather_head(head):
    size = lax.axis_size("sample")
    first, second = chip_axes(size)
    held = {mask: [flip(head, "sample", mask)] for mask in first + second}
    held[0] = [head]
    for a in first:
        for b in second:
            top, bottom = cut(held[a][0])[0], cut(held[b][0])[1]
            held[a | b] = [flip(top, "sample", b), flip(bottom, "sample", a)]
    for mask in list(held):
        held[mask | 1] = [flip(part, "sample", 1) for part in held[mask]]
    return held


def gather_features(features):
    size = lax.axis_size("cls")
    held = {0: features}
    for mask in list(range(2, size, 2)) + [1]:
        held[mask] = flip(features, "cls", mask)
    for mask in range(2, size, 2):
        held[mask | 1] = flip(held[mask], "cls", 1)
    return [held[mask] for mask in range(size)]


def fast(value):
    return pltpu.with_memory_space_constraint(value, pltpu.VMEM)


def call(kernel, outputs, operands, scratch=(), extra=(), limit=24):
    spec = pl.BlockSpec(memory_space=pltpu.VMEM)
    return pl.pallas_call(
        kernel,
        out_shape=tuple(pltpu.VMEM(shape, dtype) for shape, dtype in outputs),
        in_specs=[spec] * len(operands) + [pl.BlockSpec(memory_space=pl.ANY)] * len(extra),
        out_specs=(spec,) * len(outputs),
        scratch_shapes=list(scratch),
        compiler_params=pltpu.CompilerParams(vmem_limit_bytes=limit << 20),
        cost_estimate=pl.CostEstimate(flops=1, bytes_accessed=1, transcendentals=0),
    )(*[fast(operand) for operand in operands], *extra)


def as_column(row):
    return jnp.transpose(jnp.broadcast_to(row, (LANES, row.shape[1])))


def row_kernel(count, student_ref, scale_ref, ceiling_ref, *refs):
    part_refs, (new_ref, total_ref, partial) = refs[:count], refs[count:]
    mass = part_refs[0][...]
    for ref in part_refs[1:]:
        mass = mass + ref[...]
    new_ref[...] = scale_ref[...] * jnp.minimum(1.0, ceiling_ref[...] / mass)
    rows, columns = student_ref.shape
    block = 64

    def body(i, carry):
        at = pl.ds(pl.multiple_of(i * block, block), block)
        total = jnp.zeros((block, LANES), f32)
        for j in range(0, columns, LANES):
            value = student_ref[at, j : j + LANES]
            total = total + value * value * new_ref[:, j : j + LANES]
        partial[at, :] = total
        return carry

    lax.fori_loop(0, rows // block, body, 0)
    total_ref[...] = jnp.sum(jnp.transpose(partial[...]), axis=0, keepdims=True)


def column_kernel(count, student_ref, scale_ref, *refs):
    part_refs, (total_ref, inverse) = refs[:count], refs[count:]
    mass = part_refs[0][...]
    for ref in part_refs[1:]:
        mass = mass + ref[...]
    inverse[...] = as_column(1.0 / mass)
    rows, columns = student_ref.shape
    block = 8

    def body(i, total):
        at = pl.ds(pl.multiple_of(i * block, block), block)
        factor = inverse[at, :]
        new = []
        for j in range(0, columns, LANES):
            value = student_ref[at, j : j + LANES]
            new.append(total[j // LANES] + value * value * factor)
        return tuple(new)

    start = tuple(jnp.zeros((block, LANES), f32) for _ in range(0, columns, LANES))
    total = lax.fori_loop(0, rows // block, body, start, unroll=4)
    for j, value in enumerate(total):
        at = slice(j * LANES, (j + 1) * LANES)
        total_ref[:, at] = jnp.sum(value, axis=0, keepdims=True) * scale_ref[:, at]


def split_by_core(result, core, depth):
    top, bottom = result[:depth], result[depth:]
    return jnp.where(core == 0, top, bottom), jnp.where(core == 0, bottom, top)


def gradient_kernel(count, depth, far, masks, student_ref, slope_ref, scale_ref, students_ref, turned_ref, *refs):
    part_refs, head_refs = refs[:count], refs[count : count + len(masks)]
    targets_ref, grad_ref, mine_ref, theirs_ref, share_ref, inverse, students = refs[count + len(masks) :]
    me, place = lax.axis_index("sample"), lax.axis_index("cls")
    chip, core = me // 2, me % 2
    groups = lax.axis_size("cls")
    mass = part_refs[0][...]
    for ref in part_refs[1:]:
        mass = mass + ref[...]
    inverse[...] = as_column(1.0 / mass)
    students[...] = as_column(1.0 / students_ref[...])
    columns = student_ref.shape[1]
    tile = min(256, columns)
    turned = turned_ref.at[place ^ chip ^ far]

    def body(i, carry):
        for j in range(0, tile, LANES):
            at = pl.ds(pl.multiple_of(i * tile + j, LANES), LANES)
            student = student_ref[:, at]
            target = (student * student * scale_ref[:, at] * inverse[...]).astype(bf16)
            targets_ref[:, at] = target
            grad_ref[:, at] = ((student * students[...] - wide(target)) * wide(slope_ref[:, at])).astype(bf16)
        at = pl.ds(pl.multiple_of(i * tile, tile), tile)
        result = jnp.dot(turned[...], grad_ref[:, at], preferred_element_type=f32)
        mine, theirs = split_by_core(result, core, depth)
        mine_ref[:, at] = mine.astype(bf16)
        theirs_ref[:, at] = theirs.astype(bf16)
        return carry

    lax.fori_loop(0, columns // tile, body, 0)
    for mask, ref in zip(masks, head_refs):

        @pl.when((chip ^ mask) == (place ^ (groups - 1)))
        def _():
            share_ref[...] = matmul(grad_ref[...], ref[...], ((1,), (1,))).astype(bf16)


def products_kernel(count, depth, near, masks, grad_ref, turned_ref, *refs):
    head_refs, refs = refs[: len(masks)], refs[len(masks) + count :]
    pairs, (shares_ref,) = refs[:-1], refs[-1:]
    me, place = lax.axis_index("sample"), lax.axis_index("cls")
    chip, core = me // 2, me % 2
    columns = grad_ref.shape[1]
    tile = min(256, columns)
    for index, mask in enumerate(near):
        mine_ref, theirs_ref = pairs[2 * index], pairs[2 * index + 1]
        turned = turned_ref.at[place ^ chip ^ mask]

        def body(i, carry):
            at = pl.ds(pl.multiple_of(i * tile, tile), tile)
            result = jnp.dot(turned[...], grad_ref[:, at], preferred_element_type=f32)
            mine, theirs = split_by_core(result, core, depth)
            mine_ref[:, at] = mine.astype(bf16)
            theirs_ref[:, at] = theirs.astype(bf16)
            return carry

        lax.fori_loop(0, columns // tile, body, 0)
    for mask, ref in zip(masks, head_refs):
        shares_ref[chip ^ mask ^ place] = matmul(grad_ref[...], ref[...], ((1,), (1,))).astype(bf16)


def per_device(features, head, class_cap):
    rows, width = features.shape
    depth, classes = head.shape
    samples = lax.axis_size("sample")
    groups = lax.axis_size("cls")
    ratio = rows * samples / (classes * groups)
    me = lax.axis_index("sample")
    place = lax.axis_index("cls")
    chip, core = me // 2, me % 2
    first, second = chip_axes(samples)

    pieces = gather_head(head)
    blocks = jnp.stack(gather_features(features))

    order = [0] + first + second + [a | b for a in first for b in second]
    heads, logits = {}, None
    for mask in order:
        same, other = pieces[mask], pieces[mask | 1]
        parts = [jnp.where(core == 0, s, o) for s, o in zip(same, other)]
        parts += [jnp.where(core == 0, o, s) for s, o in zip(same, other)]
        heads[mask] = lax.optimization_barrier(jnp.concatenate(parts, axis=0))
        group = lax.dynamic_index_in_dim(blocks, chip ^ (mask // 2) ^ place, 0, keepdims=False)
        product = matmul(group, heads[mask], ((1,), (0,)))
        logits = product if logits is None else logits + product

    tanh = jnp.tanh(logits / softcap)
    student = jnp.exp(softcap * tanh)
    slope = (1.0 - tanh * tanh).astype(bf16)
    sums = jnp.stack([jnp.sum(student, axis=1), jnp.sum(student * student, axis=1)])
    student, slope, sums = lax.optimization_barrier((student, slope, sums))
    turned = lax.optimization_barrier(jnp.transpose(blocks, (0, 2, 1)))

    def row_parts(value):
        return [value] + [flip(value, "cls", mask) for mask in range(1, groups)]

    def column_parts(value):
        value = value + flip(value, "sample", 1)
        return [value] + [flip(value, "sample", mask) for mask in range(2, samples, 2)]

    ceiling = (wide(class_cap) * ratio)[None]
    parts = row_parts(sums)
    students_mass = sum([part[0:1] for part in parts[1:]], parts[0][0:1])
    parts = [part[1:2] for part in parts]
    scale = jnp.ones((1, classes), f32)
    for _ in range(ITERS):
        (mass,) = call(
            functools.partial(column_kernel, len(parts)),
            [((1, classes), f32)],
            [student, scale] + parts,
            [pltpu.VMEM((rows, LANES), f32)],
        )
        sent = column_parts(mass)
        scale, mass = call(
            functools.partial(row_kernel, len(sent)),
            [((1, classes), f32), ((1, rows), f32)],
            [student, scale, ceiling] + sent,
            [pltpu.VMEM((rows, LANES), f32)],
        )
        parts = row_parts(mass)

    chip_masks = [mask // 2 for mask in order]
    head_list = [heads[mask] for mask in order]
    near = [mask // 2 for mask in first + second] + [0]
    diagonal = [(a, b) for a in first for b in second]
    far = (diagonal[-1][0] | diagonal[-1][1]) // 2
    near = [(a | b) // 2 for a, b in diagonal[:-1]] + near
    targets, grad, mine, theirs, share = call(
        functools.partial(gradient_kernel, len(parts), depth, far, chip_masks),
        [((rows, classes), bf16)] * 2 + [((depth, classes), bf16)] * 2 + [((rows, width), bf16)],
        [student, slope, scale, students_mass, turned] + parts + head_list,
        [pltpu.VMEM((rows, LANES), f32)] * 2,
    )
    extra = {}

    def send_diagonal(a, b, top, bottom):
        extra.setdefault((b, 0), []).append(flip(top, "sample", a))
        extra.setdefault((a, 1), []).append(flip(bottom, "sample", b))

    block = (wide(mine) + wide(flip(theirs, "sample", 1))).astype(bf16)
    halves = lax.optimization_barrier(cut(block))
    send_diagonal(*diagonal[-1], *halves)
    share_from = {groups - 2: flip(share, "cls", 1)}

    results = call(
        functools.partial(products_kernel, len(halves), depth, near, chip_masks),
        [((depth, classes), bf16)] * (2 * len(near)) + [((groups, rows, width), bf16)],
        [grad, turned] + head_list,
        extra=halves,
    )
    shares = results[-1]
    mixed = {
        2 * mask: wide(results[2 * i]) + wide(flip(results[2 * i + 1], "sample", 1)) for i, mask in enumerate(near)
    }
    for a, b in diagonal[:-1]:
        send_diagonal(a, b, *cut(mixed[a | b].astype(bf16)))

    total = wide(shares[0]) + wide(flip(shares[1], "cls", 1))
    for mask in range(2, groups, 2):
        received = share_from[mask] if mask in share_from else flip(shares[mask | 1], "cls", 1)
        total = total + wide(flip((wide(shares[mask]) + wide(received)).astype(bf16), "cls", mask))
    grad_features = total.astype(bf16)

    halves = list(cut(mixed[0]))
    for late in (False, True):
        for mask in first + second:
            for part, value in enumerate(cut(mixed[mask])):
                if ((mask, part) in extra) == late:
                    for more in extra.get((mask, part), []):
                        value = value + wide(more)
                    halves[part] = halves[part] + wide(flip(value.astype(bf16), "sample", mask))
    grad_head = jnp.concatenate(halves, axis=0).astype(bf16)
    return (targets, grad_features, grad_head)


def solution(mesh):
    return jax.shard_map(
        per_device,
        mesh=mesh,
        in_specs=(P("sample", "cls"), P("sample", "cls"), P("cls")),
        out_specs=(P("sample", "cls"), P("sample", "cls"), P("sample", "cls")),
        check_vma=False,
    )
```

```python
import functools

import jax
import jax.numpy as jnp
from jax import lax
from jax.experimental import pallas as pl
from jax.experimental.pallas import tpu as pltpu
from jax.sharding import PartitionSpec as P

ITERS = 3


softcap = 15.0
sharpen = 2.0
f32 = jnp.float32
bf16 = jnp.bfloat16
LANES = 128


def wide(value):
    return value.astype(f32)


def matmul(left, right, dims):
    return lax.dot_general(left, right, (dims, ((), ())), preferred_element_type=f32)


def flip(value, axis, mask):
    return lax.ppermute(value, axis, [(i, i ^ mask) for i in range(lax.axis_size(axis))])


def cut(value):
    half = value.shape[0] // 2
    return value[:half], value[half:]


def chip_axes(size):
    chips = size // 2
    bits = chips.bit_length() - 1
    low = 1 << ((bits + 1) // 2)
    first = [2 * m for m in range(1, low)]
    second = [2 * low * m for m in range(1, chips // low)]
    return first, second


def gather_head(head):
    size = lax.axis_size("sample")
    first, second = chip_axes(size)
    held = {mask: [flip(head, "sample", mask)] for mask in first + second}
    held[0] = [head]
    for a in first:
        for b in second:
            top, bottom = cut(held[a][0])[0], cut(held[b][0])[1]
            held[a | b] = [flip(top, "sample", b), flip(bottom, "sample", a)]
    return held


def gather_features(features):
    size = lax.axis_size("cls")
    held = {0: features}
    for mask in list(range(2, size, 2)) + [1]:
        held[mask] = flip(features, "cls", mask)
    for mask in range(2, size, 2):
        held[mask | 1] = flip(held[mask], "cls", 1)
    return [held[mask] for mask in range(size)]


def fast(value):
    return pltpu.with_memory_space_constraint(value, pltpu.VMEM)


def call(kernel, outputs, operands, scratch=(), extra=(), limit=24):
    spec = pl.BlockSpec(memory_space=pltpu.VMEM)
    return pl.pallas_call(
        kernel,
        out_shape=tuple(pltpu.VMEM(shape, dtype) for shape, dtype in outputs),
        in_specs=[spec] * len(operands) + [pl.BlockSpec(memory_space=pl.ANY)] * len(extra),
        out_specs=(spec,) * len(outputs),
        scratch_shapes=list(scratch),
        compiler_params=pltpu.CompilerParams(vmem_limit_bytes=limit << 20),
        cost_estimate=pl.CostEstimate(flops=1, bytes_accessed=1, transcendentals=0),
    )(*[fast(operand) for operand in operands], *extra)


def as_column(row):
    return jnp.transpose(jnp.broadcast_to(row, (LANES, row.shape[1])))


def row_kernel(count, student_ref, scale_ref, ceiling_ref, *refs):
    part_refs, (new_ref, total_ref, partial) = refs[:count], refs[count:]
    mass = part_refs[0][...]
    for ref in part_refs[1:]:
        mass = mass + ref[...]
    new_ref[...] = scale_ref[...] * jnp.minimum(1.0, ceiling_ref[...] / mass)
    rows, columns = student_ref.shape
    block = 64

    def body(i, carry):
        at = pl.ds(pl.multiple_of(i * block, block), block)
        total = jnp.zeros((block, LANES), f32)
        for j in range(0, columns, LANES):
            value = student_ref[at, j : j + LANES]
            total = total + value * value * new_ref[:, j : j + LANES]
        partial[at, :] = total
        return carry

    lax.fori_loop(0, rows // block, body, 0)
    total_ref[...] = jnp.sum(jnp.transpose(partial[...]), axis=0, keepdims=True)


def turn_kernel(blocks_ref, turned_ref):
    for i in range(blocks_ref.shape[0]):
        turned_ref[i] = jnp.transpose(blocks_ref[i])


def column_kernel(count, early, student_ref, scale_ref, *refs):
    part_refs, (total_ref, inverse) = refs[:count], refs[count + early :]
    mass = part_refs[0][...]
    for ref in part_refs[1:]:
        mass = mass + ref[...]
    inverse[...] = as_column(1.0 / mass)
    rows, columns = student_ref.shape
    block = 8

    def body(i, total):
        at = pl.ds(pl.multiple_of(i * block, block), block)
        factor = inverse[at, :]
        new = []
        for j in range(0, columns, LANES):
            value = student_ref[at, j : j + LANES]
            new.append(total[j // LANES] + value * value * factor)
        return tuple(new)

    start = tuple(jnp.zeros((block, LANES), f32) for _ in range(0, columns, LANES))
    total = lax.fori_loop(0, rows // block, body, start, unroll=4)
    for j, value in enumerate(total):
        at = slice(j * LANES, (j + 1) * LANES)
        total_ref[:, at] = jnp.sum(value, axis=0, keepdims=True) * scale_ref[:, at]


def head_products(turned_ref, core, depth, grad_ref, at, mine_ref, theirs_ref):
    for where, out_ref in ((core, mine_ref), (1 - core, theirs_ref)):
        left = turned_ref[pl.ds(pl.multiple_of(where * depth, depth), depth), :]
        out_ref[:, at] = jnp.dot(left, grad_ref[:, at], preferred_element_type=f32).astype(bf16)


def gradient_kernel(count, depth, far, masks, student_ref, slope_ref, scale_ref, students_ref, turned_ref, *refs):
    part_refs, head_refs = refs[:count], refs[count : count + len(masks)]
    targets_ref, grad_ref, mine_ref, theirs_ref, share_ref, inverse, students = refs[count + len(masks) :]
    me, place = lax.axis_index("sample"), lax.axis_index("cls")
    chip, core = me // 2, me % 2
    groups = lax.axis_size("cls")
    mass = part_refs[0][...]
    for ref in part_refs[1:]:
        mass = mass + ref[...]
    inverse[...] = as_column(1.0 / mass)
    students[...] = as_column(1.0 / students_ref[...])
    columns = student_ref.shape[1]
    tile = min(256, columns)
    turned = turned_ref.at[place ^ chip ^ far]

    for i in range(0, columns, tile):
        for j in range(i, i + tile, LANES):
            at = slice(j, j + LANES)
            student = student_ref[:, at]
            target = (student * student * scale_ref[:, at] * inverse[...]).astype(bf16)
            targets_ref[:, at] = target
            grad_ref[:, at] = ((student * students[...] - wide(target)) * wide(slope_ref[:, at])).astype(bf16)
        head_products(turned, core, depth, grad_ref, slice(i, i + tile), mine_ref, theirs_ref)
    for mask, ref in zip(masks, head_refs):

        @pl.when((chip ^ mask) == (place ^ (groups - 1)))
        def _():
            share_ref[...] = matmul(grad_ref[...], ref[...], ((1,), (1,))).astype(bf16)


def products_kernel(count, depth, near, masks, grad_ref, turned_ref, *refs):
    head_refs, refs = refs[: len(masks)], refs[len(masks) + count :]
    pairs, (shares_ref,) = refs[:-1], refs[-1:]
    me, place = lax.axis_index("sample"), lax.axis_index("cls")
    chip, core = me // 2, me % 2
    columns = grad_ref.shape[1]
    tile = min(256, columns)
    for index, mask in enumerate(near):
        mine_ref, theirs_ref = pairs[2 * index], pairs[2 * index + 1]
        turned = turned_ref.at[place ^ chip ^ mask]
        for i in range(0, columns, tile):
            head_products(turned, core, depth, grad_ref, slice(i, i + tile), mine_ref, theirs_ref)
    for mask, ref in zip(masks, head_refs):
        shares_ref[chip ^ mask ^ place] = matmul(grad_ref[...], ref[...], ((1,), (1,))).astype(bf16)


def per_device(features, head, class_cap):
    rows, width = features.shape
    depth, classes = head.shape
    samples = lax.axis_size("sample")
    groups = lax.axis_size("cls")
    ratio = rows * samples / (classes * groups)
    me = lax.axis_index("sample")
    place = lax.axis_index("cls")
    chip, core = me // 2, me % 2
    first, second = chip_axes(samples)

    pieces = gather_head(head)
    blocks = jnp.stack(gather_features(features))

    order = [0] + first + second + [a | b for a in first for b in second]
    heads, logits = {}, None
    for mask in order:
        same = pieces[mask]
        if len(same) > 1:
            same = list(lax.optimization_barrier((logits, *same))[1:])
        other = [flip(part, "sample", 1) for part in same]
        parts = [jnp.where(core == 0, s, o) for s, o in zip(same, other)]
        parts += [jnp.where(core == 0, o, s) for s, o in zip(same, other)]
        heads[mask] = lax.optimization_barrier(jnp.concatenate(parts, axis=0))
        group = lax.dynamic_index_in_dim(blocks, chip ^ (mask // 2) ^ place, 0, keepdims=False)
        product = matmul(group, heads[mask], ((1,), (0,)))
        logits = product if logits is None else logits + product

    tanh = jnp.tanh(logits / softcap)
    student = jnp.exp(softcap * tanh)
    slope = (1.0 - tanh * tanh).astype(bf16)
    sums = jnp.stack([jnp.sum(student, axis=1), jnp.sum(student * student, axis=1)])
    student, slope, sums = lax.optimization_barrier((student, slope, sums))
    (turned,) = call(turn_kernel, [((groups, width, rows), bf16)], [blocks])

    def row_parts(value):
        return [value] + [flip(value, "cls", mask) for mask in range(groups - 1, 0, -1)]

    def column_parts(value):
        value = value + flip(value, "sample", 1)
        return [value] + [flip(value, "sample", mask) for mask in range(samples - 2, 0, -2)]

    ceiling = (wide(class_cap) * ratio)[None]
    parts = row_parts(sums)
    students_mass = sum([part[0:1] for part in parts[1:]], parts[0][0:1])
    parts = [part[1:2] for part in parts]
    scale = jnp.ones((1, classes), f32)
    for iteration in range(ITERS):
        early = [turned] if iteration == 0 else []
        (mass,) = call(
            functools.partial(column_kernel, len(parts), len(early)),
            [((1, classes), f32)],
            [student, scale] + parts,
            [pltpu.VMEM((rows, LANES), f32)],
            early,
        )
        sent = column_parts(mass)
        scale, mass = call(
            functools.partial(row_kernel, len(sent)),
            [((1, classes), f32), ((1, rows), f32)],
            [student, scale, ceiling] + sent,
            [pltpu.VMEM((rows, LANES), f32)],
        )
        parts = row_parts(mass)

    chip_masks = [mask // 2 for mask in order]
    head_list = [heads[mask] for mask in order]
    near = [mask // 2 for mask in first + second] + [0]
    diagonal = [(a, b) for a in first for b in second]
    far = (diagonal[-1][0] | diagonal[-1][1]) // 2
    near = [(a | b) // 2 for a, b in diagonal[:-1]] + near
    targets, grad, mine, theirs, share = call(
        functools.partial(gradient_kernel, len(parts), depth, far, chip_masks),
        [((rows, classes), bf16)] * 2 + [((depth, classes), bf16)] * 2 + [((rows, width), bf16)],
        [student, slope, scale, students_mass, turned] + parts + head_list,
        [pltpu.VMEM((rows, LANES), f32)] * 2,
    )
    extra = {}

    def send_diagonal(a, b, top, bottom):
        extra.setdefault((b, 0), []).append(flip(top, "sample", a))
        extra.setdefault((a, 1), []).append(flip(bottom, "sample", b))

    block = (wide(mine) + wide(flip(theirs, "sample", 1))).astype(bf16)
    halves = lax.optimization_barrier(cut(block))
    send_diagonal(*diagonal[-1], *halves)
    share_from = {groups - 2: flip(share, "cls", 1)}

    results = call(
        functools.partial(products_kernel, len(halves), depth, near, chip_masks),
        [((depth, classes), bf16)] * (2 * len(near)) + [((groups, rows, width), bf16)],
        [grad, turned] + head_list,
        extra=halves,
    )
    shares = results[-1]
    arrived = [part for parts in extra.values() for part in parts]
    theirs = lax.optimization_barrier((*results[1:-1:2], *arrived))
    arrived = iter(theirs[len(near) :])
    extra = {at: [next(arrived) for _ in parts] for at, parts in extra.items()}
    mixed = {
        2 * mask: wide(results[2 * i]) + wide(flip(theirs[i], "sample", 1)) for i, mask in enumerate(near)
    }
    for a, b in diagonal[:-1]:
        send_diagonal(a, b, *cut(mixed[a | b].astype(bf16)))

    returned = [flip(shares[1], "cls", 1)]
    for mask in range(2, groups, 2):
        received = share_from[mask] if mask in share_from else flip(shares[mask | 1], "cls", 1)
        returned.append(flip((wide(shares[mask]) + wide(received)).astype(bf16), "cls", mask))

    halves = list(cut(mixed[0]))
    sent = {}
    for late in (False, True):
        for mask in first + second:
            for part, value in enumerate(cut(mixed[mask])):
                if ((mask, part) in extra) == late:
                    for more in extra.get((mask, part), []):
                        value = value + wide(more)
                    sent[mask, part] = value.astype(bf16)
    for (mask, part), value in sent.items():
        halves[part] = halves[part] + wide(flip(value, "sample", mask))
    returned = lax.optimization_barrier((*returned, *sent.values()))[: len(returned)]
    grad_features = sum([wide(value) for value in returned], wide(shares[0])).astype(bf16)
    grad_head = jnp.concatenate(halves, axis=0).astype(bf16)
    return (targets, grad_features, grad_head)


def solution(mesh):
    return jax.shard_map(
        per_device,
        mesh=mesh,
        in_specs=(P("sample", "cls"), P("sample", "cls"), P("cls")),
        out_specs=(P("sample", "cls"), P("sample", "cls"), P("sample", "cls")),
        check_vma=False,
    )
```

```python
import functools

import jax
import jax.numpy as jnp
from jax import lax
from jax.experimental import pallas as pl
from jax.experimental.pallas import tpu as pltpu
from jax.sharding import PartitionSpec as P

ITERS = 3


softcap = 15.0
sharpen = 2.0
f32 = jnp.float32
bf16 = jnp.bfloat16
LANES = 128


def wide(value):
    return value.astype(f32)


def matmul(left, right, dims):
    return lax.dot_general(left, right, (dims, ((), ())), preferred_element_type=f32)


def flip(value, axis, mask):
    return lax.ppermute(value, axis, [(i, i ^ mask) for i in range(lax.axis_size(axis))])


def cut(value):
    half = value.shape[0] // 2
    return value[:half], value[half:]


def chip_axes(size):
    chips = size // 2
    bits = chips.bit_length() - 1
    low = 1 << ((bits + 1) // 2)
    first = [2 * m for m in range(1, low)]
    second = [2 * low * m for m in range(1, chips // low)]
    return first, second


def gather_head(head):
    size = lax.axis_size("sample")
    first, second = chip_axes(size)
    held = {mask: [flip(head, "sample", mask)] for mask in first + second}
    held[0] = [head]
    for a in first:
        for b in second:
            top, bottom = cut(held[a][0])[0], cut(held[b][0])[1]
            held[a | b] = [flip(top, "sample", b), flip(bottom, "sample", a)]
    return held


def gather_features(features):
    size = lax.axis_size("cls")
    held = {0: features}
    for mask in list(range(2, size, 2)) + [1]:
        held[mask] = flip(features, "cls", mask)
    for mask in range(2, size, 2):
        held[mask | 1] = flip(held[mask], "cls", 1)
    return [held[mask] for mask in range(size)]


def fast(value):
    return pltpu.with_memory_space_constraint(value, pltpu.VMEM)


def call(kernel, outputs, operands, scratch=(), extra=(), limit=16):
    spec = pl.BlockSpec(memory_space=pltpu.VMEM)
    return pl.pallas_call(
        kernel,
        out_shape=tuple(pltpu.VMEM(shape, dtype) for shape, dtype in outputs),
        in_specs=[spec] * len(operands) + [pl.BlockSpec(memory_space=pl.ANY)] * len(extra),
        out_specs=(spec,) * len(outputs),
        scratch_shapes=list(scratch),
        compiler_params=pltpu.CompilerParams(vmem_limit_bytes=limit << 20),
        cost_estimate=pl.CostEstimate(flops=1, bytes_accessed=1, transcendentals=0),
    )(*[fast(operand) for operand in operands], *extra)


def as_column(row):
    return jnp.transpose(jnp.broadcast_to(row, (LANES, row.shape[1])))


def row_kernel(count, student_ref, scale_ref, ceiling_ref, *refs):
    part_refs, (new_ref, total_ref, partial) = refs[:count], refs[count:]
    mass = part_refs[0][...]
    for ref in part_refs[1:]:
        mass = mass + ref[...]
    new_ref[...] = scale_ref[...] * jnp.minimum(1.0, ceiling_ref[...] / mass)
    rows, columns = student_ref.shape
    block = 64

    def body(i, carry):
        at = pl.ds(pl.multiple_of(i * block, block), block)
        total = jnp.zeros((block, LANES), f32)
        for j in range(0, columns, LANES):
            value = student_ref[at, j : j + LANES]
            total = total + value * value * new_ref[:, j : j + LANES]
        partial[at, :] = total
        return carry

    lax.fori_loop(0, rows // block, body, 0)
    total_ref[...] = jnp.sum(jnp.transpose(partial[...]), axis=0, keepdims=True)


def rows_at(depth, side, paired):
    if paired:
        return 0
    core = lax.axis_index("sample") % 2
    return pl.multiple_of((core if side == 0 else 1 - core) * depth, LANES)


def products(at, parts, refs, blocks_ref, depth, paired):
    chip, place = lax.axis_index("sample") // 2, lax.axis_index("cls")
    total = None
    for (mask, side), ref in zip(parts, refs):
        left = blocks_ref[chip ^ mask ^ place, :, pl.ds(rows_at(depth, side, paired), ref.shape[0])]
        part = jnp.dot(left, ref[:, at], preferred_element_type=f32)
        total = part if total is None else total + part
    return total


def partial_kernel(count, depth, paired, parts, *refs):
    feature_refs, head_refs = refs[:count], refs[count : count + len(parts)]
    blocks_ref, turned_ref, logits_ref = refs[count + len(parts) :]
    for i, ref in enumerate(feature_refs):
        blocks_ref[i] = ref[...]
    columns = logits_ref.shape[1]
    tile = min(256, columns)
    for i in range(0, columns, tile):
        at = slice(i, i + tile)
        logits_ref[:, at] = products(at, parts, head_refs, blocks_ref, depth, paired)
    for i, ref in enumerate(feature_refs):
        turned_ref[i] = jnp.transpose(ref[...])


def student_kernel(depth, paired, parts, logits_ref, blocks_ref, *refs):
    head_refs = refs[: len(parts)]
    student_ref, slope_ref, sums_ref, buffer, student_sum, plan_sum = refs[len(parts) :]
    rows, columns = logits_ref.shape
    tile = min(256, columns)
    block = min(128, rows)
    for i in range(0, columns, tile):
        at = slice(i, i + tile)
        slot = (i // tile) % 2
        buffer[slot] = logits_ref[:, at] + products(at, parts, head_refs, blocks_ref, depth, paired)
        for first in range(0, rows, block):
            row = slice(first, first + block)
            student_total = plan_total = None
            for j in range(0, tile, LANES):
                out = slice(i + j, i + j + LANES)
                tanh = jnp.tanh(buffer[slot, row, j : j + LANES] * (1.0 / softcap))
                student = jnp.exp(softcap * tanh)
                plan = student * student
                student_ref[row, out] = student
                slope_ref[row, out] = (1.0 - tanh * tanh).astype(bf16)
                student_total = student if student_total is None else student_total + student
                plan_total = plan if plan_total is None else plan_total + plan
            if i > 0:
                student_total, plan_total = student_total + student_sum[row, :], plan_total + plan_sum[row, :]
            student_sum[row, :] = student_total
            plan_sum[row, :] = plan_total
    sums_ref[0:1, :] = jnp.sum(jnp.transpose(student_sum[...]), axis=0, keepdims=True)
    sums_ref[1:2, :] = jnp.sum(jnp.transpose(plan_sum[...]), axis=0, keepdims=True)


def column_kernel(count, student_ref, scale_ref, *refs):
    part_refs, (total_ref, inverse) = refs[:count], refs[count:]
    mass = part_refs[0][...]
    for ref in part_refs[1:]:
        mass = mass + ref[...]
    inverse[...] = as_column(1.0 / mass)
    rows, columns = student_ref.shape
    block = 8

    def body(i, total):
        at = pl.ds(pl.multiple_of(i * block, block), block)
        factor = inverse[at, :]
        new = []
        for j in range(0, columns, LANES):
            value = student_ref[at, j : j + LANES]
            new.append(total[j // LANES] + value * value * factor)
        return tuple(new)

    start = tuple(jnp.zeros((block, LANES), f32) for _ in range(0, columns, LANES))
    total = lax.fori_loop(0, rows // block, body, start, unroll=4)
    for j, value in enumerate(total):
        at = slice(j * LANES, (j + 1) * LANES)
        total_ref[:, at] = jnp.sum(value, axis=0, keepdims=True) * scale_ref[:, at]


def head_products(turned_ref, core, depth, grad_ref, at, mine_ref, theirs_ref):
    for where, out_ref in ((core, mine_ref), (1 - core, theirs_ref)):
        left = turned_ref[pl.ds(pl.multiple_of(where * depth, depth), depth), :]
        out_ref[:, at] = jnp.dot(left, grad_ref[:, at], preferred_element_type=f32).astype(bf16)


def gradient_kernel(count, depth, paired, far, parts, student_ref, slope_ref, scale_ref, students_ref, turned_ref, *refs):
    part_refs, head_refs = refs[:count], refs[count : count + len(parts)]
    targets_ref, grad_ref, mine_ref, theirs_ref, share_ref, inverse, students = refs[count + len(parts) :]
    me, place = lax.axis_index("sample"), lax.axis_index("cls")
    chip, core = me // 2, me % 2
    groups = lax.axis_size("cls")
    mass = part_refs[0][...]
    for ref in part_refs[1:]:
        mass = mass + ref[...]
    inverse[...] = as_column(1.0 / mass)
    students[...] = as_column(1.0 / students_ref[...])
    columns = student_ref.shape[1]
    tile = min(256, columns)
    turned = turned_ref.at[place ^ chip ^ far]

    for i in range(0, columns, tile):
        for j in range(i, i + tile, LANES):
            at = slice(j, j + LANES)
            student = student_ref[:, at]
            target = (student * student * scale_ref[:, at] * inverse[...]).astype(bf16)
            targets_ref[:, at] = target
            grad_ref[:, at] = ((student * students[...] - wide(target)) * wide(slope_ref[:, at])).astype(bf16)
        head_products(turned, core, depth, grad_ref, slice(i, i + tile), mine_ref, theirs_ref)
    for (mask, side), ref in zip(parts, head_refs):

        @pl.when((chip ^ mask) == (place ^ (groups - 1)))
        def _():
            at = pl.ds(rows_at(depth, side, paired), ref.shape[0])
            share_ref[:, at] = matmul(grad_ref[...], ref[...], ((1,), (1,))).astype(bf16)


def products_kernel(count, depth, paired, near, parts, grad_ref, turned_ref, *refs):
    head_refs, refs = refs[: len(parts)], refs[len(parts) + count :]
    pairs, (shares_ref,) = refs[:-1], refs[-1:]
    me, place = lax.axis_index("sample"), lax.axis_index("cls")
    chip, core = me // 2, me % 2
    columns = grad_ref.shape[1]
    tile = min(256, columns)
    for index, mask in enumerate(near):
        mine_ref, theirs_ref = pairs[2 * index], pairs[2 * index + 1]
        turned = turned_ref.at[place ^ chip ^ mask]
        for i in range(0, columns, tile):
            head_products(turned, core, depth, grad_ref, slice(i, i + tile), mine_ref, theirs_ref)
    for (mask, side), ref in zip(parts, head_refs):
        at = pl.ds(rows_at(depth, side, paired), ref.shape[0])
        shares_ref[chip ^ mask ^ place, :, at] = matmul(grad_ref[...], ref[...], ((1,), (1,))).astype(bf16)


def per_device(features, head, class_cap):
    rows, width = features.shape
    depth, classes = head.shape
    samples = lax.axis_size("sample")
    groups = lax.axis_size("cls")
    ratio = rows * samples / (classes * groups)
    me = lax.axis_index("sample")
    place = lax.axis_index("cls")
    chip, core = me // 2, me % 2
    first, second = chip_axes(samples)

    pieces = gather_head(head)
    features_from = gather_features(features)
    paired = depth % LANES != 0

    def sides(mask, same):
        other = [flip(part, "sample", 1) for part in same]
        if paired:
            pairs = [(jnp.where(core == 0, s, o), jnp.where(core == 0, o, s)) for s, o in zip(same, other)]
            return [((mask // 2, 0), jnp.concatenate([p[0] for p in pairs] + [p[1] for p in pairs], axis=0))]
        both = [part[0] if len(part) == 1 else jnp.concatenate(part, axis=0) for part in (same, other)]
        return [((mask // 2, side), part) for side, part in enumerate(both)]

    early = [part for mask in [0] + first + second for part in sides(mask, pieces[mask])]
    blocks, turned, logits = call(
        functools.partial(partial_kernel, groups, depth, paired, [at for at, _ in early]),
        [((groups, rows, width), bf16), ((groups, width, rows), bf16), ((rows, classes), f32)],
        features_from + [part for _, part in early],
    )
    late = []
    for mask in [a | b for a in first for b in second]:
        late += sides(mask, list(lax.optimization_barrier((logits, *pieces[mask]))[1:]))
    tile = min(256, classes)
    student, slope, sums = call(
        functools.partial(student_kernel, depth, paired, [at for at, _ in late]),
        [((rows, classes), f32), ((rows, classes), bf16), ((2, rows), f32)],
        [logits, blocks] + [part for _, part in late],
        [pltpu.VMEM((2, rows, tile), f32), pltpu.VMEM((rows, LANES), f32), pltpu.VMEM((rows, LANES), f32)],
    )

    def row_parts(value):
        return [value] + [flip(value, "cls", mask) for mask in range(groups - 1, 0, -1)]

    def column_parts(value):
        value = value + flip(value, "sample", 1)
        return [value] + [flip(value, "sample", mask) for mask in range(samples - 2, 0, -2)]

    ceiling = (wide(class_cap) * ratio)[None]
    parts = row_parts(sums)
    students_mass = sum([part[0:1] for part in parts[1:]], parts[0][0:1])
    parts = [part[1:2] for part in parts]
    scale = jnp.ones((1, classes), f32)
    for _ in range(ITERS):
        (mass,) = call(
            functools.partial(column_kernel, len(parts)),
            [((1, classes), f32)],
            [student, scale] + parts,
            [pltpu.VMEM((rows, LANES), f32)],
        )
        sent = column_parts(mass)
        scale, mass = call(
            functools.partial(row_kernel, len(sent)),
            [((1, classes), f32), ((1, rows), f32)],
            [student, scale, ceiling] + sent,
            [pltpu.VMEM((rows, LANES), f32)],
        )
        parts = row_parts(mass)

    head_at = [at for at, _ in early + late]
    head_list = [part for _, part in early + late]
    near = [mask // 2 for mask in first + second] + [0]
    diagonal = [(a, b) for a in first for b in second]
    far = (diagonal[-1][0] | diagonal[-1][1]) // 2
    near = [(a | b) // 2 for a, b in diagonal[:-1]] + near
    targets, grad, mine, theirs, share = call(
        functools.partial(gradient_kernel, len(parts), depth, paired, far, head_at),
        [((rows, classes), bf16)] * 2 + [((depth, classes), bf16)] * 2 + [((rows, width), bf16)],
        [student, slope, scale, students_mass, turned] + parts + head_list,
        [pltpu.VMEM((rows, LANES), f32)] * 2,
    )
    extra = {}

    def send_diagonal(a, b, top, bottom):
        extra.setdefault((b, 0), []).append(flip(top, "sample", a))
        extra.setdefault((a, 1), []).append(flip(bottom, "sample", b))

    block = (wide(mine) + wide(flip(theirs, "sample", 1))).astype(bf16)
    halves = lax.optimization_barrier(cut(block))
    send_diagonal(*diagonal[-1], *halves)
    share_from = {groups - 2: flip(share, "cls", 1)}

    results = call(
        functools.partial(products_kernel, len(halves), depth, paired, near, head_at),
        [((depth, classes), bf16)] * (2 * len(near)) + [((groups, rows, width), bf16)],
        [grad, turned] + head_list,
        extra=halves,
    )
    shares = results[-1]
    arrived = [part for parts in extra.values() for part in parts] + list(share_from.values())
    theirs = lax.optimization_barrier((*results[1:-1:2], *arrived))
    arrived = iter(theirs[len(near) :])
    extra = {at: [next(arrived) for _ in parts] for at, parts in extra.items()}
    share_from = {mask: next(arrived) for mask in share_from}
    mixed = {
        2 * mask: wide(results[2 * i]) + wide(flip(theirs[i], "sample", 1)) for i, mask in enumerate(near)
    }
    for a, b in diagonal[:-1]:
        send_diagonal(a, b, *cut(mixed[a | b].astype(bf16)))

    returned = [flip(shares[1], "cls", 1)]
    for mask in range(2, groups, 2):
        received = share_from[mask] if mask in share_from else flip(shares[mask | 1], "cls", 1)
        returned.append(flip((wide(shares[mask]) + wide(received)).astype(bf16), "cls", mask))

    received = []
    for mask in first + second:
        halves = list(cut(mixed[mask]))
        for part in (0, 1):
            for more in extra.get((mask, part), []):
                halves[part] = halves[part] + wide(more)
        received.append(flip(jnp.concatenate(halves, axis=0).astype(bf16), "sample", mask))
    grad_head = sum([wide(part) for part in received], mixed[0]).astype(bf16)
    returned = lax.optimization_barrier((*returned, *received))[: len(returned)]
    grad_features = sum([wide(value) for value in returned], wide(shares[0])).astype(bf16)
    return (targets, grad_features, grad_head)


def solution(mesh):
    return jax.shard_map(
        per_device,
        mesh=mesh,
        in_specs=(P("sample", "cls"), P("sample", "cls"), P("cls")),
        out_specs=(P("sample", "cls"), P("sample", "cls"), P("sample", "cls")),
        check_vma=False,
    )
```

```python
import functools

import jax
import jax.numpy as jnp
from jax import lax
from jax.experimental import pallas as pl
from jax.experimental.pallas import tpu as pltpu
from jax.sharding import PartitionSpec as P

ITERS = 3


softcap = 15.0
sharpen = 2.0
f32 = jnp.float32
bf16 = jnp.bfloat16
LANES = 128


def wide(value):
    return value.astype(f32)


def matmul(left, right, dims):
    return lax.dot_general(left, right, (dims, ((), ())), preferred_element_type=f32)


def flip(value, axis, mask):
    return lax.ppermute(value, axis, [(i, i ^ mask) for i in range(lax.axis_size(axis))])


def cross(value, even, odd):
    size = lax.axis_size("sample")
    return lax.ppermute(value, "sample", [(i, i ^ (odd if i % 2 else even)) for i in range(size)])


def chip_axes(size):
    chips = size // 2
    bits = chips.bit_length() - 1
    low = 1 << ((bits + 1) // 2)
    first = [2 * m for m in range(1, low)]
    second = [2 * low * m for m in range(1, chips // low)]
    return first, second


def gather_head(head):
    size = lax.axis_size("sample")
    core = lax.axis_index("sample") % 2
    first, second = chip_axes(size)
    held = {mask: flip(head, "sample", mask) for mask in first + second}
    held[0] = head
    sibling = flip(head, "sample", 1)
    for a in first:
        for b in second:
            passed = lax.optimization_barrier((jnp.where(core == 0, held[a], held[b]), sibling))[0]
            held[a | b] = cross(passed, b, a)
    return held, sibling


def gather_features(features):
    size = lax.axis_size("cls")
    held = {0: features}
    for mask in list(range(2, size, 2)) + [1]:
        held[mask] = flip(features, "cls", mask)
    for mask in range(2, size, 2):
        held[mask | 1] = flip(lax.optimization_barrier((held[mask], held[1]))[0], "cls", 1)
    return [held[mask] for mask in range(size)]


def fast(value):
    return pltpu.with_memory_space_constraint(value, pltpu.VMEM)


def call(kernel, outputs, operands, scratch=(), extra=(), limit=16):
    spec = pl.BlockSpec(memory_space=pltpu.VMEM)
    return pl.pallas_call(
        kernel,
        out_shape=tuple(pltpu.VMEM(shape, dtype) for shape, dtype in outputs),
        in_specs=[spec] * len(operands) + [pl.BlockSpec(memory_space=pl.ANY)] * len(extra),
        out_specs=(spec,) * len(outputs),
        scratch_shapes=list(scratch),
        compiler_params=pltpu.CompilerParams(vmem_limit_bytes=limit << 20),
        cost_estimate=pl.CostEstimate(flops=1, bytes_accessed=1, transcendentals=0),
    )(*[fast(operand) for operand in operands], *extra)


def as_column(row):
    return jnp.transpose(jnp.broadcast_to(row, (LANES, row.shape[1])))


def row_kernel(student_ref, scale_ref, ceiling_ref, mass_ref, new_ref, total_ref, partial):
    new_ref[...] = scale_ref[...] * jnp.minimum(1.0, ceiling_ref[...] / mass_ref[...])
    rows, columns = student_ref.shape
    block = 64

    def body(i, carry):
        at = pl.ds(pl.multiple_of(i * block, block), block)
        total = jnp.zeros((block, LANES), f32)
        for j in range(0, columns, LANES):
            value = student_ref[at, j : j + LANES]
            total = total + value * value * new_ref[:, j : j + LANES]
        partial[at, :] = total
        return carry

    lax.fori_loop(0, rows // block, body, 0)
    total_ref[...] = jnp.sum(jnp.transpose(partial[...]), axis=0, keepdims=True)


def rows_at(depth, side, paired):
    if paired:
        return 0
    core = lax.axis_index("sample") % 2
    return pl.multiple_of((core if side == 0 else 1 - core) * depth, LANES)


def products(at, parts, refs, blocks_ref, depth, paired):
    chip, place = lax.axis_index("sample") // 2, lax.axis_index("cls")
    total = None
    for (mask, side), ref in zip(parts, refs):
        left = blocks_ref[chip ^ mask ^ place, :, pl.ds(rows_at(depth, side, paired), ref.shape[0])]
        part = jnp.dot(left, ref[:, at], preferred_element_type=f32)
        total = part if total is None else total + part
    return total


def partial_kernel(count, depth, paired, parts, *refs):
    feature_refs, head_refs = refs[:count], refs[count : count + len(parts)]
    blocks_ref, turned_ref, logits_ref = refs[count + len(parts) :]
    for i, ref in enumerate(feature_refs):
        blocks_ref[i] = ref[...]
    columns = logits_ref.shape[1]
    tile = min(256, columns)
    for i in range(0, columns, tile):
        at = slice(i, i + tile)
        logits_ref[:, at] = products(at, parts, head_refs, blocks_ref, depth, paired)
    for i, ref in enumerate(feature_refs):
        turned_ref[i] = jnp.transpose(ref[...])


def student_kernel(depth, paired, parts, logits_ref, blocks_ref, *refs):
    head_refs = refs[: len(parts)]
    student_ref, slope_ref, sums_ref, buffer, student_sum, plan_sum = refs[len(parts) :]
    rows, columns = logits_ref.shape
    tile = min(256, columns)
    block = min(128, rows)
    for i in range(0, columns, tile):
        at = slice(i, i + tile)
        slot = (i // tile) % 2
        buffer[slot] = logits_ref[:, at] + products(at, parts, head_refs, blocks_ref, depth, paired)
        for first in range(0, rows, block):
            row = slice(first, first + block)
            student_total = plan_total = None
            for j in range(0, tile, LANES):
                out = slice(i + j, i + j + LANES)
                tanh = jnp.tanh(buffer[slot, row, j : j + LANES] * (1.0 / softcap))
                student = jnp.exp(softcap * tanh)
                plan = student * student
                student_ref[row, out] = student
                slope_ref[row, out] = (1.0 - tanh * tanh).astype(bf16)
                student_total = student if student_total is None else student_total + student
                plan_total = plan if plan_total is None else plan_total + plan
            if i > 0:
                student_total, plan_total = student_total + student_sum[row, :], plan_total + plan_sum[row, :]
            student_sum[row, :] = student_total
            plan_sum[row, :] = plan_total
    sums_ref[0:1, :] = jnp.sum(jnp.transpose(student_sum[...]), axis=0, keepdims=True)
    sums_ref[1:2, :] = jnp.sum(jnp.transpose(plan_sum[...]), axis=0, keepdims=True)


def column_kernel(student_ref, scale_ref, mass_ref, total_ref, inverse):
    inverse[...] = as_column(1.0 / mass_ref[...])
    rows, columns = student_ref.shape
    block = 8

    def body(i, total):
        at = pl.ds(pl.multiple_of(i * block, block), block)
        factor = inverse[at, :]
        new = []
        for j in range(0, columns, LANES):
            value = student_ref[at, j : j + LANES]
            new.append(total[j // LANES] + value * value * factor)
        return tuple(new)

    start = tuple(jnp.zeros((block, LANES), f32) for _ in range(0, columns, LANES))
    total = lax.fori_loop(0, rows // block, body, start, unroll=4)
    for j, value in enumerate(total):
        at = slice(j * LANES, (j + 1) * LANES)
        total_ref[:, at] = jnp.sum(value, axis=0, keepdims=True) * scale_ref[:, at]


def head_products(turned_ref, core, depth, grad_ref, at, mine_ref, theirs_ref):
    for where, out_ref in ((core, mine_ref), (1 - core, theirs_ref)):
        left = turned_ref[pl.ds(pl.multiple_of(where * depth, depth), depth), :]
        out_ref[:, at] = jnp.dot(left, grad_ref[:, at], preferred_element_type=f32).astype(bf16)


def gradient_kernel(
    depth, paired, far, parts, student_ref, slope_ref, scale_ref, students_ref, mass_ref, turned_ref, *refs
):
    head_refs = refs[: len(parts)]
    targets_ref, grad_ref, mine_ref, theirs_ref, share_ref, inverse, students = refs[len(parts) :]
    me, place = lax.axis_index("sample"), lax.axis_index("cls")
    chip, core = me // 2, me % 2
    groups = lax.axis_size("cls")
    inverse[...] = as_column(1.0 / mass_ref[...])
    students[...] = as_column(1.0 / students_ref[...])
    columns = student_ref.shape[1]
    tile = min(256, columns)
    turned = turned_ref.at[place ^ chip ^ far]

    for i in range(0, columns, tile):
        for j in range(i, i + tile, LANES):
            at = slice(j, j + LANES)
            student = student_ref[:, at]
            target = (student * student * scale_ref[:, at] * inverse[...]).astype(bf16)
            targets_ref[:, at] = target
            grad_ref[:, at] = ((student * students[...] - wide(target)) * wide(slope_ref[:, at])).astype(bf16)
        head_products(turned, core, depth, grad_ref, slice(i, i + tile), mine_ref, theirs_ref)
    for (mask, side), ref in zip(parts, head_refs):

        @pl.when((chip ^ mask) == (place ^ (groups - 1)))
        def _():
            at = pl.ds(rows_at(depth, side, paired), ref.shape[0])
            share_ref[:, at] = matmul(grad_ref[...], ref[...], ((1,), (1,))).astype(bf16)


def products_kernel(count, depth, paired, near, parts, grad_ref, turned_ref, *refs):
    head_refs, refs = refs[: len(parts)], refs[len(parts) + count :]
    pairs, (shares_ref,) = refs[:-1], refs[-1:]
    me, place = lax.axis_index("sample"), lax.axis_index("cls")
    chip, core = me // 2, me % 2
    columns = grad_ref.shape[1]
    tile = min(256, columns)
    for index, mask in enumerate(near):
        mine_ref, theirs_ref = pairs[2 * index], pairs[2 * index + 1]
        turned = turned_ref.at[place ^ chip ^ mask]
        for i in range(0, columns, tile):
            head_products(turned, core, depth, grad_ref, slice(i, i + tile), mine_ref, theirs_ref)
    for (mask, side), ref in zip(parts, head_refs):
        at = pl.ds(rows_at(depth, side, paired), ref.shape[0])
        shares_ref[chip ^ mask ^ place, :, at] = matmul(grad_ref[...], ref[...], ((1,), (1,))).astype(bf16)


def per_device(features, head, class_cap):
    rows, width = features.shape
    depth, classes = head.shape
    samples = lax.axis_size("sample")
    groups = lax.axis_size("cls")
    ratio = rows * samples / (classes * groups)
    me = lax.axis_index("sample")
    place = lax.axis_index("cls")
    chip, core = me // 2, me % 2
    first, second = chip_axes(samples)

    pieces, sibling = gather_head(head)
    features_from = gather_features(features)
    paired = depth % LANES != 0

    def sides(mask, same):
        other = flip(same, "sample", 1) if mask else sibling
        if paired:
            pair = jnp.where(core == 0, same, other), jnp.where(core == 0, other, same)
            return [((mask // 2, 0), jnp.concatenate(pair, axis=0))]
        return [((mask // 2, 0), same), ((mask // 2, 1), other)]

    early = [part for mask in [0] + first + second for part in sides(mask, pieces[mask])]
    blocks, turned, logits = call(
        functools.partial(partial_kernel, groups, depth, paired, [at for at, _ in early]),
        [((groups, rows, width), bf16), ((groups, width, rows), bf16), ((rows, classes), f32)],
        features_from + [part for _, part in early],
    )
    late = []
    for mask in [a | b for a in first for b in second]:
        late += sides(mask, lax.optimization_barrier((logits, pieces[mask]))[1])
    tile = min(256, classes)
    student, slope, sums = call(
        functools.partial(student_kernel, depth, paired, [at for at, _ in late]),
        [((rows, classes), f32), ((rows, classes), bf16), ((2, rows), f32)],
        [logits, blocks] + [part for _, part in late],
        [pltpu.VMEM((2, rows, tile), f32), pltpu.VMEM((rows, LANES), f32), pltpu.VMEM((rows, LANES), f32)],
    )

    def total(value, axis, masks):
        for part in [flip(value, axis, mask) for mask in reversed(masks)]:
            value = lax.optimization_barrier(value + part)
        return value

    def row_total(value):
        return total(value, "cls", range(1, groups))

    def column_total(value):
        return total(value + flip(value, "sample", 1), "sample", range(2, samples, 2))

    ceiling = (wide(class_cap) * ratio)[None]
    sums = row_total(sums)
    students_mass, mass = sums[0:1], sums[1:2]
    scale = jnp.ones((1, classes), f32)
    for _ in range(ITERS):
        (mass,) = call(
            column_kernel,
            [((1, classes), f32)],
            [student, scale, mass],
            [pltpu.VMEM((rows, LANES), f32)],
        )
        scale, mass = call(
            row_kernel,
            [((1, classes), f32), ((1, rows), f32)],
            [student, scale, ceiling, column_total(mass)],
            [pltpu.VMEM((rows, LANES), f32)],
        )
        mass = row_total(mass)

    head_at = [at for at, _ in early + late]
    head_list = [part for _, part in early + late]
    near = [mask // 2 for mask in first + second] + [0]
    diagonal = [(a, b) for a in first for b in second]
    far = (diagonal[-1][0] | diagonal[-1][1]) // 2
    near = [(a | b) // 2 for a, b in diagonal[:-1]] + near
    targets, grad, mine, theirs, share = call(
        functools.partial(gradient_kernel, depth, paired, far, head_at),
        [((rows, classes), bf16)] * 2 + [((depth, classes), bf16)] * 2 + [((rows, width), bf16)],
        [student, slope, scale, students_mass, mass, turned] + head_list,
        [pltpu.VMEM((rows, LANES), f32)] * 2,
    )
    block = lax.optimization_barrier((wide(mine) + wide(flip(theirs, "sample", 1))).astype(bf16))
    passed = {diagonal[-1]: cross(block, *diagonal[-1])}
    share_from = {groups - 2: flip(share, "cls", 1)}

    results = call(
        functools.partial(products_kernel, 1, depth, paired, near, head_at),
        [((depth, classes), bf16)] * (2 * len(near)) + [((groups, rows, width), bf16)],
        [grad, turned] + head_list,
        extra=[block],
    )
    shares = results[-1]
    arrived = list(passed.values()) + list(share_from.values())
    theirs = lax.optimization_barrier((*results[1:-1:2], *arrived))
    arrived = iter(theirs[len(near) :])
    passed = {at: next(arrived) for at in passed}
    share_from = {mask: next(arrived) for mask in share_from}

    onward = {1: shares[1]}
    for mask in range(2, groups, 2):
        received = share_from[mask] if mask in share_from else flip(shares[mask | 1], "cls", 1)
        onward[mask] = (wide(shares[mask]) + wide(received)).astype(bf16)
    ready = lax.optimization_barrier((*onward.values(), *theirs[: len(near)]))
    theirs = ready[len(onward) :]
    returned = [flip(value, "cls", mask) for mask, value in zip(onward, ready)]
    grad_features = sum([wide(value) for value in returned], wide(shares[0])).astype(bf16)

    mixed = {
        2 * mask: wide(results[2 * i]) + wide(flip(theirs[i], "sample", 1)) for i, mask in enumerate(near)
    }
    for a, b in diagonal[:-1]:
        passed[a, b] = cross(mixed[a | b].astype(bf16), a, b)
    received = []
    for mask in first + second:
        block = mixed[mask]
        for (a, b), more in passed.items():
            if mask == (b if mask in second else a):
                block = block + jnp.where((core == 0) == (mask in second), wide(more), 0.0)
        received.append(flip(block.astype(bf16), "sample", mask))
    received = lax.optimization_barrier((*received, grad_features))
    grad_features = received[-1]
    grad_head = sum([wide(part) for part in received[:-1]], mixed[0]).astype(bf16)
    return (targets, grad_features, grad_head)


def solution(mesh):
    return jax.shard_map(
        per_device,
        mesh=mesh,
        in_specs=(P("sample", "cls"), P("sample", "cls"), P("cls")),
        out_specs=(P("sample", "cls"), P("sample", "cls"), P("sample", "cls")),
        check_vma=False,
    )
```

```python
import functools

import jax
import jax.numpy as jnp
from jax import lax
from jax.experimental import pallas as pl
from jax.experimental.pallas import tpu as pltpu
from jax.sharding import PartitionSpec as P

ITERS = 3


softcap = 15.0
sharpen = 2.0
f32 = jnp.float32
bf16 = jnp.bfloat16
LANES = 128


def wide(value):
    return value.astype(f32)


def matmul(left, right, dims):
    return lax.dot_general(left, right, (dims, ((), ())), preferred_element_type=f32)


def flip(value, axis, mask):
    return lax.ppermute(value, axis, [(i, i ^ mask) for i in range(lax.axis_size(axis))])


def cross(value, even, odd):
    size = lax.axis_size("sample")
    return lax.ppermute(value, "sample", [(i, i ^ (odd if i % 2 else even)) for i in range(size)])


def chip_axes(size):
    chips = size // 2
    bits = chips.bit_length() - 1
    low = 1 << ((bits + 1) // 2)
    first = [2 * m for m in range(1, low)]
    second = [2 * low * m for m in range(1, chips // low)]
    return first, second


def gather(features, head):
    samples, groups = lax.axis_size("sample"), lax.axis_size("cls")
    core = lax.axis_index("sample") % 2
    first, second = chip_axes(samples)
    blocks = {mask: flip(features, "cls", mask) for mask in range(2, groups, 2)}
    held = {mask: flip(head, "sample", mask) for mask in first + second}
    blocks[1] = flip(features, "cls", 1)
    sibling = flip(head, "sample", 1)
    for mask in range(2, groups, 2):
        blocks[mask | 1] = flip(blocks[mask], "cls", 1)
    ready = lax.optimization_barrier((*held.values(), *[blocks[mask] for mask in range(2, groups, 2)]))
    held = dict(zip(held, ready))
    for a in first:
        for b in second:
            passed = jnp.where(core == 0, held[a], held[b])
            passed = lax.optimization_barrier((passed, sibling, blocks[1]))[0]
            held[a | b] = cross(passed, b, a)
    blocks[0], held[0] = features, head
    return [blocks[mask] for mask in range(groups)], held, sibling


def fast(value):
    return pltpu.with_memory_space_constraint(value, pltpu.VMEM)


def call(kernel, outputs, operands, scratch=(), extra=(), aliases=None, limit=6):
    spec = pl.BlockSpec(memory_space=pltpu.VMEM)
    return pl.pallas_call(
        kernel,
        out_shape=tuple(pltpu.VMEM(shape, dtype) for shape, dtype in outputs),
        in_specs=[spec] * len(operands) + [pl.BlockSpec(memory_space=pl.ANY)] * len(extra),
        out_specs=(spec,) * len(outputs),
        scratch_shapes=list(scratch),
        input_output_aliases=aliases or {},
        compiler_params=pltpu.CompilerParams(vmem_limit_bytes=limit << 20),
        cost_estimate=pl.CostEstimate(flops=1, bytes_accessed=1, transcendentals=0),
    )(*[fast(operand) for operand in operands], *extra)


def as_column(row):
    return jnp.transpose(jnp.broadcast_to(row, (LANES, row.shape[1])))


def row_kernel(student_ref, scale_ref, ceiling_ref, mass_ref, new_ref, total_ref, partial):
    new_ref[...] = scale_ref[...] * jnp.minimum(1.0, ceiling_ref[...] / mass_ref[...])
    rows, columns = student_ref.shape
    block = 64

    def body(i, carry):
        at = pl.ds(pl.multiple_of(i * block, block), block)
        total = jnp.zeros((block, LANES), f32)
        for j in range(0, columns, LANES):
            value = student_ref[at, j : j + LANES]
            total = total + value * value * new_ref[:, j : j + LANES]
        partial[at, :] = total
        return carry

    lax.fori_loop(0, rows // block, body, 0)
    total_ref[...] = jnp.sum(jnp.transpose(partial[...]), axis=0, keepdims=True)


def rows_at(depth, side, paired):
    if paired:
        return 0
    core = lax.axis_index("sample") % 2
    return pl.multiple_of((core if side == 0 else 1 - core) * depth, LANES)


def products(at, parts, refs, blocks_ref, depth, paired):
    chip, place = lax.axis_index("sample") // 2, lax.axis_index("cls")
    total = None
    for (mask, side), ref in zip(parts, refs):
        left = blocks_ref[chip ^ mask ^ place, :, pl.ds(rows_at(depth, side, paired), ref.shape[0])]
        part = jnp.dot(left, ref[:, at], preferred_element_type=f32)
        total = part if total is None else total + part
    return total


def partial_kernel(count, depth, paired, parts, *refs):
    feature_refs, head_refs = refs[:count], refs[count : count + len(parts)]
    blocks_ref, logits_ref = refs[count + len(parts) :]
    for i, ref in enumerate(feature_refs):
        blocks_ref[i] = ref[...]
    columns = logits_ref.shape[1]
    tile = min(256, columns)
    for i in range(0, columns, tile):
        at = slice(i, i + tile)
        logits_ref[:, at] = products(at, parts, head_refs, blocks_ref, depth, paired)


def turn_kernel(blocks_ref, turned_ref):
    for i in range(blocks_ref.shape[0]):
        turned_ref[i] = jnp.transpose(blocks_ref[i])


def student_kernel(depth, paired, parts, logits_ref, blocks_ref, *refs):
    head_refs = refs[: len(parts)]
    student_ref, slope_ref, sums_ref, buffer, student_sum, plan_sum = refs[len(parts) :]
    rows, columns = logits_ref.shape
    tile = min(256, columns)
    block = min(128, rows)
    for i in range(0, columns, tile):
        at = slice(i, i + tile)
        slot = (i // tile) % 2
        buffer[slot] = logits_ref[:, at] + products(at, parts, head_refs, blocks_ref, depth, paired)
        for first in range(0, rows, block):
            row = slice(first, first + block)
            student_total = plan_total = None
            for j in range(0, tile, LANES):
                out = slice(i + j, i + j + LANES)
                tanh = jnp.tanh(buffer[slot, row, j : j + LANES] * (1.0 / softcap))
                student = jnp.exp(softcap * tanh)
                plan = student * student
                student_ref[row, out] = student
                slope_ref[row, out] = (1.0 - tanh * tanh).astype(bf16)
                student_total = student if student_total is None else student_total + student
                plan_total = plan if plan_total is None else plan_total + plan
            if i > 0:
                student_total, plan_total = student_total + student_sum[row, :], plan_total + plan_sum[row, :]
            student_sum[row, :] = student_total
            plan_sum[row, :] = plan_total
    sums_ref[0:1, :] = jnp.sum(jnp.transpose(student_sum[...]), axis=0, keepdims=True)
    sums_ref[1:2, :] = jnp.sum(jnp.transpose(plan_sum[...]), axis=0, keepdims=True)


def column_kernel(student_ref, scale_ref, mass_ref, *refs):
    total_ref, inverse = refs[-2:]
    inverse[...] = as_column(1.0 / mass_ref[...])
    rows, columns = student_ref.shape
    block = 8

    def body(i, total):
        at = pl.ds(pl.multiple_of(i * block, block), block)
        factor = inverse[at, :]
        new = []
        for j in range(0, columns, LANES):
            value = student_ref[at, j : j + LANES]
            new.append(total[j // LANES] + value * value * factor)
        return tuple(new)

    start = tuple(jnp.zeros((block, LANES), f32) for _ in range(0, columns, LANES))
    total = lax.fori_loop(0, rows // block, body, start, unroll=4)
    for j, value in enumerate(total):
        at = slice(j * LANES, (j + 1) * LANES)
        total_ref[:, at] = jnp.sum(value, axis=0, keepdims=True) * scale_ref[:, at]


def head_products(turned_ref, core, depth, grad_ref, at, mine_ref, theirs_ref):
    for where, out_ref in ((core, mine_ref), (1 - core, theirs_ref)):
        left = turned_ref[pl.ds(pl.multiple_of(where * depth, depth), depth), :]
        out_ref[:, at] = jnp.dot(left, grad_ref[:, at], preferred_element_type=f32).astype(bf16)


def gradient_kernel(
    depth, paired, far, parts, student_ref, slope_ref, scale_ref, students_ref, mass_ref, turned_ref, *refs
):
    head_refs = refs[: len(parts)]
    targets_ref, grad_ref, mine_ref, theirs_ref, share_ref, inverse, students = refs[len(parts) :]
    me, place = lax.axis_index("sample"), lax.axis_index("cls")
    chip, core = me // 2, me % 2
    groups = lax.axis_size("cls")
    inverse[...] = as_column(1.0 / mass_ref[...])
    students[...] = as_column(1.0 / students_ref[...])
    columns = student_ref.shape[1]
    tile = min(256, columns)
    turned = turned_ref.at[place ^ chip ^ far]

    for i in range(0, columns, tile):
        for j in range(i, i + tile, LANES):
            at = slice(j, j + LANES)
            student = student_ref[:, at]
            target = (student * student * scale_ref[:, at] * inverse[...]).astype(bf16)
            targets_ref[:, at] = target
            grad_ref[:, at] = ((student * students[...] - wide(target)) * wide(slope_ref[:, at])).astype(bf16)
        head_products(turned, core, depth, grad_ref, slice(i, i + tile), mine_ref, theirs_ref)
    for (mask, side), ref in zip(parts, head_refs):

        @pl.when((chip ^ mask) == (place ^ (groups - 1)))
        def _():
            at = pl.ds(rows_at(depth, side, paired), ref.shape[0])
            share_ref[:, at] = matmul(grad_ref[...], ref[...], ((1,), (1,))).astype(bf16)


def near_kernel(depth, near, grad_ref, turned_ref, *refs):
    me, place = lax.axis_index("sample"), lax.axis_index("cls")
    chip, core = me // 2, me % 2
    columns = grad_ref.shape[1]
    tile = min(256, columns)
    for index, mask in enumerate(near):
        turned = turned_ref.at[place ^ chip ^ mask]
        for i in range(0, columns, tile):
            head_products(turned, core, depth, grad_ref, slice(i, i + tile), refs[2 * index], refs[2 * index + 1])


def shares_kernel(depth, paired, parts, grad_ref, turned_ref, *refs):
    head_refs, pair, shares_ref = refs[: len(parts)], refs[-3:-1], refs[-1]
    chip, place = lax.axis_index("sample") // 2, lax.axis_index("cls")
    for (mask, side), ref in zip(parts, head_refs):
        at = pl.ds(rows_at(depth, side, paired), ref.shape[0])
        shares_ref[chip ^ mask ^ place, :, at] = matmul(grad_ref[...], ref[...], ((1,), (1,))).astype(bf16)
    near_kernel(depth, [0], grad_ref, turned_ref, *pair)


def per_device(features, head, class_cap):
    rows, width = features.shape
    depth, classes = head.shape
    samples = lax.axis_size("sample")
    groups = lax.axis_size("cls")
    ratio = rows * samples / (classes * groups)
    me = lax.axis_index("sample")
    place = lax.axis_index("cls")
    chip, core = me // 2, me % 2
    first, second = chip_axes(samples)

    features_from, pieces, sibling = gather(features, head)
    paired = depth % LANES != 0

    def sides(mask, same):
        other = flip(same, "sample", 1) if mask else sibling
        if paired:
            pair = jnp.where(core == 0, same, other), jnp.where(core == 0, other, same)
            return [((mask // 2, 0), jnp.concatenate(pair, axis=0))]
        return [((mask // 2, 0), same), ((mask // 2, 1), other)]

    early = [part for mask in [0] + first + second for part in sides(mask, pieces[mask])]
    blocks, logits = call(
        functools.partial(partial_kernel, groups, depth, paired, [at for at, _ in early]),
        [((groups, rows, width), bf16), ((rows, classes), f32)],
        features_from + [part for _, part in early],
    )
    late = []
    for mask in [a | b for a in first for b in second]:
        late += sides(mask, lax.optimization_barrier((logits, pieces[mask]))[1])
    tile = min(256, classes)
    student, slope, sums = call(
        functools.partial(student_kernel, depth, paired, [at for at, _ in late]),
        [((rows, classes), f32), ((rows, classes), bf16), ((2, rows), f32)],
        [logits, blocks] + [part for _, part in late],
        [pltpu.VMEM((2, rows, tile), f32), pltpu.VMEM((rows, LANES), f32), pltpu.VMEM((rows, LANES), f32)],
        aliases={0: 0},
    )
    (turned,) = call(turn_kernel, [((groups, width, rows), bf16)], [blocks])

    def total(value, axis, masks):
        for part in [flip(value, axis, mask) for mask in reversed(masks)]:
            value = lax.optimization_barrier(value + part)
        return value

    def row_total(value):
        return total(value, "cls", range(1, groups))

    def column_total(value):
        return total(value + flip(value, "sample", 1), "sample", range(2, samples, 2))

    ceiling = (wide(class_cap) * ratio)[None]
    sums = row_total(sums)
    students_mass, mass = sums[0:1], sums[1:2]
    scale = jnp.ones((1, classes), f32)
    for iteration in range(ITERS):
        (mass,) = call(
            column_kernel,
            [((1, classes), f32)],
            [student, scale, mass],
            [pltpu.VMEM((rows, LANES), f32)],
            [turned] if iteration == 0 else [],
        )
        scale, mass = call(
            row_kernel,
            [((1, classes), f32), ((1, rows), f32)],
            [student, scale, ceiling, column_total(mass)],
            [pltpu.VMEM((rows, LANES), f32)],
        )
        mass = row_total(mass)

    head_at = [at for at, _ in early + late]
    head_list = [part for _, part in early + late]
    near = first + second
    diagonal = [(a, b) for a in first for b in second]
    far = (diagonal[-1][0] | diagonal[-1][1]) // 2
    near = [a | b for a, b in diagonal[:-1]] + near
    targets, grad, mine, theirs, share = call(
        functools.partial(gradient_kernel, depth, paired, far, head_at),
        [((rows, classes), bf16)] * 2 + [((depth, classes), bf16)] * 2 + [((rows, width), bf16)],
        [student, slope, scale, students_mass, mass, turned] + head_list,
        [pltpu.VMEM((rows, LANES), f32)] * 2,
    )
    theirs = flip(theirs, "sample", 1)
    pairs = call(
        functools.partial(near_kernel, depth, [mask // 2 for mask in near]),
        [((depth, classes), bf16)] * (2 * len(near)),
        [grad, turned],
    )
    theirs, *pairs = lax.optimization_barrier((theirs, *pairs))
    block = lax.optimization_barrier((wide(mine) + wide(theirs)).astype(bf16))
    passed = {diagonal[-1]: cross(block, *diagonal[-1])}
    share_from = {groups - 2: flip(share, "cls", 1)}
    others = {mask: flip(pairs[2 * i + 1], "sample", 1) for i, mask in enumerate(near)}
    mine, theirs, shares = call(
        functools.partial(shares_kernel, depth, paired, head_at),
        [((depth, classes), bf16)] * 2 + [((groups, rows, width), bf16)],
        [grad, turned] + head_list,
        extra=[block],
    )

    onward = {1: shares[1]}
    for mask in range(2, groups, 2):
        received = share_from[mask] if mask in share_from else flip(shares[mask | 1], "cls", 1)
        onward[mask] = (wide(shares[mask]) + wide(received)).astype(bf16)
    ready = lax.optimization_barrier((*onward.values(), *others.values(), *passed.values(), theirs))
    onward = dict(zip(onward, ready))
    others = dict(zip(others, ready[len(onward) :]))
    passed = dict(zip(passed, ready[len(onward) + len(others) :]))
    own = wide(mine) + wide(flip(ready[-1], "sample", 1))
    returned = [flip(value, "cls", mask) for mask, value in onward.items()]
    grad_features = sum([wide(value) for value in returned], wide(shares[0])).astype(bf16)

    mixed = {mask: wide(pairs[2 * i]) + wide(others[mask]) for i, mask in enumerate(near)}
    for a, b in diagonal[:-1]:
        passed[a, b] = cross(mixed[a | b].astype(bf16), a, b)
    received = []
    for mask in first + second:
        total_of = mixed[mask]
        for (a, b), more in passed.items():
            if mask == (b if mask in second else a):
                total_of = total_of + jnp.where((core == 0) == (mask in second), wide(more), 0.0)
        received.append(flip(total_of.astype(bf16), "sample", mask))
    received = lax.optimization_barrier((*received, grad_features))
    grad_features = received[-1]
    grad_head = sum([wide(part) for part in received[:-1]], own).astype(bf16)
    return (targets, grad_features, grad_head)


def solution(mesh):
    return jax.shard_map(
        per_device,
        mesh=mesh,
        in_specs=(P("sample", "cls"), P("sample", "cls"), P("cls")),
        out_specs=(P("sample", "cls"), P("sample", "cls"), P("sample", "cls")),
        check_vma=False,
    )
```

```python
import functools

import jax
import jax.numpy as jnp
from jax import lax
from jax.experimental import pallas as pl
from jax.experimental.pallas import tpu as pltpu
from jax.sharding import PartitionSpec as P

ITERS = 3


softcap = 15.0
sharpen = 2.0
f32 = jnp.float32
bf16 = jnp.bfloat16
LANES = 128


def wide(value):
    return value.astype(f32)


def matmul(left, right, dims):
    return lax.dot_general(left, right, (dims, ((), ())), preferred_element_type=f32)


def flip(value, axis, mask):
    return lax.ppermute(value, axis, [(i, i ^ mask) for i in range(lax.axis_size(axis))])


def cross(value, even, odd):
    size = lax.axis_size("sample")
    return lax.ppermute(value, "sample", [(i, i ^ (odd if i % 2 else even)) for i in range(size)])


def chip_axes(size):
    chips = size // 2
    bits = chips.bit_length() - 1
    low = 1 << ((bits + 1) // 2)
    first = [2 * m for m in range(1, low)]
    second = [2 * low * m for m in range(1, chips // low)]
    return first, second


def gather(features, head):
    samples, groups = lax.axis_size("sample"), lax.axis_size("cls")
    core = lax.axis_index("sample") % 2
    first, second = chip_axes(samples)
    blocks = {mask: flip(features, "cls", mask) for mask in range(2, groups, 2)}
    held = {mask: flip(head, "sample", mask) for mask in first + second}
    blocks[1] = flip(features, "cls", 1)
    sibling = flip(head, "sample", 1)
    for mask in range(2, groups, 2):
        blocks[mask | 1] = flip(blocks[mask], "cls", 1)
    ready = lax.optimization_barrier((*held.values(), *[blocks[mask] for mask in range(2, groups, 2)]))
    held = dict(zip(held, ready))
    for a in first:
        for b in second:
            passed = jnp.where(core == 0, held[a], held[b])
            passed = lax.optimization_barrier((passed, sibling, blocks[1]))[0]
            held[a | b] = cross(passed, b, a)
    blocks[0], held[0] = features, head
    return [blocks[mask] for mask in range(groups)], held, sibling


def fast(value):
    return pltpu.with_memory_space_constraint(value, pltpu.VMEM)


def call(kernel, outputs, operands, scratch=(), extra=(), aliases=None, slow=(), limit=16):
    spec = pl.BlockSpec(memory_space=pltpu.VMEM)
    return pl.pallas_call(
        kernel,
        out_shape=tuple(
            jax.ShapeDtypeStruct(shape, dtype) if i in slow else pltpu.VMEM(shape, dtype)
            for i, (shape, dtype) in enumerate(outputs)
        ),
        in_specs=[spec] * len(operands) + [pl.BlockSpec(memory_space=pl.ANY)] * len(extra),
        out_specs=tuple(pl.BlockSpec(memory_space=pl.ANY) if i in slow else spec for i in range(len(outputs))),
        scratch_shapes=list(scratch),
        input_output_aliases=aliases or {},
        compiler_params=pltpu.CompilerParams(vmem_limit_bytes=limit << 20),
        cost_estimate=pl.CostEstimate(flops=1, bytes_accessed=1, transcendentals=0),
    )(*[fast(operand) for operand in operands], *extra)


def as_column(row):
    return jnp.transpose(jnp.broadcast_to(row, (LANES, row.shape[1])))


def row_kernel(student_ref, scale_ref, ceiling_ref, mass_ref, new_ref, total_ref, partial):
    new_ref[...] = scale_ref[...] * jnp.minimum(1.0, ceiling_ref[...] / mass_ref[...])
    rows, columns = student_ref.shape
    block = 64

    def body(i, carry):
        at = pl.ds(pl.multiple_of(i * block, block), block)
        total = jnp.zeros((block, LANES), f32)
        for j in range(0, columns, LANES):
            value = student_ref[at, j : j + LANES]
            total = total + value * value * new_ref[:, j : j + LANES]
        partial[at, :] = total
        return carry

    lax.fori_loop(0, rows // block, body, 0)
    total_ref[...] = jnp.sum(jnp.transpose(partial[...]), axis=0, keepdims=True)


def rows_at(depth, side, paired):
    if paired:
        return 0
    core = lax.axis_index("sample") % 2
    return pl.multiple_of((core if side == 0 else 1 - core) * depth, LANES)


def products(at, parts, refs, blocks_ref, depth, paired):
    chip, place = lax.axis_index("sample") // 2, lax.axis_index("cls")
    total = None
    for (mask, side), ref in zip(parts, refs):
        left = blocks_ref[chip ^ mask ^ place, :, pl.ds(rows_at(depth, side, paired), ref.shape[0])]
        part = jnp.dot(left, ref[:, at], preferred_element_type=f32)
        total = part if total is None else total + part
    return total


def partial_kernel(count, depth, paired, parts, *refs):
    feature_refs, head_refs = refs[:count], refs[count : count + len(parts)]
    blocks_ref, logits_ref = refs[count + len(parts) :]
    for i, ref in enumerate(feature_refs):
        blocks_ref[i] = ref[...]
    columns = logits_ref.shape[1]
    tile = min(256, columns)
    for i in range(0, columns, tile):
        at = slice(i, i + tile)
        logits_ref[:, at] = products(at, parts, head_refs, blocks_ref, depth, paired)


def turn_kernel(blocks_ref, turned_ref):
    for i in range(blocks_ref.shape[0]):
        turned_ref[i] = jnp.transpose(blocks_ref[i])


def student_kernel(depth, paired, parts, logits_ref, blocks_ref, *refs):
    head_refs = refs[: len(parts)]
    student_ref, slope_ref, sums_ref, buffer, student_sum, plan_sum = refs[len(parts) :]
    rows, columns = logits_ref.shape
    tile = min(256, columns)
    block = min(128, rows)
    for i in range(0, columns, tile):
        at = slice(i, i + tile)
        slot = (i // tile) % 2
        buffer[slot] = logits_ref[:, at] + products(at, parts, head_refs, blocks_ref, depth, paired)
        for first in range(0, rows, block):
            row = slice(first, first + block)
            student_total = plan_total = None
            for j in range(0, tile, LANES):
                out = slice(i + j, i + j + LANES)
                tanh = jnp.tanh(buffer[slot, row, j : j + LANES] * (1.0 / softcap))
                student = jnp.exp(softcap * tanh)
                plan = student * student
                student_ref[row, out] = student
                slope_ref[row, out] = (1.0 - tanh * tanh).astype(bf16)
                student_total = student if student_total is None else student_total + student
                plan_total = plan if plan_total is None else plan_total + plan
            if i > 0:
                student_total, plan_total = student_total + student_sum[row, :], plan_total + plan_sum[row, :]
            student_sum[row, :] = student_total
            plan_sum[row, :] = plan_total
    sums_ref[0:1, :] = jnp.sum(jnp.transpose(student_sum[...]), axis=0, keepdims=True)
    sums_ref[1:2, :] = jnp.sum(jnp.transpose(plan_sum[...]), axis=0, keepdims=True)


def column_kernel(student_ref, scale_ref, mass_ref, *refs):
    total_ref, inverse = refs[-2:]
    inverse[...] = as_column(1.0 / mass_ref[...])
    rows, columns = student_ref.shape
    block = 8

    def body(i, total):
        at = pl.ds(pl.multiple_of(i * block, block), block)
        factor = inverse[at, :]
        new = []
        for j in range(0, columns, LANES):
            value = student_ref[at, j : j + LANES]
            new.append(total[j // LANES] + value * value * factor)
        return tuple(new)

    start = tuple(jnp.zeros((block, LANES), f32) for _ in range(0, columns, LANES))
    total = lax.fori_loop(0, rows // block, body, start, unroll=4)
    for j, value in enumerate(total):
        at = slice(j * LANES, (j + 1) * LANES)
        total_ref[:, at] = jnp.sum(value, axis=0, keepdims=True) * scale_ref[:, at]


def head_products(turned_ref, core, depth, grad_ref, at, mine_ref, theirs_ref):
    for where, out_ref in ((core, mine_ref), (1 - core, theirs_ref)):
        left = turned_ref[pl.ds(pl.multiple_of(where * depth, depth), depth), :]
        out_ref[:, at] = jnp.dot(left, grad_ref[:, at], preferred_element_type=f32).astype(bf16)


def gradient_kernel(
    depth, paired, far, parts, student_ref, slope_ref, scale_ref, students_ref, mass_ref, turned_ref, *refs
):
    head_refs = refs[: len(parts)]
    out_ref, grad_ref, mine_ref, theirs_ref, share_ref, inverse, students, targets_ref, sent = refs[len(parts) :]
    me, place = lax.axis_index("sample"), lax.axis_index("cls")
    chip, core = me // 2, me % 2
    groups = lax.axis_size("cls")
    inverse[...] = as_column(1.0 / mass_ref[...])
    students[...] = as_column(1.0 / students_ref[...])
    columns = student_ref.shape[1]
    tile = min(256, columns)
    turned = turned_ref.at[place ^ chip ^ far]

    for i in range(0, columns, tile):
        for j in range(i, i + tile, LANES):
            at = slice(j, j + LANES)
            student = student_ref[:, at]
            target = (student * student * scale_ref[:, at] * inverse[...]).astype(bf16)
            targets_ref[:, at] = target
            grad_ref[:, at] = ((student * students[...] - wide(target)) * wide(slope_ref[:, at])).astype(bf16)
        head_products(turned, core, depth, grad_ref, slice(i, i + tile), mine_ref, theirs_ref)
    copy = pltpu.make_async_copy(targets_ref, out_ref, sent)
    copy.start()
    for (mask, side), ref in zip(parts, head_refs):

        @pl.when((chip ^ mask) == (place ^ (groups - 1)))
        def _():
            at = pl.ds(rows_at(depth, side, paired), ref.shape[0])
            share_ref[:, at] = matmul(grad_ref[...], ref[...], ((1,), (1,))).astype(bf16)

    copy.wait()


def near_kernel(depth, near, grad_ref, turned_ref, *refs):
    me, place = lax.axis_index("sample"), lax.axis_index("cls")
    chip, core = me // 2, me % 2
    columns = grad_ref.shape[1]
    tile = min(256, columns)
    for index, mask in enumerate(near):
        turned = turned_ref.at[place ^ chip ^ mask]
        for i in range(0, columns, tile):
            head_products(turned, core, depth, grad_ref, slice(i, i + tile), refs[2 * index], refs[2 * index + 1])


def shares_kernel(depth, paired, parts, grad_ref, *refs):
    head_refs, shares_ref = refs[: len(parts)], refs[-1]
    chip, place = lax.axis_index("sample") // 2, lax.axis_index("cls")
    for (mask, side), ref in zip(parts, head_refs):
        at = pl.ds(rows_at(depth, side, paired), ref.shape[0])
        shares_ref[chip ^ mask ^ place, :, at] = matmul(grad_ref[...], ref[...], ((1,), (1,))).astype(bf16)

def per_device(features, head, class_cap):
    rows, width = features.shape
    depth, classes = head.shape
    samples = lax.axis_size("sample")
    groups = lax.axis_size("cls")
    ratio = rows * samples / (classes * groups)
    me = lax.axis_index("sample")
    place = lax.axis_index("cls")
    chip, core = me // 2, me % 2
    first, second = chip_axes(samples)

    features_from, pieces, sibling = gather(features, head)
    paired = depth % LANES != 0

    def sides(mask, same):
        other = flip(same, "sample", 1) if mask else sibling
        if paired:
            pair = jnp.where(core == 0, same, other), jnp.where(core == 0, other, same)
            return [((mask // 2, 0), jnp.concatenate(pair, axis=0))]
        return [((mask // 2, 0), same), ((mask // 2, 1), other)]

    early = [part for mask in [0] + first + second for part in sides(mask, pieces[mask])]
    blocks, logits = call(
        functools.partial(partial_kernel, groups, depth, paired, [at for at, _ in early]),
        [((groups, rows, width), bf16), ((rows, classes), f32)],
        features_from + [part for _, part in early],
    )
    late = []
    for mask in [a | b for a in first for b in second]:
        late += sides(mask, lax.optimization_barrier((logits, pieces[mask]))[1])
    tile = min(256, classes)
    student, slope, sums = call(
        functools.partial(student_kernel, depth, paired, [at for at, _ in late]),
        [((rows, classes), f32), ((rows, classes), bf16), ((2, rows), f32)],
        [logits, blocks] + [part for _, part in late],
        [pltpu.VMEM((2, rows, tile), f32), pltpu.VMEM((rows, LANES), f32), pltpu.VMEM((rows, LANES), f32)],
        aliases={0: 0},
    )
    (turned,) = call(turn_kernel, [((groups, width, rows), bf16)], [blocks])

    def total(value, axis, masks):
        for part in [flip(value, axis, mask) for mask in reversed(masks)]:
            value = lax.optimization_barrier(value + part)
        return value

    def row_total(value):
        return total(value, "cls", range(1, groups))

    def column_total(value):
        return total(value + flip(value, "sample", 1), "sample", range(2, samples, 2))

    ceiling = (wide(class_cap) * ratio)[None]
    sums = row_total(sums)
    students_mass, mass = sums[0:1], sums[1:2]
    scale = jnp.ones((1, classes), f32)
    for iteration in range(ITERS):
        (mass,) = call(
            column_kernel,
            [((1, classes), f32)],
            [student, scale, mass],
            [pltpu.VMEM((rows, LANES), f32)],
            [turned] if iteration == 0 else [],
        )
        scale, mass = call(
            row_kernel,
            [((1, classes), f32), ((1, rows), f32)],
            [student, scale, ceiling, column_total(mass)],
            [pltpu.VMEM((rows, LANES), f32)],
        )
        mass = row_total(mass)

    head_at = [at for at, _ in early + late]
    head_list = [part for _, part in early + late]
    near = first + second + [0]
    diagonal = [(a, b) for a in first for b in second]
    far = (diagonal[-1][0] | diagonal[-1][1]) // 2
    near = [a | b for a, b in diagonal[:-1]] + near
    targets, grad, mine, theirs, share = call(
        functools.partial(gradient_kernel, depth, paired, far, head_at),
        [((rows, classes), bf16)] * 2 + [((depth, classes), bf16)] * 2 + [((rows, width), bf16)],
        [student, slope, scale, students_mass, mass, turned] + head_list,
        [pltpu.VMEM((rows, LANES), f32)] * 2 + [pltpu.VMEM((rows, classes), bf16), pltpu.SemaphoreType.DMA],
        slow=(0,),
    )
    theirs = flip(theirs, "sample", 1)
    pairs = call(
        functools.partial(near_kernel, depth, [mask // 2 for mask in near]),
        [((depth, classes), bf16)] * (2 * len(near)),
        [grad, turned],
    )
    theirs, *pairs = lax.optimization_barrier((theirs, *pairs))
    block = lax.optimization_barrier((wide(mine) + wide(theirs)).astype(bf16))
    passed = {diagonal[-1]: cross(block, *diagonal[-1])}
    share_from = {groups - 2: flip(share, "cls", 1)}
    others = {mask: flip(pairs[2 * i + 1], "sample", 1) for i, mask in enumerate(near) if mask}
    (shares,) = call(
        functools.partial(shares_kernel, depth, paired, head_at),
        [((groups, rows, width), bf16)],
        [grad] + head_list,
        extra=[block],
    )

    onward = {1: shares[1]}
    for mask in range(2, groups, 2):
        received = share_from[mask] if mask in share_from else flip(shares[mask | 1], "cls", 1)
        onward[mask] = (wide(shares[mask]) + wide(received)).astype(bf16)
    ready = lax.optimization_barrier((*onward.values(), *others.values(), *passed.values(), pairs[-1]))
    onward = dict(zip(onward, ready))
    others = dict(zip(others, ready[len(onward) :]))
    passed = dict(zip(passed, ready[len(onward) + len(others) :]))
    own = wide(pairs[-2]) + wide(flip(ready[-1], "sample", 1))
    returned = [flip(value, "cls", mask) for mask, value in onward.items()]
    grad_features = sum([wide(value) for value in returned], wide(shares[0])).astype(bf16)

    mixed = {mask: wide(pairs[2 * i]) + wide(others[mask]) for i, mask in enumerate(near) if mask}
    for a, b in diagonal[:-1]:
        passed[a, b] = cross(mixed[a | b].astype(bf16), a, b)
    received = []
    for mask in first + second:
        total_of = mixed[mask]
        for (a, b), more in passed.items():
            if mask == (b if mask in second else a):
                total_of = total_of + jnp.where((core == 0) == (mask in second), wide(more), 0.0)
        received.append(flip(total_of.astype(bf16), "sample", mask))
    received = lax.optimization_barrier((*received, grad_features))
    grad_features = received[-1]
    grad_head = sum([wide(part) for part in received[:-1]], own).astype(bf16)
    return (targets, grad_features, grad_head)


def solution(mesh):
    return jax.shard_map(
        per_device,
        mesh=mesh,
        in_specs=(P("sample", "cls"), P("sample", "cls"), P("cls")),
        out_specs=(P("sample", "cls"), P("sample", "cls"), P("sample", "cls")),
        check_vma=False,
    )
```

```python
import functools

import jax
import jax.numpy as jnp
from jax import lax
from jax.experimental import pallas as pl
from jax.experimental.pallas import tpu as pltpu
from jax.sharding import PartitionSpec as P

ITERS = 3


softcap = 15.0
sharpen = 2.0
f32 = jnp.float32
bf16 = jnp.bfloat16
LANES = 128


def wide(value):
    return value.astype(f32)


def matmul(left, right, dims):
    return lax.dot_general(left, right, (dims, ((), ())), preferred_element_type=f32)


def flip(value, axis, mask):
    return lax.ppermute(value, axis, [(i, i ^ mask) for i in range(lax.axis_size(axis))])


def cross(value, even, odd):
    size = lax.axis_size("sample")
    return lax.ppermute(value, "sample", [(i, i ^ (odd if i % 2 else even)) for i in range(size)])


def chip_axes(size):
    chips = size // 2
    bits = chips.bit_length() - 1
    low = 1 << ((bits + 1) // 2)
    first = [2 * m for m in range(1, low)]
    second = [2 * low * m for m in range(1, chips // low)]
    return first, second


def gather(features, head):
    samples, groups = lax.axis_size("sample"), lax.axis_size("cls")
    core = lax.axis_index("sample") % 2
    first, second = chip_axes(samples)
    blocks = {mask: flip(features, "cls", mask) for mask in range(2, groups, 2)}
    held = {mask: flip(head, "sample", mask) for mask in first + second}
    blocks[1] = flip(features, "cls", 1)
    sibling = flip(head, "sample", 1)
    for mask in range(2, groups, 2):
        blocks[mask | 1] = flip(blocks[mask], "cls", 1)
    ready = lax.optimization_barrier((*held.values(), *[blocks[mask] for mask in range(2, groups, 2)]))
    held = dict(zip(held, ready))
    for a in first:
        for b in second:
            passed = jnp.where(core == 0, held[a], held[b])
            passed = lax.optimization_barrier((passed, sibling, blocks[1]))[0]
            held[a | b] = cross(passed, b, a)
    blocks[0], held[0] = features, head
    return [blocks[mask] for mask in range(groups)], held, sibling


def fast(value):
    return pltpu.with_memory_space_constraint(value, pltpu.VMEM)


def call(kernel, outputs, operands, scratch=(), extra=(), slow=(), limit=16):
    spec = pl.BlockSpec(memory_space=pltpu.VMEM)
    return pl.pallas_call(
        kernel,
        out_shape=tuple(
            jax.ShapeDtypeStruct(shape, dtype) if i in slow else pltpu.VMEM(shape, dtype)
            for i, (shape, dtype) in enumerate(outputs)
        ),
        in_specs=[spec] * len(operands) + [pl.BlockSpec(memory_space=pl.ANY)] * len(extra),
        out_specs=tuple(pl.BlockSpec(memory_space=pl.ANY) if i in slow else spec for i in range(len(outputs))),
        scratch_shapes=list(scratch),
        compiler_params=pltpu.CompilerParams(vmem_limit_bytes=limit << 20),
        cost_estimate=pl.CostEstimate(flops=1, bytes_accessed=1, transcendentals=0),
    )(*[fast(operand) for operand in operands], *extra)


def as_column(row):
    return jnp.transpose(jnp.broadcast_to(row, (LANES, row.shape[1])))


def row_kernel(student_ref, scale_ref, ceiling_ref, mass_ref, new_ref, total_ref, partial):
    new_ref[...] = scale_ref[...] * jnp.minimum(1.0, ceiling_ref[...] / mass_ref[...])
    rows, columns = student_ref.shape
    block = 64

    def body(i, carry):
        at = pl.ds(pl.multiple_of(i * block, block), block)
        total = jnp.zeros((block, LANES), f32)
        for j in range(0, columns, LANES):
            value = student_ref[at, j : j + LANES]
            total = total + value * value * new_ref[:, j : j + LANES]
        partial[at, :] = total
        return carry

    lax.fori_loop(0, rows // block, body, 0)
    total_ref[...] = jnp.sum(jnp.transpose(partial[...]), axis=0, keepdims=True)


def rows_at(depth, side, paired):
    if paired:
        return 0
    core = lax.axis_index("sample") % 2
    return pl.multiple_of((core if side == 0 else 1 - core) * depth, LANES)


def products(at, parts, refs, blocks_ref, depth, paired):
    chip, place = lax.axis_index("sample") // 2, lax.axis_index("cls")
    total = None
    for (mask, side), ref in zip(parts, refs):
        left = blocks_ref[chip ^ mask ^ place, :, pl.ds(rows_at(depth, side, paired), ref.shape[0])]
        part = jnp.dot(left, ref[:, at], preferred_element_type=f32)
        total = part if total is None else total + part
    return total


def partial_kernel(count, depth, paired, parts, *refs):
    feature_refs, head_refs = refs[:count], refs[count : count + len(parts)]
    blocks_ref, logits_ref = refs[count + len(parts) :]
    for i, ref in enumerate(feature_refs):
        blocks_ref[i] = ref[...]
    columns = logits_ref.shape[1]
    tile = min(256, columns)
    for i in range(0, columns, tile):
        at = slice(i, i + tile)
        logits_ref[:, at] = products(at, parts, head_refs, blocks_ref, depth, paired)


def turn_kernel(blocks_ref, turned_ref):
    for i in range(blocks_ref.shape[0]):
        turned_ref[i] = jnp.transpose(blocks_ref[i])


def student_kernel(depth, paired, parts, logits_ref, blocks_ref, *refs):
    head_refs = refs[: len(parts)]
    student_ref, slope_ref, sums_ref, buffer, student_sum, plan_sum = refs[len(parts) :]
    rows, columns = logits_ref.shape
    tile = min(256, columns)
    block = min(128, rows)
    for i in range(0, columns, tile):
        at = slice(i, i + tile)
        slot = (i // tile) % 2
        buffer[slot] = logits_ref[:, at] + products(at, parts, head_refs, blocks_ref, depth, paired)
        for first in range(0, rows, block):
            row = slice(first, first + block)
            student_total = plan_total = None
            for j in range(0, tile, LANES):
                out = slice(i + j, i + j + LANES)
                tanh = jnp.tanh(buffer[slot, row, j : j + LANES] * (1.0 / softcap))
                student = jnp.exp(softcap * tanh)
                plan = student * student
                student_ref[row, out] = student
                slope_ref[row, out] = (1.0 - tanh * tanh).astype(bf16)
                student_total = student if student_total is None else student_total + student
                plan_total = plan if plan_total is None else plan_total + plan
            if i > 0:
                student_total, plan_total = student_total + student_sum[row, :], plan_total + plan_sum[row, :]
            student_sum[row, :] = student_total
            plan_sum[row, :] = plan_total
    sums_ref[0:1, :] = jnp.sum(jnp.transpose(student_sum[...]), axis=0, keepdims=True)
    sums_ref[1:2, :] = jnp.sum(jnp.transpose(plan_sum[...]), axis=0, keepdims=True)


def column_kernel(student_ref, scale_ref, mass_ref, *refs):
    total_ref, inverse = refs[-2:]
    inverse[...] = as_column(1.0 / mass_ref[...])
    rows, columns = student_ref.shape
    block = 8

    def body(i, total):
        at = pl.ds(pl.multiple_of(i * block, block), block)
        factor = inverse[at, :]
        new = []
        for j in range(0, columns, LANES):
            value = student_ref[at, j : j + LANES]
            new.append(total[j // LANES] + value * value * factor)
        return tuple(new)

    start = tuple(jnp.zeros((block, LANES), f32) for _ in range(0, columns, LANES))
    total = lax.fori_loop(0, rows // block, body, start, unroll=4)
    for j, value in enumerate(total):
        at = slice(j * LANES, (j + 1) * LANES)
        total_ref[:, at] = jnp.sum(value, axis=0, keepdims=True) * scale_ref[:, at]


def head_products(turned_ref, core, depth, grad_ref, at, mine_ref, theirs_ref):
    for where, out_ref in ((core, mine_ref), (1 - core, theirs_ref)):
        left = turned_ref[pl.ds(pl.multiple_of(where * depth, depth), depth), :]
        out_ref[:, at] = jnp.dot(left, grad_ref[:, at], preferred_element_type=f32).astype(bf16)


def gradient_kernel(
    depth, paired, far, parts, student_ref, slope_ref, scale_ref, students_ref, mass_ref, turned_ref, *refs
):
    head_refs = refs[: len(parts)]
    out_ref, grad_ref, mine_ref, theirs_ref, share_ref, inverse, students, targets_ref, sent = refs[len(parts) :]
    me, place = lax.axis_index("sample"), lax.axis_index("cls")
    chip, core = me // 2, me % 2
    groups = lax.axis_size("cls")
    inverse[...] = as_column(1.0 / mass_ref[...])
    students[...] = as_column(1.0 / students_ref[...])
    columns = student_ref.shape[1]
    tile = min(256, columns)
    turned = turned_ref.at[place ^ chip ^ far]

    for i in range(0, columns, tile):
        for j in range(i, i + tile, LANES):
            at = slice(j, j + LANES)
            student = student_ref[:, at]
            target = (student * student * scale_ref[:, at] * inverse[...]).astype(bf16)
            targets_ref[:, at] = target
            grad_ref[:, at] = ((student * students[...] - wide(target)) * wide(slope_ref[:, at])).astype(bf16)
        head_products(turned, core, depth, grad_ref, slice(i, i + tile), mine_ref, theirs_ref)
    copy = pltpu.make_async_copy(targets_ref, out_ref, sent)
    copy.start()
    for (mask, side), ref in zip(parts, head_refs):

        @pl.when((chip ^ mask) == (place ^ (groups - 1)))
        def _():
            at = pl.ds(rows_at(depth, side, paired), ref.shape[0])
            share_ref[:, at] = matmul(grad_ref[...], ref[...], ((1,), (1,))).astype(bf16)

    copy.wait()


def near_kernel(depth, near, grad_ref, turned_ref, *refs):
    me, place = lax.axis_index("sample"), lax.axis_index("cls")
    chip, core = me // 2, me % 2
    columns = grad_ref.shape[1]
    tile = min(256, columns)
    for index, mask in enumerate(near):
        turned = turned_ref.at[place ^ chip ^ mask]
        for i in range(0, columns, tile):
            head_products(turned, core, depth, grad_ref, slice(i, i + tile), refs[2 * index], refs[2 * index + 1])


def shares_kernel(depth, paired, parts, grad_ref, *refs):
    head_refs, shares_ref = refs[: len(parts)], refs[-1]
    chip, place = lax.axis_index("sample") // 2, lax.axis_index("cls")
    for (mask, side), ref in zip(parts, head_refs):
        at = pl.ds(rows_at(depth, side, paired), ref.shape[0])
        shares_ref[chip ^ mask ^ place, :, at] = matmul(grad_ref[...], ref[...], ((1,), (1,))).astype(bf16)

def per_device(features, head, class_cap):
    rows, width = features.shape
    depth, classes = head.shape
    samples = lax.axis_size("sample")
    groups = lax.axis_size("cls")
    ratio = rows * samples / (classes * groups)
    me = lax.axis_index("sample")
    place = lax.axis_index("cls")
    chip, core = me // 2, me % 2
    first, second = chip_axes(samples)

    features_from, pieces, sibling = gather(features, head)
    paired = depth % LANES != 0

    def sides(mask, same):
        other = flip(same, "sample", 1) if mask else sibling
        if paired:
            pair = jnp.where(core == 0, same, other), jnp.where(core == 0, other, same)
            return [((mask // 2, 0), jnp.concatenate(pair, axis=0))]
        return [((mask // 2, 0), same), ((mask // 2, 1), other)]

    early = [part for mask in [0] + first + second for part in sides(mask, pieces[mask])]
    blocks, logits = call(
        functools.partial(partial_kernel, groups, depth, paired, [at for at, _ in early]),
        [((groups, rows, width), bf16), ((rows, classes), f32)],
        features_from + [part for _, part in early],
    )
    late = []
    for mask in [a | b for a in first for b in second]:
        late += sides(mask, lax.optimization_barrier((logits, pieces[mask]))[1])
    tile = min(256, classes)
    student, slope, sums = call(
        functools.partial(student_kernel, depth, paired, [at for at, _ in late]),
        [((rows, classes), f32), ((rows, classes), bf16), ((2, rows), f32)],
        [logits, blocks] + [part for _, part in late],
        [pltpu.VMEM((2, rows, tile), f32), pltpu.VMEM((rows, LANES), f32), pltpu.VMEM((rows, LANES), f32)],
    )
    (turned,) = call(turn_kernel, [((groups, width, rows), bf16)], [blocks])

    def total(value, axis, masks):
        for part in [flip(value, axis, mask) for mask in reversed(masks)]:
            value = lax.optimization_barrier(value + part)
        return value

    def row_total(value):
        return total(value, "cls", range(1, groups))

    def column_total(value):
        return total(value + flip(value, "sample", 1), "sample", range(2, samples, 2))

    ceiling = (wide(class_cap) * ratio)[None]
    sums = row_total(sums)
    students_mass, mass = sums[0:1], sums[1:2]
    scale = jnp.ones((1, classes), f32)
    for iteration in range(ITERS):
        (mass,) = call(
            column_kernel,
            [((1, classes), f32)],
            [student, scale, mass],
            [pltpu.VMEM((rows, LANES), f32)],
            [turned] if iteration == 0 else [],
        )
        scale, mass = call(
            row_kernel,
            [((1, classes), f32), ((1, rows), f32)],
            [student, scale, ceiling, column_total(mass)],
            [pltpu.VMEM((rows, LANES), f32)],
        )
        mass = row_total(mass)

    head_at = [at for at, _ in early + late]
    head_list = [part for _, part in early + late]
    near = first + second + [0]
    diagonal = [(a, b) for a in first for b in second]
    far = (diagonal[-1][0] | diagonal[-1][1]) // 2
    near = [a | b for a, b in diagonal[:-1]] + near
    targets, grad, mine, theirs, share = call(
        functools.partial(gradient_kernel, depth, paired, far, head_at),
        [((rows, classes), bf16)] * 2 + [((depth, classes), bf16)] * 2 + [((rows, width), bf16)],
        [student, slope, scale, students_mass, mass, turned] + head_list,
        [pltpu.VMEM((rows, LANES), f32)] * 2 + [pltpu.VMEM((rows, classes), bf16), pltpu.SemaphoreType.DMA],
        slow=(0,),
    )
    theirs = flip(theirs, "sample", 1)
    pairs = call(
        functools.partial(near_kernel, depth, [mask // 2 for mask in near]),
        [((depth, classes), bf16)] * (2 * len(near)),
        [grad, turned],
    )
    theirs, *pairs = lax.optimization_barrier((theirs, *pairs))
    block = lax.optimization_barrier((wide(mine) + wide(theirs)).astype(bf16))
    passed = {diagonal[-1]: cross(block, *diagonal[-1])}
    share_from = {groups - 2: flip(share, "cls", 1)}
    others = {mask: flip(pairs[2 * i + 1], "sample", 1) for i, mask in enumerate(near) if mask}
    (shares,) = call(
        functools.partial(shares_kernel, depth, paired, head_at),
        [((groups, rows, width), bf16)],
        [grad] + head_list,
        extra=[block],
    )

    onward = {1: shares[1]}
    for mask in range(2, groups, 2):
        received = share_from[mask] if mask in share_from else flip(shares[mask | 1], "cls", 1)
        onward[mask] = (wide(shares[mask]) + wide(received)).astype(bf16)
    ready = lax.optimization_barrier((*onward.values(), *others.values(), *passed.values(), pairs[-1]))
    onward = dict(zip(onward, ready))
    others = dict(zip(others, ready[len(onward) :]))
    passed = dict(zip(passed, ready[len(onward) + len(others) :]))
    own = wide(pairs[-2]) + wide(flip(ready[-1], "sample", 1))
    returned = [flip(value, "cls", mask) for mask, value in onward.items()]
    grad_features = sum([wide(value) for value in returned], wide(shares[0])).astype(bf16)

    mixed = {mask: wide(pairs[2 * i]) + wide(others[mask]) for i, mask in enumerate(near) if mask}
    for a, b in diagonal[:-1]:
        passed[a, b] = cross(mixed[a | b].astype(bf16), a, b)
    received = []
    for mask in first + second:
        total_of = mixed[mask]
        for (a, b), more in passed.items():
            if mask == (b if mask in second else a):
                total_of = total_of + jnp.where((core == 0) == (mask in second), wide(more), 0.0)
        received.append(flip(total_of.astype(bf16), "sample", mask))
    received = lax.optimization_barrier((*received, grad_features))
    grad_features = received[-1]
    grad_head = sum([wide(part) for part in received[:-1]], own).astype(bf16)
    return (targets, grad_features, grad_head)


def solution(mesh):
    return jax.shard_map(
        per_device,
        mesh=mesh,
        in_specs=(P("sample", "cls"), P("sample", "cls"), P("cls")),
        out_specs=(P("sample", "cls"), P("sample", "cls"), P("sample", "cls")),
        check_vma=False,
    )
```

```python
import functools

import jax
import jax.numpy as jnp
from jax import lax
from jax.experimental import pallas as pl
from jax.experimental.pallas import tpu as pltpu
from jax.sharding import PartitionSpec as P

ITERS = 3


softcap = 15.0
sharpen = 2.0
f32 = jnp.float32
bf16 = jnp.bfloat16
LANES = 128


def wide(value):
    return value.astype(f32)


def matmul(left, right, dims):
    return lax.dot_general(left, right, (dims, ((), ())), preferred_element_type=f32)


def flip(value, axis, mask):
    return lax.ppermute(value, axis, [(i, i ^ mask) for i in range(lax.axis_size(axis))])


def cross(value, even, odd):
    size = lax.axis_size("sample")
    return lax.ppermute(value, "sample", [(i, i ^ (odd if i % 2 else even)) for i in range(size)])


def chip_axes(size):
    chips = size // 2
    bits = chips.bit_length() - 1
    low = 1 << ((bits + 1) // 2)
    first = [2 * m for m in range(1, low)]
    second = [2 * low * m for m in range(1, chips // low)]
    return first, second


def gather(features, head):
    samples, groups = lax.axis_size("sample"), lax.axis_size("cls")
    core = lax.axis_index("sample") % 2
    first, second = chip_axes(samples)
    blocks = {mask: flip(features, "cls", mask) for mask in range(2, groups, 2)}
    held = {mask: flip(head, "sample", mask) for mask in first + second}
    blocks[1] = flip(features, "cls", 1)
    sibling = flip(head, "sample", 1)
    for mask in range(2, groups, 2):
        blocks[mask | 1] = flip(blocks[mask], "cls", 1)
    ready = lax.optimization_barrier((*held.values(), *[blocks[mask] for mask in range(2, groups, 2)]))
    held = dict(zip(held, ready))
    for a in first:
        for b in second:
            passed = jnp.where(core == 0, held[a], held[b])
            passed = lax.optimization_barrier((passed, sibling, blocks[1]))[0]
            held[a | b] = cross(passed, b, a)
    blocks[0], held[0] = features, head
    return [blocks[mask] for mask in range(groups)], held, sibling


def fast(value):
    return pltpu.with_memory_space_constraint(value, pltpu.VMEM)


def call(kernel, outputs, operands, scratch=(), extra=(), slow=(), limit=16):
    spec = pl.BlockSpec(memory_space=pltpu.VMEM)
    return pl.pallas_call(
        kernel,
        out_shape=tuple(
            jax.ShapeDtypeStruct(shape, dtype) if i in slow else pltpu.VMEM(shape, dtype)
            for i, (shape, dtype) in enumerate(outputs)
        ),
        in_specs=[spec] * len(operands) + [pl.BlockSpec(memory_space=pl.ANY)] * len(extra),
        out_specs=tuple(pl.BlockSpec(memory_space=pl.ANY) if i in slow else spec for i in range(len(outputs))),
        scratch_shapes=list(scratch),
        compiler_params=pltpu.CompilerParams(vmem_limit_bytes=limit << 20),
        cost_estimate=pl.CostEstimate(flops=1, bytes_accessed=1, transcendentals=0),
    )(*[fast(operand) for operand in operands], *extra)


def as_column(row):
    return jnp.transpose(jnp.broadcast_to(row, (LANES, row.shape[1])))


def row_kernel(student_ref, scale_ref, ceiling_ref, mass_ref, new_ref, total_ref, partial):
    new_ref[...] = scale_ref[...] * jnp.minimum(1.0, ceiling_ref[...] / mass_ref[...])
    rows, columns = student_ref.shape
    block = 64

    def body(i, carry):
        at = pl.ds(pl.multiple_of(i * block, block), block)
        total = jnp.zeros((block, LANES), f32)
        for j in range(0, columns, LANES):
            value = student_ref[at, j : j + LANES]
            total = total + value * value * new_ref[:, j : j + LANES]
        partial[at, :] = total
        return carry

    lax.fori_loop(0, rows // block, body, 0)
    total_ref[...] = jnp.sum(jnp.transpose(partial[...]), axis=0, keepdims=True)


def rows_at(depth, side, paired):
    if paired:
        return 0
    core = lax.axis_index("sample") % 2
    return pl.multiple_of((core if side == 0 else 1 - core) * depth, LANES)


def products(at, parts, refs, blocks_ref, depth, paired):
    chip, place = lax.axis_index("sample") // 2, lax.axis_index("cls")
    total = None
    for (mask, side), ref in zip(parts, refs):
        left = blocks_ref[chip ^ mask ^ place, :, pl.ds(rows_at(depth, side, paired), ref.shape[0])]
        part = jnp.dot(left, ref[:, at], preferred_element_type=f32)
        total = part if total is None else total + part
    return total


def partial_kernel(count, depth, paired, parts, *refs):
    feature_refs, head_refs = refs[:count], refs[count : count + len(parts)]
    blocks_ref, logits_ref = refs[count + len(parts) :]
    for i, ref in enumerate(feature_refs):
        blocks_ref[i] = ref[...]
    columns = logits_ref.shape[1]
    tile = min(256, columns)
    for i in range(0, columns, tile):
        at = slice(i, i + tile)
        logits_ref[:, at] = products(at, parts, head_refs, blocks_ref, depth, paired)


def turn_kernel(blocks_ref, turned_ref):
    for i in range(blocks_ref.shape[0]):
        turned_ref[i] = jnp.transpose(blocks_ref[i])


def student_kernel(depth, paired, parts, logits_ref, blocks_ref, *refs):
    head_refs = refs[: len(parts)]
    student_ref, slope_ref, sums_ref, buffer, student_sum, plan_sum = refs[len(parts) :]
    rows, columns = logits_ref.shape
    tile = min(256, columns)
    block = min(128, rows)
    for i in range(0, columns, tile):
        at = slice(i, i + tile)
        slot = (i // tile) % 2
        buffer[slot] = logits_ref[:, at] + products(at, parts, head_refs, blocks_ref, depth, paired)
        for first in range(0, rows, block):
            row = slice(first, first + block)
            student_total = plan_total = None
            for j in range(0, tile, LANES):
                out = slice(i + j, i + j + LANES)
                tanh = jnp.tanh(buffer[slot, row, j : j + LANES] * (1.0 / softcap))
                student = jnp.exp(softcap * tanh)
                plan = student * student
                student_ref[row, out] = student
                slope_ref[row, out] = (1.0 - tanh * tanh).astype(bf16)
                student_total = student if student_total is None else student_total + student
                plan_total = plan if plan_total is None else plan_total + plan
            if i > 0:
                student_total, plan_total = student_total + student_sum[row, :], plan_total + plan_sum[row, :]
            student_sum[row, :] = student_total
            plan_sum[row, :] = plan_total
    sums_ref[0:1, :] = jnp.sum(jnp.transpose(student_sum[...]), axis=0, keepdims=True)
    sums_ref[1:2, :] = jnp.sum(jnp.transpose(plan_sum[...]), axis=0, keepdims=True)


def column_kernel(student_ref, scale_ref, mass_ref, *refs):
    total_ref, inverse = refs[-2:]
    inverse[...] = as_column(1.0 / mass_ref[...])
    rows, columns = student_ref.shape
    block = 8

    def body(i, total):
        at = pl.ds(pl.multiple_of(i * block, block), block)
        factor = inverse[at, :]
        new = []
        for j in range(0, columns, LANES):
            value = student_ref[at, j : j + LANES]
            new.append(total[j // LANES] + value * value * factor)
        return tuple(new)

    start = tuple(jnp.zeros((block, LANES), f32) for _ in range(0, columns, LANES))
    total = lax.fori_loop(0, rows // block, body, start, unroll=4)
    for j, value in enumerate(total):
        at = slice(j * LANES, (j + 1) * LANES)
        total_ref[:, at] = jnp.sum(value, axis=0, keepdims=True) * scale_ref[:, at]


def head_products(turned_ref, core, depth, grad_ref, at, mine_ref, theirs_ref):
    for where, out_ref in ((core, mine_ref), (1 - core, theirs_ref)):
        left = turned_ref[pl.ds(pl.multiple_of(where * depth, depth), depth), :]
        out_ref[:, at] = jnp.dot(left, grad_ref[:, at], preferred_element_type=f32).astype(bf16)


def gradient_kernel(
    depth, paired, far, parts, student_ref, slope_ref, scale_ref, students_ref, mass_ref, turned_ref, *refs
):
    head_refs = refs[: len(parts)]
    out_ref, grad_ref, mine_ref, theirs_ref, share_ref, inverse, students, targets_ref, sent = refs[len(parts) :]
    me, place = lax.axis_index("sample"), lax.axis_index("cls")
    chip, core = me // 2, me % 2
    groups = lax.axis_size("cls")
    inverse[...] = as_column(1.0 / mass_ref[...])
    students[...] = as_column(1.0 / students_ref[...])
    columns = student_ref.shape[1]
    tile = min(256, columns)
    turned = turned_ref.at[place ^ chip ^ far]
    copies = []

    for i in range(0, columns, tile):
        for j in range(i, i + tile, LANES):
            at = slice(j, j + LANES)
            student = student_ref[:, at]
            target = (student * student * scale_ref[:, at] * inverse[...]).astype(bf16)
            targets_ref[:, at] = target
            grad_ref[:, at] = ((student * students[...] - wide(target)) * wide(slope_ref[:, at])).astype(bf16)
        at = slice(i, i + tile)
        copies.append(pltpu.make_async_copy(targets_ref.at[:, at], out_ref.at[:, at], sent.at[i // tile]))
        copies[-1].start()
        head_products(turned, core, depth, grad_ref, at, mine_ref, theirs_ref)
    for (mask, side), ref in zip(parts, head_refs):

        @pl.when((chip ^ mask) == (place ^ (groups - 1)))
        def _():
            at = pl.ds(rows_at(depth, side, paired), ref.shape[0])
            share_ref[:, at] = matmul(grad_ref[...], ref[...], ((1,), (1,))).astype(bf16)

    for copy in copies:
        copy.wait()


def near_kernel(depth, near, grad_ref, turned_ref, *refs):
    me, place = lax.axis_index("sample"), lax.axis_index("cls")
    chip, core = me // 2, me % 2
    columns = grad_ref.shape[1]
    tile = min(256, columns)
    for index, mask in enumerate(near):
        turned = turned_ref.at[place ^ chip ^ mask]
        for i in range(0, columns, tile):
            head_products(turned, core, depth, grad_ref, slice(i, i + tile), refs[2 * index], refs[2 * index + 1])


def shares_kernel(depth, paired, parts, grad_ref, *refs):
    count = len(parts)
    head_refs, shares_ref, buffers, arrived = refs[:count], refs[count + 1], refs[count + 2 : -1], refs[-1]
    chip, place = lax.axis_index("sample") // 2, lax.axis_index("cls")
    copies = [
        pltpu.make_async_copy(ref, buffer, arrived.at[i]) for i, (ref, buffer) in enumerate(zip(head_refs, buffers))
    ]
    for copy in copies:
        copy.start()
    for (mask, side), buffer, copy in zip(parts, buffers, copies):
        copy.wait()
        at = pl.ds(rows_at(depth, side, paired), buffer.shape[0])
        shares_ref[chip ^ mask ^ place, :, at] = matmul(grad_ref[...], buffer[...], ((1,), (1,))).astype(bf16)


def per_device(features, head, class_cap):
    rows, width = features.shape
    depth, classes = head.shape
    samples = lax.axis_size("sample")
    groups = lax.axis_size("cls")
    ratio = rows * samples / (classes * groups)
    me = lax.axis_index("sample")
    place = lax.axis_index("cls")
    chip, core = me // 2, me % 2
    first, second = chip_axes(samples)

    features_from, pieces, sibling = gather(features, head)
    paired = depth % LANES != 0

    def sides(mask, same):
        other = flip(same, "sample", 1) if mask else sibling
        if paired:
            pair = jnp.where(core == 0, same, other), jnp.where(core == 0, other, same)
            return [((mask // 2, 0), jnp.concatenate(pair, axis=0))]
        return [((mask // 2, 0), same), ((mask // 2, 1), other)]

    early = [part for mask in [0] + first + second for part in sides(mask, pieces[mask])]
    blocks, logits = call(
        functools.partial(partial_kernel, groups, depth, paired, [at for at, _ in early]),
        [((groups, rows, width), bf16), ((rows, classes), f32)],
        features_from + [part for _, part in early],
    )
    late = []
    for mask in [a | b for a in first for b in second]:
        late += sides(mask, lax.optimization_barrier((logits, pieces[mask]))[1])
    tile = min(256, classes)
    student, slope, sums = call(
        functools.partial(student_kernel, depth, paired, [at for at, _ in late]),
        [((rows, classes), f32), ((rows, classes), bf16), ((2, rows), f32)],
        [logits, blocks] + [part for _, part in late],
        [pltpu.VMEM((2, rows, tile), f32), pltpu.VMEM((rows, LANES), f32), pltpu.VMEM((rows, LANES), f32)],
    )
    (turned,) = call(turn_kernel, [((groups, width, rows), bf16)], [blocks])

    def total(value, axis, masks):
        for part in [flip(value, axis, mask) for mask in reversed(masks)]:
            value = lax.optimization_barrier(value + part)
        return value

    def row_total(value):
        return total(value, "cls", range(1, groups))

    def column_total(value):
        return total(value + flip(value, "sample", 1), "sample", range(2, samples, 2))

    ceiling = (wide(class_cap) * ratio)[None]
    sums = row_total(sums)
    students_mass, mass = sums[0:1], sums[1:2]
    scale = jnp.ones((1, classes), f32)
    for iteration in range(ITERS):
        (mass,) = call(
            column_kernel,
            [((1, classes), f32)],
            [student, scale, mass],
            [pltpu.VMEM((rows, LANES), f32)],
            [turned] if iteration == 0 else [],
        )
        scale, mass = call(
            row_kernel,
            [((1, classes), f32), ((1, rows), f32)],
            [student, scale, ceiling, column_total(mass)],
            [pltpu.VMEM((rows, LANES), f32)],
        )
        mass = row_total(mass)

    head_at = [at for at, _ in early + late]
    head_list = [part for _, part in early + late]
    near = first + second + [0]
    diagonal = [(a, b) for a in first for b in second]
    far = (diagonal[-1][0] | diagonal[-1][1]) // 2
    near = [a | b for a, b in diagonal[:-1]] + near
    targets, grad, mine, theirs, share = call(
        functools.partial(gradient_kernel, depth, paired, far, head_at),
        [((rows, classes), bf16)] * 2 + [((depth, classes), bf16)] * 2 + [((rows, width), bf16)],
        [student, slope, scale, students_mass, mass, turned] + head_list,
        [pltpu.VMEM((rows, LANES), f32)] * 2 + [pltpu.VMEM((rows, classes), bf16), pltpu.SemaphoreType.DMA((classes // tile,))],
        slow=(0,),
    )
    theirs = flip(theirs, "sample", 1)
    pairs = call(
        functools.partial(near_kernel, depth, [mask // 2 for mask in near]),
        [((depth, classes), bf16)] * (2 * len(near)),
        [grad, turned],
    )
    theirs, *pairs = lax.optimization_barrier((theirs, *pairs))
    block = lax.optimization_barrier((wide(mine) + wide(theirs)).astype(bf16))
    passed = {diagonal[-1]: cross(block, *diagonal[-1])}
    share_from = {groups - 2: flip(share, "cls", 1)}
    others = {mask: flip(pairs[2 * i + 1], "sample", 1) for i, mask in enumerate(near) if mask}
    (shares,) = call(
        functools.partial(shares_kernel, depth, paired, head_at),
        [((groups, rows, width), bf16)],
        [grad],
        [pltpu.VMEM(part.shape, bf16) for part in head_list] + [pltpu.SemaphoreType.DMA((len(head_list),))],
        extra=head_list + [block],
    )

    onward = {1: shares[1]}
    for mask in range(2, groups, 2):
        received = share_from[mask] if mask in share_from else flip(shares[mask | 1], "cls", 1)
        onward[mask] = (wide(shares[mask]) + wide(received)).astype(bf16)
    ready = lax.optimization_barrier((*onward.values(), *others.values(), *passed.values(), pairs[-1]))
    onward = dict(zip(onward, ready))
    others = dict(zip(others, ready[len(onward) :]))
    passed = dict(zip(passed, ready[len(onward) + len(others) :]))
    own = wide(pairs[-2]) + wide(flip(ready[-1], "sample", 1))
    returned = [flip(value, "cls", mask) for mask, value in onward.items()]
    grad_features = sum([wide(value) for value in returned], wide(shares[0])).astype(bf16)

    mixed = {mask: wide(pairs[2 * i]) + wide(others[mask]) for i, mask in enumerate(near) if mask}
    for a, b in diagonal[:-1]:
        passed[a, b] = cross(mixed[a | b].astype(bf16), a, b)
    received = []
    for mask in first + second:
        total_of = mixed[mask]
        for (a, b), more in passed.items():
            if mask == (b if mask in second else a):
                total_of = total_of + jnp.where((core == 0) == (mask in second), wide(more), 0.0)
        received.append(flip(total_of.astype(bf16), "sample", mask))
    received = lax.optimization_barrier((*received, grad_features))
    grad_features = received[-1]
    grad_head = sum([wide(part) for part in received[:-1]], own).astype(bf16)
    return (targets, grad_features, grad_head)


def solution(mesh):
    return jax.shard_map(
        per_device,
        mesh=mesh,
        in_specs=(P("sample", "cls"), P("sample", "cls"), P("cls")),
        out_specs=(P("sample", "cls"), P("sample", "cls"), P("sample", "cls")),
        check_vma=False,
    )
```

```python
import functools

import jax
import jax.numpy as jnp
from jax import lax
from jax.experimental import pallas as pl
from jax.experimental.pallas import tpu as pltpu
from jax.sharding import PartitionSpec as P

ITERS = 3


softcap = 15.0
sharpen = 2.0
f32 = jnp.float32
bf16 = jnp.bfloat16
LANES = 128


def wide(value):
    return value.astype(f32)


def matmul(left, right, dims):
    return lax.dot_general(left, right, (dims, ((), ())), preferred_element_type=f32)


def flip(value, axis, mask):
    return lax.ppermute(value, axis, [(i, i ^ mask) for i in range(lax.axis_size(axis))])


def cross(value, even, odd):
    size = lax.axis_size("sample")
    return lax.ppermute(value, "sample", [(i, i ^ (odd if i % 2 else even)) for i in range(size)])


def chip_axes(size):
    chips = size // 2
    bits = chips.bit_length() - 1
    low = 1 << ((bits + 1) // 2)
    first = [2 * m for m in range(1, low)]
    second = [2 * low * m for m in range(1, chips // low)]
    return first, second


def gather_head(head):
    size = lax.axis_size("sample")
    core = lax.axis_index("sample") % 2
    first, second = chip_axes(size)
    held = {mask: flip(head, "sample", mask) for mask in first + second}
    held[0] = head
    sibling = flip(head, "sample", 1)
    for a in first:
        for b in second:
            passed = lax.optimization_barrier((jnp.where(core == 0, held[a], held[b]), sibling))[0]
            held[a | b] = cross(passed, b, a)
    return held, sibling


def gather_features(features):
    size = lax.axis_size("cls")
    held = {0: features}
    for mask in list(range(2, size, 2)) + [1]:
        held[mask] = flip(features, "cls", mask)
    for mask in range(2, size, 2):
        held[mask | 1] = flip(lax.optimization_barrier((held[mask], held[1]))[0], "cls", 1)
    return [held[mask] for mask in range(size)]


def fast(value):
    return pltpu.with_memory_space_constraint(value, pltpu.VMEM)


def call(kernel, outputs, operands, scratch=(), extra=(), limit=16):
    spec = pl.BlockSpec(memory_space=pltpu.VMEM)
    return pl.pallas_call(
        kernel,
        out_shape=tuple(pltpu.VMEM(shape, dtype) for shape, dtype in outputs),
        in_specs=[spec] * len(operands) + [pl.BlockSpec(memory_space=pl.ANY)] * len(extra),
        out_specs=(spec,) * len(outputs),
        scratch_shapes=list(scratch),
        compiler_params=pltpu.CompilerParams(vmem_limit_bytes=limit << 20),
        cost_estimate=pl.CostEstimate(flops=1, bytes_accessed=1, transcendentals=0),
    )(*[fast(operand) for operand in operands], *extra)


def as_column(row):
    return jnp.transpose(jnp.broadcast_to(row, (LANES, row.shape[1])))


def row_kernel(student_ref, scale_ref, ceiling_ref, mass_ref, new_ref, total_ref, partial):
    new_ref[...] = scale_ref[...] * jnp.minimum(1.0, ceiling_ref[...] / mass_ref[...])
    rows, columns = student_ref.shape
    block = 64

    def body(i, carry):
        at = pl.ds(pl.multiple_of(i * block, block), block)
        total = jnp.zeros((block, LANES), f32)
        for j in range(0, columns, LANES):
            value = student_ref[at, j : j + LANES]
            total = total + value * value * new_ref[:, j : j + LANES]
        partial[at, :] = total
        return carry

    lax.fori_loop(0, rows // block, body, 0)
    total_ref[...] = jnp.sum(jnp.transpose(partial[...]), axis=0, keepdims=True)


def rows_at(depth, side, paired):
    if paired:
        return 0
    core = lax.axis_index("sample") % 2
    return pl.multiple_of((core if side == 0 else 1 - core) * depth, LANES)


def products(at, parts, refs, blocks_ref, depth, paired):
    chip, place = lax.axis_index("sample") // 2, lax.axis_index("cls")
    total = None
    for (mask, side), ref in zip(parts, refs):
        left = blocks_ref[chip ^ mask ^ place, :, pl.ds(rows_at(depth, side, paired), ref.shape[0])]
        part = jnp.dot(left, ref[:, at], preferred_element_type=f32)
        total = part if total is None else total + part
    return total


def partial_kernel(count, depth, paired, parts, *refs):
    feature_refs, head_refs = refs[:count], refs[count : count + len(parts)]
    blocks_ref, turned_ref, logits_ref = refs[count + len(parts) :]
    for i, ref in enumerate(feature_refs):
        blocks_ref[i] = ref[...]
    columns = logits_ref.shape[1]
    tile = min(256, columns)
    for i in range(0, columns, tile):
        at = slice(i, i + tile)
        logits_ref[:, at] = products(at, parts, head_refs, blocks_ref, depth, paired)
    for i, ref in enumerate(feature_refs):
        turned_ref[i] = jnp.transpose(ref[...])


def student_kernel(depth, paired, parts, logits_ref, blocks_ref, *refs):
    head_refs = refs[: len(parts)]
    student_ref, slope_ref, sums_ref, buffer, student_sum, plan_sum = refs[len(parts) :]
    rows, columns = logits_ref.shape
    tile = min(256, columns)
    block = min(128, rows)
    for i in range(0, columns, tile):
        at = slice(i, i + tile)
        slot = (i // tile) % 2
        buffer[slot] = logits_ref[:, at] + products(at, parts, head_refs, blocks_ref, depth, paired)
        for first in range(0, rows, block):
            row = slice(first, first + block)
            student_total = plan_total = None
            for j in range(0, tile, LANES):
                out = slice(i + j, i + j + LANES)
                tanh = jnp.tanh(buffer[slot, row, j : j + LANES] * (1.0 / softcap))
                student = jnp.exp(softcap * tanh)
                plan = student * student
                student_ref[row, out] = student
                slope_ref[row, out] = (1.0 - tanh * tanh).astype(bf16)
                student_total = student if student_total is None else student_total + student
                plan_total = plan if plan_total is None else plan_total + plan
            if i > 0:
                student_total, plan_total = student_total + student_sum[row, :], plan_total + plan_sum[row, :]
            student_sum[row, :] = student_total
            plan_sum[row, :] = plan_total
    sums_ref[0:1, :] = jnp.sum(jnp.transpose(student_sum[...]), axis=0, keepdims=True)
    sums_ref[1:2, :] = jnp.sum(jnp.transpose(plan_sum[...]), axis=0, keepdims=True)


def column_kernel(student_ref, scale_ref, mass_ref, total_ref, inverse):
    inverse[...] = as_column(1.0 / mass_ref[...])
    rows, columns = student_ref.shape
    block = 8

    def body(i, total):
        at = pl.ds(pl.multiple_of(i * block, block), block)
        factor = inverse[at, :]
        new = []
        for j in range(0, columns, LANES):
            value = student_ref[at, j : j + LANES]
            new.append(total[j // LANES] + value * value * factor)
        return tuple(new)

    start = tuple(jnp.zeros((block, LANES), f32) for _ in range(0, columns, LANES))
    total = lax.fori_loop(0, rows // block, body, start, unroll=4)
    for j, value in enumerate(total):
        at = slice(j * LANES, (j + 1) * LANES)
        total_ref[:, at] = jnp.sum(value, axis=0, keepdims=True) * scale_ref[:, at]


def head_products(turned_ref, core, depth, grad_ref, at, mine_ref, theirs_ref):
    for where, out_ref in ((core, mine_ref), (1 - core, theirs_ref)):
        left = turned_ref[pl.ds(pl.multiple_of(where * depth, depth), depth), :]
        out_ref[:, at] = jnp.dot(left, grad_ref[:, at], preferred_element_type=f32).astype(bf16)


def gradient_kernel(
    depth, paired, far, parts, student_ref, slope_ref, scale_ref, students_ref, mass_ref, turned_ref, *refs
):
    head_refs = refs[: len(parts)]
    targets_ref, grad_ref, mine_ref, theirs_ref, share_ref, inverse, students = refs[len(parts) :]
    me, place = lax.axis_index("sample"), lax.axis_index("cls")
    chip, core = me // 2, me % 2
    groups = lax.axis_size("cls")
    inverse[...] = as_column(1.0 / mass_ref[...])
    students[...] = as_column(1.0 / students_ref[...])
    columns = student_ref.shape[1]
    tile = min(256, columns)
    turned = turned_ref.at[place ^ chip ^ far]

    for i in range(0, columns, tile):
        for j in range(i, i + tile, LANES):
            at = slice(j, j + LANES)
            student = student_ref[:, at]
            target = (student * student * scale_ref[:, at] * inverse[...]).astype(bf16)
            targets_ref[:, at] = target
            grad_ref[:, at] = ((student * students[...] - wide(target)) * wide(slope_ref[:, at])).astype(bf16)
        head_products(turned, core, depth, grad_ref, slice(i, i + tile), mine_ref, theirs_ref)
    for (mask, side), ref in zip(parts, head_refs):

        @pl.when((chip ^ mask) == (place ^ (groups - 1)))
        def _():
            at = pl.ds(rows_at(depth, side, paired), ref.shape[0])
            share_ref[:, at] = matmul(grad_ref[...], ref[...], ((1,), (1,))).astype(bf16)


def near_kernel(depth, near, grad_ref, turned_ref, *refs):
    me, place = lax.axis_index("sample"), lax.axis_index("cls")
    chip, core = me // 2, me % 2
    columns = grad_ref.shape[1]
    tile = min(256, columns)
    pairs = refs[len(refs) - 2 * len(near) :]
    for index, mask in enumerate(near):
        turned = turned_ref.at[place ^ chip ^ mask]
        for i in range(0, columns, tile):
            at = slice(i, i + tile)
            head_products(turned, core, depth, grad_ref, at, pairs[2 * index], pairs[2 * index + 1])


def products_kernel(depth, paired, near, parts, grad_ref, turned_ref, *refs):
    head_refs, pairs, shares_ref = refs[: len(parts)], refs[-1 - 2 * len(near) : -1], refs[-1]
    chip, place = lax.axis_index("sample") // 2, lax.axis_index("cls")
    near_kernel(depth, near, grad_ref, turned_ref, *pairs)
    for (mask, side), ref in zip(parts, head_refs):
        at = pl.ds(rows_at(depth, side, paired), ref.shape[0])
        shares_ref[chip ^ mask ^ place, :, at] = matmul(grad_ref[...], ref[...], ((1,), (1,))).astype(bf16)


def per_device(features, head, class_cap):
    rows, width = features.shape
    depth, classes = head.shape
    samples = lax.axis_size("sample")
    groups = lax.axis_size("cls")
    ratio = rows * samples / (classes * groups)
    me = lax.axis_index("sample")
    place = lax.axis_index("cls")
    chip, core = me // 2, me % 2
    first, second = chip_axes(samples)

    pieces, sibling = gather_head(head)
    features_from = gather_features(features)
    paired = depth % LANES != 0

    def sides(mask, same):
        other = flip(same, "sample", 1) if mask else sibling
        if paired:
            pair = jnp.where(core == 0, same, other), jnp.where(core == 0, other, same)
            return [((mask // 2, 0), jnp.concatenate(pair, axis=0))]
        return [((mask // 2, 0), same), ((mask // 2, 1), other)]

    early = [part for mask in [0] + first + second for part in sides(mask, pieces[mask])]
    blocks, turned, logits = call(
        functools.partial(partial_kernel, groups, depth, paired, [at for at, _ in early]),
        [((groups, rows, width), bf16), ((groups, width, rows), bf16), ((rows, classes), f32)],
        features_from + [part for _, part in early],
    )
    late = []
    for mask in [a | b for a in first for b in second]:
        late += sides(mask, lax.optimization_barrier((logits, pieces[mask]))[1])
    tile = min(256, classes)
    student, slope, sums = call(
        functools.partial(student_kernel, depth, paired, [at for at, _ in late]),
        [((rows, classes), f32), ((rows, classes), bf16), ((2, rows), f32)],
        [logits, blocks] + [part for _, part in late],
        [pltpu.VMEM((2, rows, tile), f32), pltpu.VMEM((rows, LANES), f32), pltpu.VMEM((rows, LANES), f32)],
    )

    def total(value, axis, masks):
        for part in [flip(value, axis, mask) for mask in reversed(masks)]:
            value = lax.optimization_barrier(value + part)
        return value

    def row_total(value):
        return total(value, "cls", range(1, groups))

    def column_total(value):
        return total(value + flip(value, "sample", 1), "sample", range(2, samples, 2))

    ceiling = (wide(class_cap) * ratio)[None]
    sums = row_total(sums)
    students_mass, mass = sums[0:1], sums[1:2]
    scale = jnp.ones((1, classes), f32)
    for _ in range(ITERS):
        (mass,) = call(
            column_kernel,
            [((1, classes), f32)],
            [student, scale, mass],
            [pltpu.VMEM((rows, LANES), f32)],
        )
        scale, mass = call(
            row_kernel,
            [((1, classes), f32), ((1, rows), f32)],
            [student, scale, ceiling, column_total(mass)],
            [pltpu.VMEM((rows, LANES), f32)],
        )
        mass = row_total(mass)

    head_at = [at for at, _ in early + late]
    head_list = [part for _, part in early + late]
    near = [mask // 2 for mask in first + second]
    diagonal = [(a, b) for a in first for b in second]
    far = (diagonal[-1][0] | diagonal[-1][1]) // 2
    near = [(a | b) // 2 for a, b in diagonal[:-1]] + near
    targets, grad, mine, theirs, share = call(
        functools.partial(gradient_kernel, depth, paired, far, head_at),
        [((rows, classes), bf16)] * 2 + [((depth, classes), bf16)] * 2 + [((rows, width), bf16)],
        [student, slope, scale, students_mass, mass, turned] + head_list,
        [pltpu.VMEM((rows, LANES), f32)] * 2,
    )
    block = lax.optimization_barrier((wide(mine) + wide(flip(theirs, "sample", 1))).astype(bf16))
    passed = {diagonal[-1]: cross(block, *diagonal[-1])}
    share_from = {groups - 2: flip(share, "cls", 1)}

    results = call(
        functools.partial(products_kernel, depth, paired, near, head_at),
        [((depth, classes), bf16)] * (2 * len(near)) + [((groups, rows, width), bf16)],
        [grad, turned] + head_list,
        extra=[block],
    )
    shares = results[-1]
    arrived = list(passed.values()) + list(share_from.values())
    theirs = lax.optimization_barrier((*results[1:-1:2], *arrived))
    arrived = iter(theirs[len(near) :])
    passed = {at: next(arrived) for at in passed}
    share_from = {mask: next(arrived) for mask in share_from}

    onward = {1: shares[1]}
    for mask in range(2, groups, 2):
        received = share_from[mask] if mask in share_from else flip(shares[mask | 1], "cls", 1)
        onward[mask] = (wide(shares[mask]) + wide(received)).astype(bf16)
    ready = lax.optimization_barrier((*onward.values(), *theirs[: len(near)]))
    theirs = ready[len(onward) :]
    returned = [flip(value, "cls", mask) for mask, value in zip(onward, ready)]
    grad_features = sum([wide(value) for value in returned], wide(shares[0])).astype(bf16)

    mixed = {
        2 * mask: wide(results[2 * i]) + wide(flip(theirs[i], "sample", 1)) for i, mask in enumerate(near)
    }
    for a, b in diagonal[:-1]:
        passed[a, b] = cross(mixed[a | b].astype(bf16), a, b)
    sent = {}
    for mask in first + second:
        block = mixed[mask]
        for (a, b), more in passed.items():
            if mask == (b if mask in second else a):
                block = block + jnp.where((core == 0) == (mask in second), wide(more), 0.0)
        sent[mask] = block.astype(bf16)
    received = [flip(value, "sample", mask) for mask, value in sent.items()]
    mine, theirs = call(
        functools.partial(near_kernel, depth, [0]),
        [((depth, classes), bf16)] * 2,
        [grad, turned],
        extra=list(sent.values()),
    )
    own = wide(mine) + wide(flip(theirs, "sample", 1))
    received = lax.optimization_barrier((*received, grad_features))
    grad_features = received[-1]
    grad_head = sum([wide(part) for part in received[:-1]], own).astype(bf16)
    return (targets, grad_features, grad_head)


def solution(mesh):
    return jax.shard_map(
        per_device,
        mesh=mesh,
        in_specs=(P("sample", "cls"), P("sample", "cls"), P("cls")),
        out_specs=(P("sample", "cls"), P("sample", "cls"), P("sample", "cls")),
        check_vma=False,
    )
```

```python
import functools

import jax
import jax.numpy as jnp
from jax import lax
from jax.experimental import pallas as pl
from jax.experimental.pallas import tpu as pltpu
from jax.sharding import PartitionSpec as P

ITERS = 3


softcap = 15.0
sharpen = 2.0
f32 = jnp.float32
bf16 = jnp.bfloat16
LANES = 128


def wide(value):
    return value.astype(f32)


def matmul(left, right, dims):
    return lax.dot_general(left, right, (dims, ((), ())), preferred_element_type=f32)


def flip(value, axis, mask):
    return lax.ppermute(value, axis, [(i, i ^ mask) for i in range(lax.axis_size(axis))])


def cross(value, even, odd):
    size = lax.axis_size("sample")
    return lax.ppermute(value, "sample", [(i, i ^ (odd if i % 2 else even)) for i in range(size)])


def chip_axes(size):
    chips = size // 2
    bits = chips.bit_length() - 1
    low = 1 << ((bits + 1) // 2)
    first = [2 * m for m in range(1, low)]
    second = [2 * low * m for m in range(1, chips // low)]
    return first, second


def gather(features, head):
    samples, groups = lax.axis_size("sample"), lax.axis_size("cls")
    core = lax.axis_index("sample") % 2
    first, second = chip_axes(samples)
    blocks = {mask: flip(features, "cls", mask) for mask in range(2, groups, 2)}
    held = {mask: flip(head, "sample", mask) for mask in first + second}
    blocks[1] = flip(features, "cls", 1)
    sibling = flip(head, "sample", 1)
    for mask in range(2, groups, 2):
        blocks[mask | 1] = flip(blocks[mask], "cls", 1)
    ready = lax.optimization_barrier((*held.values(), *[blocks[mask] for mask in range(2, groups, 2)]))
    held = dict(zip(held, ready))
    for a in first:
        for b in second:
            passed = jnp.where(core == 0, held[a], held[b])
            passed = lax.optimization_barrier((passed, sibling, blocks[1]))[0]
            held[a | b] = cross(passed, b, a)
    blocks[0], held[0] = features, head
    return [blocks[mask] for mask in range(groups)], held, sibling


def fast(value):
    return pltpu.with_memory_space_constraint(value, pltpu.VMEM)


def call(kernel, outputs, operands, scratch=(), extra=(), slow=(), limit=16):
    spec = pl.BlockSpec(memory_space=pltpu.VMEM)
    return pl.pallas_call(
        kernel,
        out_shape=tuple(
            jax.ShapeDtypeStruct(shape, dtype) if i in slow else pltpu.VMEM(shape, dtype)
            for i, (shape, dtype) in enumerate(outputs)
        ),
        in_specs=[spec] * len(operands) + [pl.BlockSpec(memory_space=pl.ANY)] * len(extra),
        out_specs=tuple(pl.BlockSpec(memory_space=pl.ANY) if i in slow else spec for i in range(len(outputs))),
        scratch_shapes=list(scratch),
        compiler_params=pltpu.CompilerParams(vmem_limit_bytes=limit << 20),
        cost_estimate=pl.CostEstimate(flops=1, bytes_accessed=1, transcendentals=0),
    )(*[fast(operand) for operand in operands], *extra)


def as_column(row):
    return jnp.transpose(jnp.broadcast_to(row, (LANES, row.shape[1])))


def row_kernel(student_ref, scale_ref, ceiling_ref, mass_ref, new_ref, total_ref, partial):
    new_ref[...] = scale_ref[...] * jnp.minimum(1.0, ceiling_ref[...] / mass_ref[...])
    rows, columns = student_ref.shape
    block = 64

    def body(i, carry):
        at = pl.ds(pl.multiple_of(i * block, block), block)
        total = jnp.zeros((block, LANES), f32)
        for j in range(0, columns, LANES):
            value = student_ref[at, j : j + LANES]
            total = total + value * value * new_ref[:, j : j + LANES]
        partial[at, :] = total
        return carry

    lax.fori_loop(0, rows // block, body, 0)
    total_ref[...] = jnp.sum(jnp.transpose(partial[...]), axis=0, keepdims=True)


def rows_at(depth, side, paired):
    if paired:
        return 0
    core = lax.axis_index("sample") % 2
    return pl.multiple_of((core if side == 0 else 1 - core) * depth, LANES)


def products(at, parts, refs, blocks_ref, depth, paired):
    chip, place = lax.axis_index("sample") // 2, lax.axis_index("cls")
    total = None
    for (mask, side), ref in zip(parts, refs):
        left = blocks_ref[chip ^ mask ^ place, :, pl.ds(rows_at(depth, side, paired), ref.shape[0])]
        part = jnp.dot(left, ref[:, at], preferred_element_type=f32)
        total = part if total is None else total + part
    return total


def partial_kernel(count, depth, paired, parts, *refs):
    feature_refs, head_refs = refs[:count], refs[count : count + len(parts)]
    blocks_ref, logits_ref = refs[count + len(parts) :]
    for i, ref in enumerate(feature_refs):
        blocks_ref[i] = ref[...]
    columns = logits_ref.shape[1]
    tile = min(256, columns)
    for i in range(0, columns, tile):
        at = slice(i, i + tile)
        logits_ref[:, at] = products(at, parts, head_refs, blocks_ref, depth, paired)


def turn_kernel(blocks_ref, turned_ref):
    for i in range(blocks_ref.shape[0]):
        turned_ref[i] = jnp.transpose(blocks_ref[i])


def student_kernel(depth, paired, parts, logits_ref, blocks_ref, *refs):
    head_refs = refs[: len(parts)]
    student_ref, slope_ref, sums_ref, buffer, student_sum, plan_sum = refs[len(parts) :]
    rows, columns = logits_ref.shape
    tile = min(256, columns)
    block = min(128, rows)
    for i in range(0, columns, tile):
        at = slice(i, i + tile)
        slot = (i // tile) % 2
        buffer[slot] = logits_ref[:, at] + products(at, parts, head_refs, blocks_ref, depth, paired)
        for first in range(0, rows, block):
            row = slice(first, first + block)
            student_total = plan_total = None
            for j in range(0, tile, LANES):
                out = slice(i + j, i + j + LANES)
                tanh = jnp.tanh(buffer[slot, row, j : j + LANES] * (1.0 / softcap))
                student = jnp.exp(softcap * tanh)
                plan = student * student
                student_ref[row, out] = student
                slope_ref[row, out] = (1.0 - tanh * tanh).astype(bf16)
                student_total = student if student_total is None else student_total + student
                plan_total = plan if plan_total is None else plan_total + plan
            if i > 0:
                student_total, plan_total = student_total + student_sum[row, :], plan_total + plan_sum[row, :]
            student_sum[row, :] = student_total
            plan_sum[row, :] = plan_total
    sums_ref[0:1, :] = jnp.sum(jnp.transpose(student_sum[...]), axis=0, keepdims=True)
    sums_ref[1:2, :] = jnp.sum(jnp.transpose(plan_sum[...]), axis=0, keepdims=True)


def column_kernel(student_ref, scale_ref, mass_ref, *refs):
    total_ref, inverse = refs[-2:]
    inverse[...] = as_column(1.0 / mass_ref[...])
    rows, columns = student_ref.shape
    block = 8

    def body(i, total):
        at = pl.ds(pl.multiple_of(i * block, block), block)
        factor = inverse[at, :]
        new = []
        for j in range(0, columns, LANES):
            value = student_ref[at, j : j + LANES]
            new.append(total[j // LANES] + value * value * factor)
        return tuple(new)

    start = tuple(jnp.zeros((block, LANES), f32) for _ in range(0, columns, LANES))
    total = lax.fori_loop(0, rows // block, body, start, unroll=4)
    for j, value in enumerate(total):
        at = slice(j * LANES, (j + 1) * LANES)
        total_ref[:, at] = jnp.sum(value, axis=0, keepdims=True) * scale_ref[:, at]


def head_products(turned_ref, core, depth, grad_ref, at, mine_ref, theirs_ref):
    for where, out_ref in ((core, mine_ref), (1 - core, theirs_ref)):
        left = turned_ref[pl.ds(pl.multiple_of(where * depth, depth), depth), :]
        out_ref[:, at] = jnp.dot(left, grad_ref[:, at], preferred_element_type=f32).astype(bf16)


def gradient_kernel(
    depth, paired, far, parts, student_ref, slope_ref, scale_ref, students_ref, mass_ref, turned_ref, *refs
):
    head_refs = refs[: len(parts)]
    out_ref, grad_ref, mine_ref, theirs_ref, share_ref, inverse, students, targets_ref, sent = refs[len(parts) :]
    me, place = lax.axis_index("sample"), lax.axis_index("cls")
    chip, core = me // 2, me % 2
    groups = lax.axis_size("cls")
    inverse[...] = as_column(1.0 / mass_ref[...])
    students[...] = as_column(1.0 / students_ref[...])
    columns = student_ref.shape[1]
    tile = min(256, columns)
    turned = turned_ref.at[place ^ chip ^ far]

    for i in range(0, columns, tile):
        for j in range(i, i + tile, LANES):
            at = slice(j, j + LANES)
            student = student_ref[:, at]
            target = (student * student * scale_ref[:, at] * inverse[...]).astype(bf16)
            targets_ref[:, at] = target
            grad_ref[:, at] = ((student * students[...] - wide(target)) * wide(slope_ref[:, at])).astype(bf16)
        head_products(turned, core, depth, grad_ref, slice(i, i + tile), mine_ref, theirs_ref)
    copy = pltpu.make_async_copy(targets_ref, out_ref, sent)
    copy.start()
    for (mask, side), ref in zip(parts, head_refs):

        @pl.when((chip ^ mask) == (place ^ (groups - 1)))
        def _():
            at = pl.ds(rows_at(depth, side, paired), ref.shape[0])
            share_ref[:, at] = matmul(grad_ref[...], ref[...], ((1,), (1,))).astype(bf16)

    copy.wait()


def near_kernel(depth, near, grad_ref, turned_ref, *refs):
    refs = refs[len(refs) - 2 * len(near) :]
    me, place = lax.axis_index("sample"), lax.axis_index("cls")
    chip, core = me // 2, me % 2
    columns = grad_ref.shape[1]
    tile = min(256, columns)
    for index, mask in enumerate(near):
        turned = turned_ref.at[place ^ chip ^ mask]
        for i in range(0, columns, tile):
            head_products(turned, core, depth, grad_ref, slice(i, i + tile), refs[2 * index], refs[2 * index + 1])


def shares_kernel(depth, paired, parts, grad_ref, *refs):
    head_refs, shares_ref = refs[: len(parts)], refs[-1]
    chip, place = lax.axis_index("sample") // 2, lax.axis_index("cls")
    for (mask, side), ref in zip(parts, head_refs):
        at = pl.ds(rows_at(depth, side, paired), ref.shape[0])
        shares_ref[chip ^ mask ^ place, :, at] = matmul(grad_ref[...], ref[...], ((1,), (1,))).astype(bf16)

def per_device(features, head, class_cap):
    rows, width = features.shape
    depth, classes = head.shape
    samples = lax.axis_size("sample")
    groups = lax.axis_size("cls")
    ratio = rows * samples / (classes * groups)
    me = lax.axis_index("sample")
    place = lax.axis_index("cls")
    chip, core = me // 2, me % 2
    first, second = chip_axes(samples)

    features_from, pieces, sibling = gather(features, head)
    paired = depth % LANES != 0

    def sides(mask, same):
        other = flip(same, "sample", 1) if mask else sibling
        if paired:
            pair = jnp.where(core == 0, same, other), jnp.where(core == 0, other, same)
            return [((mask // 2, 0), jnp.concatenate(pair, axis=0))]
        return [((mask // 2, 0), same), ((mask // 2, 1), other)]

    early = [part for mask in [0] + first + second for part in sides(mask, pieces[mask])]
    blocks, logits = call(
        functools.partial(partial_kernel, groups, depth, paired, [at for at, _ in early]),
        [((groups, rows, width), bf16), ((rows, classes), f32)],
        features_from + [part for _, part in early],
    )
    late = []
    for mask in [a | b for a in first for b in second]:
        late += sides(mask, lax.optimization_barrier((logits, pieces[mask]))[1])
    tile = min(256, classes)
    student, slope, sums = call(
        functools.partial(student_kernel, depth, paired, [at for at, _ in late]),
        [((rows, classes), f32), ((rows, classes), bf16), ((2, rows), f32)],
        [logits, blocks] + [part for _, part in late],
        [pltpu.VMEM((2, rows, tile), f32), pltpu.VMEM((rows, LANES), f32), pltpu.VMEM((rows, LANES), f32)],
    )
    (turned,) = call(turn_kernel, [((groups, width, rows), bf16)], [blocks])

    def total(value, axis, masks):
        for part in [flip(value, axis, mask) for mask in reversed(masks)]:
            value = lax.optimization_barrier(value + part)
        return value

    def row_total(value):
        return total(value, "cls", range(1, groups))

    def column_total(value):
        return total(value + flip(value, "sample", 1), "sample", range(2, samples, 2))

    ceiling = (wide(class_cap) * ratio)[None]
    sums = row_total(sums)
    students_mass, mass = sums[0:1], sums[1:2]
    scale = jnp.ones((1, classes), f32)
    for iteration in range(ITERS):
        (mass,) = call(
            column_kernel,
            [((1, classes), f32)],
            [student, scale, mass],
            [pltpu.VMEM((rows, LANES), f32)],
            [turned] if iteration == 0 else [],
        )
        scale, mass = call(
            row_kernel,
            [((1, classes), f32), ((1, rows), f32)],
            [student, scale, ceiling, column_total(mass)],
            [pltpu.VMEM((rows, LANES), f32)],
        )
        mass = row_total(mass)

    head_at = [at for at, _ in early + late]
    head_list = [part for _, part in early + late]
    near = first + second + [0]
    diagonal = [(a, b) for a in first for b in second]
    far = (diagonal[-1][0] | diagonal[-1][1]) // 2
    near = [a | b for a, b in diagonal[:-1]] + near
    targets, grad, mine, theirs, share = call(
        functools.partial(gradient_kernel, depth, paired, far, head_at),
        [((rows, classes), bf16)] * 2 + [((depth, classes), bf16)] * 2 + [((rows, width), bf16)],
        [student, slope, scale, students_mass, mass, turned] + head_list,
        [pltpu.VMEM((rows, LANES), f32)] * 2 + [pltpu.VMEM((rows, classes), bf16), pltpu.SemaphoreType.DMA],
        slow=(0,),
    )
    theirs = flip(theirs, "sample", 1)
    pairs = call(
        functools.partial(near_kernel, depth, [mask // 2 for mask in near]),
        [((depth, classes), bf16)] * (2 * len(near)),
        [grad, turned] + head_list,
    )
    theirs, *pairs = lax.optimization_barrier((theirs, *pairs))
    block = lax.optimization_barrier((wide(mine) + wide(theirs)).astype(bf16))
    passed = {diagonal[-1]: cross(block, *diagonal[-1])}
    share_from = {groups - 2: flip(share, "cls", 1)}
    others = {mask: flip(pairs[2 * i + 1], "sample", 1) for i, mask in enumerate(near) if mask}
    (shares,) = call(
        functools.partial(shares_kernel, depth, paired, head_at),
        [((groups, rows, width), bf16)],
        [grad] + head_list,
        extra=[block],
    )

    onward = {1: shares[1]}
    for mask in range(2, groups, 2):
        received = share_from[mask] if mask in share_from else flip(shares[mask | 1], "cls", 1)
        onward[mask] = (wide(shares[mask]) + wide(received)).astype(bf16)
    ready = lax.optimization_barrier((*onward.values(), *others.values(), *passed.values(), pairs[-1]))
    onward = dict(zip(onward, ready))
    others = dict(zip(others, ready[len(onward) :]))
    passed = dict(zip(passed, ready[len(onward) + len(others) :]))
    own = wide(pairs[-2]) + wide(flip(ready[-1], "sample", 1))
    returned = [flip(value, "cls", mask) for mask, value in onward.items()]
    grad_features = sum([wide(value) for value in returned], wide(shares[0])).astype(bf16)

    mixed = {mask: wide(pairs[2 * i]) + wide(others[mask]) for i, mask in enumerate(near) if mask}
    for a, b in diagonal[:-1]:
        passed[a, b] = cross(mixed[a | b].astype(bf16), a, b)
    received = []
    for mask in first + second:
        total_of = mixed[mask]
        for (a, b), more in passed.items():
            if mask == (b if mask in second else a):
                total_of = total_of + jnp.where((core == 0) == (mask in second), wide(more), 0.0)
        received.append(flip(total_of.astype(bf16), "sample", mask))
    received = lax.optimization_barrier((*received, grad_features))
    grad_features = received[-1]
    grad_head = sum([wide(part) for part in received[:-1]], own).astype(bf16)
    return (targets, grad_features, grad_head)


def solution(mesh):
    return jax.shard_map(
        per_device,
        mesh=mesh,
        in_specs=(P("sample", "cls"), P("sample", "cls"), P("cls")),
        out_specs=(P("sample", "cls"), P("sample", "cls"), P("sample", "cls")),
        check_vma=False,
    )
```

```python
import functools

import jax
import jax.numpy as jnp
from jax import lax
from jax.experimental import pallas as pl
from jax.experimental.pallas import tpu as pltpu
from jax.sharding import PartitionSpec as P

ITERS = 3


softcap = 15.0
sharpen = 2.0
f32 = jnp.float32
bf16 = jnp.bfloat16
LANES = 128


def wide(value):
    return value.astype(f32)


def matmul(left, right, dims):
    return lax.dot_general(left, right, (dims, ((), ())), preferred_element_type=f32)


def flip(value, axis, mask):
    return lax.ppermute(value, axis, [(i, i ^ mask) for i in range(lax.axis_size(axis))])


def cross(value, even, odd):
    size = lax.axis_size("sample")
    return lax.ppermute(value, "sample", [(i, i ^ (odd if i % 2 else even)) for i in range(size)])


def chip_axes(size):
    chips = size // 2
    bits = chips.bit_length() - 1
    low = 1 << ((bits + 1) // 2)
    first = [2 * m for m in range(1, low)]
    second = [2 * low * m for m in range(1, chips // low)]
    return first, second


def gather(features, head):
    samples, groups = lax.axis_size("sample"), lax.axis_size("cls")
    core = lax.axis_index("sample") % 2
    first, second = chip_axes(samples)
    blocks = {mask: flip(features, "cls", mask) for mask in range(2, groups, 2)}
    held = {mask: flip(head, "sample", mask) for mask in first + second}
    blocks[1] = flip(features, "cls", 1)
    sibling = flip(head, "sample", 1)
    for mask in range(2, groups, 2):
        blocks[mask | 1] = flip(blocks[mask], "cls", 1)
    ready = lax.optimization_barrier((*held.values(), *[blocks[mask] for mask in range(2, groups, 2)]))
    held = dict(zip(held, ready))
    for a in first:
        for b in second:
            passed = jnp.where(core == 0, held[a], held[b])
            passed = lax.optimization_barrier((passed, sibling, blocks[1]))[0]
            held[a | b] = cross(passed, b, a)
    blocks[0], held[0] = features, head
    return [blocks[mask] for mask in range(groups)], held, sibling


def fast(value):
    return pltpu.with_memory_space_constraint(value, pltpu.VMEM)


def call(kernel, outputs, operands, scratch=(), extra=(), slow=(), limit=16):
    spec = pl.BlockSpec(memory_space=pltpu.VMEM)
    return pl.pallas_call(
        kernel,
        out_shape=tuple(
            jax.ShapeDtypeStruct(shape, dtype) if i in slow else pltpu.VMEM(shape, dtype)
            for i, (shape, dtype) in enumerate(outputs)
        ),
        in_specs=[spec] * len(operands) + [pl.BlockSpec(memory_space=pl.ANY)] * len(extra),
        out_specs=tuple(pl.BlockSpec(memory_space=pl.ANY) if i in slow else spec for i in range(len(outputs))),
        scratch_shapes=list(scratch),
        compiler_params=pltpu.CompilerParams(vmem_limit_bytes=limit << 20),
        cost_estimate=pl.CostEstimate(flops=1, bytes_accessed=1, transcendentals=0),
    )(*[fast(operand) for operand in operands], *extra)


def as_column(row):
    return jnp.transpose(jnp.broadcast_to(row, (LANES, row.shape[1])))


def row_kernel(student_ref, scale_ref, ceiling_ref, mass_ref, new_ref, total_ref, partial):
    new_ref[...] = scale_ref[...] * jnp.minimum(1.0, ceiling_ref[...] / mass_ref[...])
    rows, columns = student_ref.shape
    block = 64

    def body(i, carry):
        at = pl.ds(pl.multiple_of(i * block, block), block)
        total = jnp.zeros((block, LANES), f32)
        for j in range(0, columns, LANES):
            value = student_ref[at, j : j + LANES]
            total = total + value * value * new_ref[:, j : j + LANES]
        partial[at, :] = total
        return carry

    lax.fori_loop(0, rows // block, body, 0)
    total_ref[...] = jnp.sum(jnp.transpose(partial[...]), axis=0, keepdims=True)


def rows_at(depth, side, paired):
    if paired:
        return 0
    core = lax.axis_index("sample") % 2
    return pl.multiple_of((core if side == 0 else 1 - core) * depth, LANES)


def products(at, parts, refs, blocks_ref, depth, paired):
    chip, place = lax.axis_index("sample") // 2, lax.axis_index("cls")
    total = None
    for (mask, side), ref in zip(parts, refs):
        left = blocks_ref[chip ^ mask ^ place, :, pl.ds(rows_at(depth, side, paired), ref.shape[0])]
        part = jnp.dot(left, ref[:, at], preferred_element_type=f32)
        total = part if total is None else total + part
    return total


def partial_kernel(count, depth, paired, parts, *refs):
    feature_refs, head_refs = refs[:count], refs[count : count + len(parts)]
    blocks_ref, logits_ref = refs[count + len(parts) :]
    for i, ref in enumerate(feature_refs):
        blocks_ref[i] = ref[...]
    columns = logits_ref.shape[1]
    tile = min(256, columns)
    for i in range(0, columns, tile):
        at = slice(i, i + tile)
        logits_ref[:, at] = products(at, parts, head_refs, blocks_ref, depth, paired)


def turn_kernel(blocks_ref, turned_ref):
    for i in range(blocks_ref.shape[0]):
        turned_ref[i] = jnp.transpose(blocks_ref[i])


def student_kernel(depth, paired, parts, logits_ref, blocks_ref, *refs):
    head_refs = refs[: len(parts)]
    student_ref, slope_ref, sums_ref, buffer, student_sum, plan_sum = refs[len(parts) :]
    rows, columns = logits_ref.shape
    tile = min(256, columns)
    block = min(128, rows)
    for i in range(0, columns, tile):
        at = slice(i, i + tile)
        slot = (i // tile) % 2
        buffer[slot] = logits_ref[:, at] + products(at, parts, head_refs, blocks_ref, depth, paired)
        for first in range(0, rows, block):
            row = slice(first, first + block)
            student_total = plan_total = None
            for j in range(0, tile, LANES):
                out = slice(i + j, i + j + LANES)
                tanh = jnp.tanh(buffer[slot, row, j : j + LANES] * (1.0 / softcap))
                student = jnp.exp(softcap * tanh)
                plan = student * student
                student_ref[row, out] = student
                slope_ref[row, out] = (1.0 - tanh * tanh).astype(bf16)
                student_total = student if student_total is None else student_total + student
                plan_total = plan if plan_total is None else plan_total + plan
            if i > 0:
                student_total, plan_total = student_total + student_sum[row, :], plan_total + plan_sum[row, :]
            student_sum[row, :] = student_total
            plan_sum[row, :] = plan_total
    sums_ref[0:1, :] = jnp.sum(jnp.transpose(student_sum[...]), axis=0, keepdims=True)
    sums_ref[1:2, :] = jnp.sum(jnp.transpose(plan_sum[...]), axis=0, keepdims=True)


def column_kernel(student_ref, scale_ref, mass_ref, *refs):
    total_ref, inverse = refs[-2:]
    inverse[...] = as_column(1.0 / mass_ref[...])
    rows, columns = student_ref.shape
    block = 8

    def body(i, total):
        at = pl.ds(pl.multiple_of(i * block, block), block)
        factor = inverse[at, :]
        new = []
        for j in range(0, columns, LANES):
            value = student_ref[at, j : j + LANES]
            new.append(total[j // LANES] + value * value * factor)
        return tuple(new)

    start = tuple(jnp.zeros((block, LANES), f32) for _ in range(0, columns, LANES))
    total = lax.fori_loop(0, rows // block, body, start, unroll=4)
    for j, value in enumerate(total):
        at = slice(j * LANES, (j + 1) * LANES)
        total_ref[:, at] = jnp.sum(value, axis=0, keepdims=True) * scale_ref[:, at]


def head_products(turned_ref, core, depth, grad_ref, at, mine_ref, theirs_ref):
    for where, out_ref in ((core, mine_ref), (1 - core, theirs_ref)):
        left = turned_ref[pl.ds(pl.multiple_of(where * depth, depth), depth), :]
        out_ref[:, at] = jnp.dot(left, grad_ref[:, at], preferred_element_type=f32).astype(bf16)


def gradient_kernel(
    depth, paired, far, parts, student_ref, slope_ref, scale_ref, students_ref, mass_ref, turned_ref, *refs
):
    head_refs = refs[: len(parts)]
    out_ref, grad_ref, mine_ref, theirs_ref, share_ref, inverse, students, targets_ref, sent = refs[len(parts) :]
    me, place = lax.axis_index("sample"), lax.axis_index("cls")
    chip, core = me // 2, me % 2
    groups = lax.axis_size("cls")
    inverse[...] = as_column(1.0 / mass_ref[...])
    students[...] = as_column(1.0 / students_ref[...])
    columns = student_ref.shape[1]
    tile = min(256, columns)
    turned = turned_ref.at[place ^ chip ^ far]

    for i in range(0, columns, tile):
        for j in range(i, i + tile, LANES):
            at = slice(j, j + LANES)
            student = student_ref[:, at]
            target = (student * student * scale_ref[:, at] * inverse[...]).astype(bf16)
            targets_ref[:, at] = target
            grad_ref[:, at] = ((student * students[...] - wide(target)) * wide(slope_ref[:, at])).astype(bf16)
        head_products(turned, core, depth, grad_ref, slice(i, i + tile), mine_ref, theirs_ref)
    copy = pltpu.make_async_copy(targets_ref, out_ref, sent)
    copy.start()
    for (mask, side), ref in zip(parts, head_refs):

        @pl.when((chip ^ mask) == (place ^ (groups - 1)))
        def _():
            at = pl.ds(rows_at(depth, side, paired), ref.shape[0])
            share_ref[:, at] = matmul(grad_ref[...], ref[...], ((1,), (1,))).astype(bf16)

    copy.wait()


def near_kernel(depth, near, grad_ref, turned_ref, *refs):
    me, place = lax.axis_index("sample"), lax.axis_index("cls")
    chip, core = me // 2, me % 2
    columns = grad_ref.shape[1]
    tile = min(256, columns)
    for index, mask in enumerate(near):
        turned = turned_ref.at[place ^ chip ^ mask]
        for i in range(0, columns, tile):
            head_products(turned, core, depth, grad_ref, slice(i, i + tile), refs[2 * index], refs[2 * index + 1])


def sum_kernel(count, chosen, *refs):
    core = lax.axis_index("sample") % 2
    out_ref = refs[-1]
    for first in range(0, out_ref.shape[0], 16):
        at = slice(first, first + 16)
        total = wide(refs[0][at, :])
        for i, ref in enumerate(refs[1:-1], 1):
            value = wide(ref[at, :])
            total = total + (value if i < count else jnp.where(core == chosen, value, 0.0))
        out_ref[at, :] = total.astype(bf16)


def onward_kernel(count, shares_ref, *refs):
    received, outputs = refs[:count], refs[count:]
    outputs[0][...] = shares_ref[1]
    for i, ref in enumerate(received):
        for first in range(0, ref.shape[0], 16):
            at = slice(first, first + 16)
            outputs[1 + i][at, :] = (wide(shares_ref[2 + 2 * i, at, :]) + wide(ref[at, :])).astype(bf16)


def shares_kernel(depth, paired, parts, grad_ref, *refs):
    head_refs, shares_ref = refs[: len(parts)], refs[-1]
    chip, place = lax.axis_index("sample") // 2, lax.axis_index("cls")
    for (mask, side), ref in zip(parts, head_refs):
        at = pl.ds(rows_at(depth, side, paired), ref.shape[0])
        shares_ref[chip ^ mask ^ place, :, at] = matmul(grad_ref[...], ref[...], ((1,), (1,))).astype(bf16)

def per_device(features, head, class_cap):
    rows, width = features.shape
    depth, classes = head.shape
    samples = lax.axis_size("sample")
    groups = lax.axis_size("cls")
    ratio = rows * samples / (classes * groups)
    me = lax.axis_index("sample")
    place = lax.axis_index("cls")
    chip, core = me // 2, me % 2
    first, second = chip_axes(samples)

    features_from, pieces, sibling = gather(features, head)
    paired = depth % LANES != 0

    def sides(mask, same):
        other = flip(same, "sample", 1) if mask else sibling
        if paired:
            pair = jnp.where(core == 0, same, other), jnp.where(core == 0, other, same)
            return [((mask // 2, 0), jnp.concatenate(pair, axis=0))]
        return [((mask // 2, 0), same), ((mask // 2, 1), other)]

    early = [part for mask in [0] + first + second for part in sides(mask, pieces[mask])]
    blocks, logits = call(
        functools.partial(partial_kernel, groups, depth, paired, [at for at, _ in early]),
        [((groups, rows, width), bf16), ((rows, classes), f32)],
        features_from + [part for _, part in early],
    )
    late = []
    for mask in [a | b for a in first for b in second]:
        late += sides(mask, lax.optimization_barrier((logits, pieces[mask]))[1])
    tile = min(256, classes)
    student, slope, sums = call(
        functools.partial(student_kernel, depth, paired, [at for at, _ in late]),
        [((rows, classes), f32), ((rows, classes), bf16), ((2, rows), f32)],
        [logits, blocks] + [part for _, part in late],
        [pltpu.VMEM((2, rows, tile), f32), pltpu.VMEM((rows, LANES), f32), pltpu.VMEM((rows, LANES), f32)],
    )
    (turned,) = call(turn_kernel, [((groups, width, rows), bf16)], [blocks])

    def total(value, axis, masks):
        for part in [flip(value, axis, mask) for mask in reversed(masks)]:
            value = lax.optimization_barrier(value + part)
        return value

    def row_total(value):
        return total(value, "cls", range(1, groups))

    def column_total(value):
        return total(value + flip(value, "sample", 1), "sample", range(2, samples, 2))

    ceiling = (wide(class_cap) * ratio)[None]
    sums = row_total(sums)
    students_mass, mass = sums[0:1], sums[1:2]
    scale = jnp.ones((1, classes), f32)
    for iteration in range(ITERS):
        (mass,) = call(
            column_kernel,
            [((1, classes), f32)],
            [student, scale, mass],
            [pltpu.VMEM((rows, LANES), f32)],
            [turned] if iteration == 0 else [],
        )
        scale, mass = call(
            row_kernel,
            [((1, classes), f32), ((1, rows), f32)],
            [student, scale, ceiling, column_total(mass)],
            [pltpu.VMEM((rows, LANES), f32)],
        )
        mass = row_total(mass)

    head_at = [at for at, _ in early + late]
    head_list = [part for _, part in early + late]
    near = first + second + [0]
    diagonal = [(a, b) for a in first for b in second]
    far = (diagonal[-1][0] | diagonal[-1][1]) // 2
    near = [a | b for a, b in diagonal[:-1]] + near
    targets, grad, mine, theirs, share = call(
        functools.partial(gradient_kernel, depth, paired, far, head_at),
        [((rows, classes), bf16)] * 2 + [((depth, classes), bf16)] * 2 + [((rows, width), bf16)],
        [student, slope, scale, students_mass, mass, turned] + head_list,
        [pltpu.VMEM((rows, LANES), f32)] * 2 + [pltpu.VMEM((rows, classes), bf16), pltpu.SemaphoreType.DMA],
        slow=(0,),
    )
    theirs = flip(theirs, "sample", 1)
    pairs = call(
        functools.partial(near_kernel, depth, [mask // 2 for mask in near]),
        [((depth, classes), bf16)] * (2 * len(near)),
        [grad, turned],
    )
    theirs, *pairs = lax.optimization_barrier((theirs, *pairs))

    def head_sum(values, more=(), chosen=0):
        kernel = functools.partial(sum_kernel, len(values), chosen)
        return call(kernel, [((depth, classes), bf16)], list(values) + list(more))[0]

    block = head_sum([mine, theirs])
    passed = {diagonal[-1]: cross(block, *diagonal[-1])}
    share_from = {groups - 2: flip(share, "cls", 1)}
    others = {mask: flip(pairs[2 * i + 1], "sample", 1) for i, mask in enumerate(near) if mask}
    (shares,) = call(
        functools.partial(shares_kernel, depth, paired, head_at),
        [((groups, rows, width), bf16)],
        [grad] + head_list,
        extra=[block],
    )

    evens = range(2, groups, 2)
    came = [share_from[mask] if mask in share_from else flip(shares[mask | 1], "cls", 1) for mask in evens]
    made = call(functools.partial(onward_kernel, len(came)), [((rows, width), bf16)] * (1 + len(came)), [shares] + came)
    onward = dict(zip([1, *evens], made))
    ready = lax.optimization_barrier((*onward.values(), *others.values(), *passed.values(), pairs[-1]))
    onward = dict(zip(onward, ready))
    others = dict(zip(others, ready[len(onward) :]))
    passed = dict(zip(passed, ready[len(onward) + len(others) :]))
    own = wide(pairs[-2]) + wide(flip(ready[-1], "sample", 1))
    returned = [flip(value, "cls", mask) for mask, value in onward.items()]
    grad_features = sum([wide(value) for value in returned], wide(shares[0])).astype(bf16)

    mine_of = {mask: pairs[2 * i] for i, mask in enumerate(near)}
    for a, b in diagonal[:-1]:
        passed[a, b] = cross(head_sum([mine_of[a | b], others[a | b]]), a, b)
    received = []
    for mask in first + second:
        chosen = 0 if mask in second else 1
        more = [value for (a, b), value in passed.items() if mask == (a if chosen else b)]
        received.append(flip(head_sum([mine_of[mask], others[mask]], more, chosen), "sample", mask))
    received = lax.optimization_barrier((*received, grad_features))
    grad_features = received[-1]
    grad_head = sum([wide(part) for part in received[:-1]], own).astype(bf16)
    return (targets, grad_features, grad_head)


def solution(mesh):
    return jax.shard_map(
        per_device,
        mesh=mesh,
        in_specs=(P("sample", "cls"), P("sample", "cls"), P("cls")),
        out_specs=(P("sample", "cls"), P("sample", "cls"), P("sample", "cls")),
        check_vma=False,
    )
```

```python
import functools

import jax
import jax.numpy as jnp
from jax import lax
from jax.experimental import pallas as pl
from jax.experimental.pallas import tpu as pltpu
from jax.sharding import PartitionSpec as P

ITERS = 3


softcap = 15.0
sharpen = 2.0
f32 = jnp.float32
bf16 = jnp.bfloat16
LANES = 128


def wide(value):
    return value.astype(f32)


def matmul(left, right, dims):
    return lax.dot_general(left, right, (dims, ((), ())), preferred_element_type=f32)


def flip(value, axis, mask):
    return lax.ppermute(value, axis, [(i, i ^ mask) for i in range(lax.axis_size(axis))])


def cross(value, even, odd):
    size = lax.axis_size("sample")
    return lax.ppermute(value, "sample", [(i, i ^ (odd if i % 2 else even)) for i in range(size)])


def chip_axes(size):
    chips = size // 2
    bits = chips.bit_length() - 1
    low = 1 << ((bits + 1) // 2)
    first = [2 * m for m in range(1, low)]
    second = [2 * low * m for m in range(1, chips // low)]
    return first, second


def gather(features, head):
    samples, groups = lax.axis_size("sample"), lax.axis_size("cls")
    core = lax.axis_index("sample") % 2
    first, second = chip_axes(samples)
    blocks = {mask: flip(features, "cls", mask) for mask in range(2, groups, 2)}
    held = {mask: flip(head, "sample", mask) for mask in first + second}
    blocks[1] = flip(features, "cls", 1)
    sibling = flip(head, "sample", 1)
    for mask in range(2, groups, 2):
        blocks[mask | 1] = flip(blocks[mask], "cls", 1)
    ready = lax.optimization_barrier((*held.values(), *[blocks[mask] for mask in range(2, groups, 2)]))
    held = dict(zip(held, ready))
    for a in first:
        for b in second:
            passed = jnp.where(core == 0, held[a], held[b])
            passed = lax.optimization_barrier((passed, sibling, blocks[1]))[0]
            held[a | b] = cross(passed, b, a)
    blocks[0], held[0] = features, head
    return [blocks[mask] for mask in range(groups)], held, sibling


def fast(value):
    return pltpu.with_memory_space_constraint(value, pltpu.VMEM)


def call(kernel, outputs, operands, scratch=(), extra=(), slow=(), limit=16):
    spec = pl.BlockSpec(memory_space=pltpu.VMEM)
    return pl.pallas_call(
        kernel,
        out_shape=tuple(
            jax.ShapeDtypeStruct(shape, dtype) if i in slow else pltpu.VMEM(shape, dtype)
            for i, (shape, dtype) in enumerate(outputs)
        ),
        in_specs=[spec] * len(operands) + [pl.BlockSpec(memory_space=pl.ANY)] * len(extra),
        out_specs=tuple(pl.BlockSpec(memory_space=pl.ANY) if i in slow else spec for i in range(len(outputs))),
        scratch_shapes=list(scratch),
        compiler_params=pltpu.CompilerParams(vmem_limit_bytes=limit << 20),
        cost_estimate=pl.CostEstimate(flops=1, bytes_accessed=1, transcendentals=0),
    )(*[fast(operand) for operand in operands], *extra)


def as_column(row):
    return jnp.transpose(jnp.broadcast_to(row, (LANES, row.shape[1])))


def row_kernel(student_ref, scale_ref, ceiling_ref, mass_ref, new_ref, total_ref, partial):
    new_ref[...] = scale_ref[...] * jnp.minimum(1.0, ceiling_ref[...] / mass_ref[...])
    rows, columns = student_ref.shape
    block = 64

    def body(i, carry):
        at = pl.ds(pl.multiple_of(i * block, block), block)
        total = jnp.zeros((block, LANES), f32)
        for j in range(0, columns, LANES):
            value = student_ref[at, j : j + LANES]
            total = total + value * value * new_ref[:, j : j + LANES]
        partial[at, :] = total
        return carry

    lax.fori_loop(0, rows // block, body, 0)
    total_ref[...] = jnp.sum(jnp.transpose(partial[...]), axis=0, keepdims=True)


def rows_at(depth, side, paired):
    if paired:
        return 0
    core = lax.axis_index("sample") % 2
    return pl.multiple_of((core if side == 0 else 1 - core) * depth, LANES)


def products(at, parts, refs, blocks_ref, depth, paired):
    chip, place = lax.axis_index("sample") // 2, lax.axis_index("cls")
    total = None
    for (mask, side), ref in zip(parts, refs):
        left = blocks_ref[chip ^ mask ^ place, :, pl.ds(rows_at(depth, side, paired), ref.shape[0])]
        part = jnp.dot(left, ref[:, at], preferred_element_type=f32)
        total = part if total is None else total + part
    return total


def partial_kernel(count, depth, paired, parts, *refs):
    feature_refs, head_refs = refs[:count], refs[count : count + len(parts)]
    blocks_ref, logits_ref = refs[count + len(parts) :]
    for i, ref in enumerate(feature_refs):
        blocks_ref[i] = ref[...]
    columns = logits_ref.shape[1]
    tile = min(256, columns)
    for i in range(0, columns, tile):
        at = slice(i, i + tile)
        logits_ref[:, at] = products(at, parts, head_refs, blocks_ref, depth, paired)


def turn_kernel(blocks_ref, turned_ref):
    for i in range(blocks_ref.shape[0]):
        turned_ref[i] = jnp.transpose(blocks_ref[i])


def student_kernel(depth, paired, parts, logits_ref, blocks_ref, *refs):
    head_refs = refs[: len(parts)]
    student_ref, slope_ref, sums_ref, buffer, student_sum, plan_sum = refs[len(parts) :]
    rows, columns = logits_ref.shape
    tile = min(256, columns)
    block = min(128, rows)
    for i in range(0, columns, tile):
        at = slice(i, i + tile)
        slot = (i // tile) % 2
        buffer[slot] = logits_ref[:, at] + products(at, parts, head_refs, blocks_ref, depth, paired)
        for first in range(0, rows, block):
            row = slice(first, first + block)
            student_total = plan_total = None
            for j in range(0, tile, LANES):
                out = slice(i + j, i + j + LANES)
                tanh = jnp.tanh(buffer[slot, row, j : j + LANES] * (1.0 / softcap))
                student = jnp.exp(softcap * tanh)
                plan = student * student
                student_ref[row, out] = student
                slope_ref[row, out] = (1.0 - tanh * tanh).astype(bf16)
                student_total = student if student_total is None else student_total + student
                plan_total = plan if plan_total is None else plan_total + plan
            if i > 0:
                student_total, plan_total = student_total + student_sum[row, :], plan_total + plan_sum[row, :]
            student_sum[row, :] = student_total
            plan_sum[row, :] = plan_total
    sums_ref[0:1, :] = jnp.sum(jnp.transpose(student_sum[...]), axis=0, keepdims=True)
    sums_ref[1:2, :] = jnp.sum(jnp.transpose(plan_sum[...]), axis=0, keepdims=True)


def column_kernel(student_ref, scale_ref, mass_ref, *refs):
    total_ref, inverse = refs[-2:]
    inverse[...] = as_column(1.0 / mass_ref[...])
    rows, columns = student_ref.shape
    block = 8

    def body(i, total):
        at = pl.ds(pl.multiple_of(i * block, block), block)
        factor = inverse[at, :]
        new = []
        for j in range(0, columns, LANES):
            value = student_ref[at, j : j + LANES]
            new.append(total[j // LANES] + value * value * factor)
        return tuple(new)

    start = tuple(jnp.zeros((block, LANES), f32) for _ in range(0, columns, LANES))
    total = lax.fori_loop(0, rows // block, body, start, unroll=4)
    for j, value in enumerate(total):
        at = slice(j * LANES, (j + 1) * LANES)
        total_ref[:, at] = jnp.sum(value, axis=0, keepdims=True) * scale_ref[:, at]


def head_products(turned_ref, core, depth, grad_ref, at, mine_ref, theirs_ref):
    for where, out_ref in ((core, mine_ref), (1 - core, theirs_ref)):
        left = turned_ref[pl.ds(pl.multiple_of(where * depth, depth), depth), :]
        out_ref[:, at] = jnp.dot(left, grad_ref[:, at], preferred_element_type=f32).astype(bf16)


def gradient_kernel(
    depth, paired, far, parts, student_ref, slope_ref, scale_ref, students_ref, mass_ref, turned_ref, *refs
):
    head_refs = refs[: len(parts)]
    out_ref, grad_ref, mine_ref, theirs_ref, share_ref, inverse, students, targets_ref, sent = refs[len(parts) :]
    me, place = lax.axis_index("sample"), lax.axis_index("cls")
    chip, core = me // 2, me % 2
    groups = lax.axis_size("cls")
    inverse[...] = as_column(1.0 / mass_ref[...])
    students[...] = as_column(1.0 / students_ref[...])
    columns = student_ref.shape[1]
    tile = min(256, columns)
    turned = turned_ref.at[place ^ chip ^ far]

    for i in range(0, columns, tile):
        for j in range(i, i + tile, LANES):
            at = slice(j, j + LANES)
            student = student_ref[:, at]
            target = (student * student * scale_ref[:, at] * inverse[...]).astype(bf16)
            targets_ref[:, at] = target
            grad_ref[:, at] = ((student * students[...] - wide(target)) * wide(slope_ref[:, at])).astype(bf16)
        head_products(turned, core, depth, grad_ref, slice(i, i + tile), mine_ref, theirs_ref)
    copy = pltpu.make_async_copy(targets_ref, out_ref, sent)
    copy.start()
    for (mask, side), ref in zip(parts, head_refs):

        @pl.when((chip ^ mask) == (place ^ (groups - 1)))
        def _():
            at = pl.ds(rows_at(depth, side, paired), ref.shape[0])
            share_ref[:, at] = matmul(grad_ref[...], ref[...], ((1,), (1,))).astype(bf16)

    copy.wait()


def near_kernel(depth, near, grad_ref, turned_ref, *refs):
    me, place = lax.axis_index("sample"), lax.axis_index("cls")
    chip, core = me // 2, me % 2
    columns = grad_ref.shape[1]
    tile = min(256, columns)
    for index, mask in enumerate(near):
        turned = turned_ref.at[place ^ chip ^ mask]
        for i in range(0, columns, tile):
            head_products(turned, core, depth, grad_ref, slice(i, i + tile), refs[2 * index], refs[2 * index + 1])


def sum_kernel(count, chosen, *refs):
    core = lax.axis_index("sample") % 2
    out_ref = refs[-1]
    for first in range(0, out_ref.shape[0], 16):
        at = slice(first, first + 16)
        total = wide(refs[0][at, :])
        for i, ref in enumerate(refs[1:-1], 1):
            value = wide(ref[at, :])
            total = total + (value if i < count else jnp.where(core == chosen, value, 0.0))
        out_ref[at, :] = total.astype(bf16)


def onward_kernel(count, shares_ref, *refs):
    received, outputs = refs[:count], refs[count:]
    outputs[0][...] = shares_ref[1]
    for i, ref in enumerate(received):
        for first in range(0, ref.shape[0], 16):
            at = slice(first, first + 16)
            outputs[1 + i][at, :] = (wide(shares_ref[2 + 2 * i, at, :]) + wide(ref[at, :])).astype(bf16)


def shares_kernel(depth, paired, parts, grad_ref, *refs):
    head_refs, shares_ref = refs[: len(parts)], refs[-1]
    chip, place = lax.axis_index("sample") // 2, lax.axis_index("cls")
    for (mask, side), ref in zip(parts, head_refs):
        at = pl.ds(rows_at(depth, side, paired), ref.shape[0])
        shares_ref[chip ^ mask ^ place, :, at] = matmul(grad_ref[...], ref[...], ((1,), (1,))).astype(bf16)

def per_device(features, head, class_cap):
    rows, width = features.shape
    depth, classes = head.shape
    samples = lax.axis_size("sample")
    groups = lax.axis_size("cls")
    ratio = rows * samples / (classes * groups)
    me = lax.axis_index("sample")
    place = lax.axis_index("cls")
    chip, core = me // 2, me % 2
    first, second = chip_axes(samples)

    features_from, pieces, sibling = gather(features, head)
    paired = depth % LANES != 0

    def sides(mask, same):
        other = flip(same, "sample", 1) if mask else sibling
        if paired:
            pair = jnp.where(core == 0, same, other), jnp.where(core == 0, other, same)
            return [((mask // 2, 0), jnp.concatenate(pair, axis=0))]
        return [((mask // 2, 0), same), ((mask // 2, 1), other)]

    early = [part for mask in [0] + first + second for part in sides(mask, pieces[mask])]
    blocks, logits = call(
        functools.partial(partial_kernel, groups, depth, paired, [at for at, _ in early]),
        [((groups, rows, width), bf16), ((rows, classes), f32)],
        features_from + [part for _, part in early],
    )
    late = []
    for mask in [a | b for a in first for b in second]:
        late += sides(mask, lax.optimization_barrier((logits, pieces[mask]))[1])
    tile = min(256, classes)
    student, slope, sums = call(
        functools.partial(student_kernel, depth, paired, [at for at, _ in late]),
        [((rows, classes), f32), ((rows, classes), bf16), ((2, rows), f32)],
        [logits, blocks] + [part for _, part in late],
        [pltpu.VMEM((2, rows, tile), f32), pltpu.VMEM((rows, LANES), f32), pltpu.VMEM((rows, LANES), f32)],
    )
    (turned,) = call(turn_kernel, [((groups, width, rows), bf16)], [blocks])

    def total(value, axis, masks):
        for part in [flip(value, axis, mask) for mask in reversed(masks)]:
            value = lax.optimization_barrier(value + part)
        return value

    def row_total(value):
        return total(value, "cls", range(1, groups))

    def column_total(value):
        return total(value + flip(value, "sample", 1), "sample", range(2, samples, 2))

    ceiling = (wide(class_cap) * ratio)[None]
    sums = row_total(sums)
    students_mass, mass = sums[0:1], sums[1:2]
    scale = jnp.ones((1, classes), f32)
    for iteration in range(ITERS):
        (mass,) = call(
            column_kernel,
            [((1, classes), f32)],
            [student, scale, mass],
            [pltpu.VMEM((rows, LANES), f32)],
            [turned] if iteration == 0 else [],
        )
        scale, mass = call(
            row_kernel,
            [((1, classes), f32), ((1, rows), f32)],
            [student, scale, ceiling, column_total(mass)],
            [pltpu.VMEM((rows, LANES), f32)],
        )
        mass = row_total(mass)

    head_at = [at for at, _ in early + late]
    head_list = [part for _, part in early + late]
    near = first + second + [0]
    diagonal = [(a, b) for a in first for b in second]
    far = (diagonal[-1][0] | diagonal[-1][1]) // 2
    near = [a | b for a, b in diagonal[:-1]] + near
    targets, grad, mine, theirs, share = call(
        functools.partial(gradient_kernel, depth, paired, far, head_at),
        [((rows, classes), bf16)] * 2 + [((depth, classes), bf16)] * 2 + [((rows, width), bf16)],
        [student, slope, scale, students_mass, mass, turned] + head_list,
        [pltpu.VMEM((rows, LANES), f32)] * 2 + [pltpu.VMEM((rows, classes), bf16), pltpu.SemaphoreType.DMA],
        slow=(0,),
    )
    theirs = flip(theirs, "sample", 1)
    pairs = call(
        functools.partial(near_kernel, depth, [mask // 2 for mask in near]),
        [((depth, classes), bf16)] * (2 * len(near)),
        [grad, turned],
    )
    theirs, *pairs = lax.optimization_barrier((theirs, *pairs))

    def head_sum(values, more=(), chosen=0):
        kernel = functools.partial(sum_kernel, len(values), chosen)
        return call(kernel, [((depth, classes), bf16)], list(values) + list(more))[0]

    block = head_sum([mine, theirs])
    passed = {diagonal[-1]: cross(block, *diagonal[-1])}
    share_from = {groups - 2: flip(share, "cls", 1)}
    others = {mask: flip(pairs[2 * i + 1], "sample", 1) for i, mask in enumerate(near) if mask}
    (shares,) = call(
        functools.partial(shares_kernel, depth, paired, head_at),
        [((groups, rows, width), bf16)],
        [grad] + head_list,
        extra=[block],
    )

    evens = range(2, groups, 2)
    came = [share_from[mask] if mask in share_from else flip(shares[mask | 1], "cls", 1) for mask in evens]
    made = call(functools.partial(onward_kernel, len(came)), [((rows, width), bf16)] * (1 + len(came)), [shares] + came)
    onward = dict(zip([1, *evens], made))
    ready = lax.optimization_barrier((*others.values(), *passed.values(), pairs[-1], shares))
    others = dict(zip(others, ready))
    passed = dict(zip(passed, ready[len(others) :]))
    own = wide(pairs[-2]) + wide(flip(ready[-2], "sample", 1))
    returned = [flip(value, "cls", mask) for mask, value in onward.items()]
    grad_features = sum([wide(value) for value in returned], wide(shares[0])).astype(bf16)

    mine_of = {mask: pairs[2 * i] for i, mask in enumerate(near)}
    for a, b in diagonal[:-1]:
        passed[a, b] = cross(head_sum([mine_of[a | b], others[a | b]]), a, b)
    received = []
    for mask in first + second:
        chosen = 0 if mask in second else 1
        more = [value for (a, b), value in passed.items() if mask == (a if chosen else b)]
        received.append(flip(head_sum([mine_of[mask], others[mask]], more, chosen), "sample", mask))
    received = lax.optimization_barrier((*received, grad_features))
    grad_features = received[-1]
    grad_head = sum([wide(part) for part in received[:-1]], own).astype(bf16)
    return (targets, grad_features, grad_head)


def solution(mesh):
    return jax.shard_map(
        per_device,
        mesh=mesh,
        in_specs=(P("sample", "cls"), P("sample", "cls"), P("cls")),
        out_specs=(P("sample", "cls"), P("sample", "cls"), P("sample", "cls")),
        check_vma=False,
    )
```
